32 devices in a mesh: expert: 16 (over z, y, x), tensor: 2 (over core).
Axes of the slice: x: 2, y: 2, z: 4, core: 2. Of those that a mesh axis runs over, the one named last changes fastest.
Arguments:
- tokens_in: float32 [25216, 768], P('expert'), may hold values from -10 to 10
- valid: int32 [128, 197], P('expert'), may hold values from 0 to 1, as said below
- routes: int32 [25216, 2], P('expert'), may hold values from 0 to 15, all different within a row; in each aligned block of 1576 rows (0 to 1575, 1576 to 3151, ...) at most 248 rows name the same one
- ln1_gain: float32 [768], replicated, may hold values from 0.5 to 1.5
- ln1_bias: float32 [768], replicated, may hold values from -0.875 to 0.875
- w_query: bfloat16 [768, 768], P(None, 'tensor'), may hold values from -0.21875 to 0.21875
- w_key: bfloat16 [768, 768], P(None, 'tensor'), may hold values from -0.21875 to 0.21875
- w_value: bfloat16 [768, 768], P(None, 'tensor'), may hold values from -0.21875 to 0.21875
- b_query: float32 [768], P('tensor'), may hold values from -3 to 3
- b_value: float32 [768], P('tensor'), may hold values from -0.625 to 0.625
- w_proj: bfloat16 [768, 768], P('tensor'), may hold values from -1.5 to 1.5
- b_proj: float32 [768], replicated, may hold values from -1.75 to 1.75
- ln2_gain: float32 [768], replicated, may hold values from 0.5 to 1.5
- ln2_bias: float32 [768], replicated, may hold values from -0.875 to 0.875
- w_router: bfloat16 [768, 16], replicated, may hold values from -0.15625 to 0.15625
- w_in: bfloat16 [16, 768, 3072], P('expert', None, 'tensor'), may hold values from -0.21875 to 0.21875
- b_in: float32 [16, 3072], P('expert', 'tensor'), may hold values from -3 to 3
- w_out: bfloat16 [16, 3072, 768], P('expert', 'tensor'), may hold values from -1.75 to 1.75
- b_out: float32 [16, 768], P('expert'), may hold values from -6 to 6
- cotangent: float32 [25216, 768], P('expert'), may hold values from -6 to 6
Outputs:
- output: float32 [25216, 768], P('expert')
- grad_input: float32 [25216, 768], P('expert')
- grad_ln1_gain: float32 [768], replicated
- grad_ln1_bias: float32 [768], replicated
- grad_w_query: float32 [768, 768], P(None, 'tensor')
- grad_w_key: float32 [768, 768], P(None, 'tensor')
- grad_w_value: float32 [768, 768], P(None, 'tensor')
- grad_b_query: float32 [768], P('tensor')
- grad_b_value: float32 [768], P('tensor')
- grad_w_proj: float32 [768, 768], P('tensor')
- grad_b_proj: float32 [768], replicated
- grad_ln2_gain: float32 [768], replicated
- grad_ln2_bias: float32 [768], replicated
- grad_w_router: float32 [768, 16], replicated
- grad_w_in: float32 [16, 768, 3072], P('expert', None, 'tensor')
- grad_b_in: float32 [16, 3072], P('expert', 'tensor')
- grad_w_out: float32 [16, 3072, 768], P('expert', 'tensor')
- grad_b_out: float32 [16, 768], P('expert')
- rms_values: float32 [5], replicated
The draws below stay inside these ranges and needn't reach their ends.
Inputs may be any that keep to these rules, and one draw needn't show every extreme that they name: `routes`: among the tokens of one index of the expert axis, no expert is named more than 248 times, a bound that some block reaches. In every image the valid tokens are a prefix of 98 or more positions.
All inputs are finite; a program needn't handle non-finite values.
Results may differ from the reference program's by a relative error of at most 0.017.
Values may be sent and summed in bfloat16 or wider, within the bound.
A program may use at most 320 MiB of HBM per device.

```python
import math
import jax
import jax.numpy as jnp
import numpy as np
from jax import lax

D = 768
HEADS = 12
HEAD_DIM = 64
FF = 3072
SEQ = 197
IMG_DEV = 8
TOK_DEV = 1576
IMAGES = 128
TOKENS = 25216
EXPERTS = 16
CAP = 248
N_EXPERT = 16


def draw_tokens_in(key, part):
    key = jax.random.fold_in(key, 11)
    image = jnp.arange(TOKENS) // SEQ
    rise = image.astype(jnp.float32) / max(IMAGES - 1, 1)
    base = jnp.clip(jax.random.normal(key, (TOKENS, D), jnp.float32), -5.0, 5.0)
    scale = 0.6 + 1.2 * rise
    return base * scale[:, None]


def draw_valid(key, part):
    key = jax.random.fold_in(key, 23)
    length = jax.random.randint(key, (IMAGES, 1), SEQ // 2, SEQ + 1)
    return (jnp.arange(SEQ)[None, :] < length).astype(jnp.int32)


def levels(own_key, dims, shards, smallest, high):
    loudness = 1.0
    for dim, shards_of in shards:
        heights = jax.random.uniform(jax.random.fold_in(jax.random.fold_in(own_key, 6), dim), (shards_of,), jnp.float32, smallest / len(shards), high / len(shards))
        loudness = loudness * jnp.repeat(jnp.exp(heights), dims[dim] // shards_of).reshape((-1,) + (1,) * (len(dims) - 1 - dim))
    return loudness


def shared_out(rng, own, number, rows, number_of, top, bound, lean):
    sequence = jax.random.permutation(rng, number_of)
    packed, common = load_shares(number_of, rows * top, bound, lean, True), load_shares(number_of, rows * top, bound, lean, False)
    places = jnp.arange(number_of)

    def named(sizes, offset_by):
        used = int((sizes > 0).sum())
        fixed = max(1, used // 4)
        moved = fixed + (places - fixed + offset_by * (used - fixed)) % max(1, number_of - fixed)
        return jnp.zeros((number_of,), jnp.int32).at[sequence[jnp.where(places < fixed, places, moved)]].set(jnp.asarray(sizes, jnp.int32))

    sizes = jnp.where(number % 4 == 0, named(packed, number // 4), named(common, number - number // 4 - 1))
    mixed = jax.random.permutation(jax.random.fold_in(own, 3), number_of)
    source_of, sink = mixed[0:number_of // 2 * 2:2], mixed[1:number_of // 2 * 2:2]
    slack = jnp.minimum(sizes[source_of] - 1, bound - sizes[sink]) // 2
    slack = jnp.where((source_of == sequence[0]) | (sink == sequence[0]) | (sizes[sink] == 0), 0, jnp.maximum(slack, 0))
    moved = jax.random.randint(jax.random.fold_in(own, 4), (number_of // 2,), 0, 1 << 20) % (slack + 1)
    sizes = sizes.at[source_of].add(-moved).at[sink].add(moved)
    items = jnp.searchsorted(jnp.cumsum(sizes), jnp.arange(rows * top), side="right").astype(jnp.int32)
    table = items.reshape(top, rows).T
    table = table[jax.random.permutation(jax.random.fold_in(own, 1), rows)]
    offset_by = jax.random.randint(jax.random.fold_in(own, 2), (rows, 1), 0, top)
    return jnp.take_along_axis(table, (jnp.arange(top)[None, :] + offset_by) % top, axis=1)


def load_shares(amount, total, limit, slope, full):
    loads = [(1 << 20) // math.isqrt(grade ** slope) + 1 for grade in range(1, amount + 1)]
    largest = limit if full else min(limit, max(-(-total // amount), total * loads[0] // sum(loads)))
    least = 1 if total - largest >= amount - 1 else 0
    holding, spare = [largest] + [least] * (amount - 1), total - largest - least * (amount - 1)
    while spare > 0:
        free = [i for i in range(1, amount) if holding[i] < largest] or [i for i in range(1, amount) if holding[i] < limit]
        whole, budget = sum([loads[i] for i in free]), spare
        for i in free:
            addition = min(limit - holding[i], max(1, budget * loads[i] // whole), spare)
            holding[i] = holding[i] + addition
            spare = spare - addition
    return np.array(holding)


def bell_draw(own_key, dims, deviation, bound, cuts=(), kind=jnp.bfloat16):
    array = jax.random.normal(own_key, dims, jnp.float32) * deviation
    if len(cuts) > 0:
        array = levels(own_key, dims, cuts, -0.22, 0.18) * array
    return jnp.clip(array, min=-bound, max=bound).astype(kind)


def setup_inputs(seed: int = 0) -> dict:
    arg_keys = jax.random.split(jax.random.key(seed), 21)
    tokens_in = draw_tokens_in(jax.random.fold_in(arg_keys[20], 71), 0)
    valid = draw_valid(jax.random.fold_in(arg_keys[20], 71), 0)
    routes_keys = jax.random.split(jax.random.fold_in(arg_keys[2], 1), TOKENS // TOK_DEV)
    routes_turns = jax.random.permutation(jax.random.fold_in(arg_keys[2], 3), TOKENS // TOK_DEV)
    routes = jax.vmap(lambda own, number: shared_out(jax.random.fold_in(arg_keys[2], 2), own, number, TOK_DEV, EXPERTS, 2, CAP, 0))(routes_keys, routes_turns).reshape((TOKENS, 2))
    ln1_gain = jnp.clip(1.0 + 0.1 * jax.random.normal(arg_keys[3], (D,), jnp.float32), 0.5, 1.5)
    ln1_bias = bell_draw(arg_keys[4], (D,), 0.15, 0.875, (), jnp.float32)
    w_query = bell_draw(arg_keys[5], (D, D), D ** -0.5, 0.21875, ((1, 2),))
    w_key = bell_draw(arg_keys[6], (D, D), D ** -0.5, 0.21875, ((1, 2),))
    w_value = bell_draw(arg_keys[7], (D, D), D ** -0.5, 0.21875, ((1, 2),))
    b_query = bell_draw(arg_keys[8], (D,), 0.5, 3.0, ((0, 2),), jnp.float32)
    b_value = bell_draw(arg_keys[9], (D,), 0.1, 0.625, ((0, 2),), jnp.float32)
    w_proj = bell_draw(arg_keys[10], (D, D), (max(D // 48, 1)) ** -0.5, 1.5, ((0, 2),))
    b_proj = bell_draw(arg_keys[11], (D,), 0.3, 1.75, (), jnp.float32)
    ln2_gain = jnp.clip(1.0 + 0.1 * jax.random.normal(arg_keys[12], (D,), jnp.float32), 0.5, 1.5)
    ln2_bias = bell_draw(arg_keys[13], (D,), 0.15, 0.875, (), jnp.float32)
    w_router = bell_draw(arg_keys[14], (D, EXPERTS), (2 * D) ** -0.5, 0.15625)
    w_in = bell_draw(arg_keys[15], (EXPERTS, D, FF), D ** -0.5, 0.21875, ((0, 16), (2, 2)))
    b_in = bell_draw(arg_keys[16], (EXPERTS, FF), 0.5, 3.0, ((0, 16), (1, 2)), jnp.float32)
    w_out = bell_draw(arg_keys[17], (EXPERTS, FF, D), (max(FF // 256, 1)) ** -0.5, 1.75, ((0, 16), (1, 2)))
    b_out = bell_draw(arg_keys[18], (EXPERTS, D), 1.0, 6.0, ((0, 16),), jnp.float32)
    cotangent = bell_draw(arg_keys[19], (TOKENS, D), 1.0, 6.0, ((0, 16),), jnp.float32)
    return dict(tokens_in=tokens_in, valid=valid, routes=routes, ln1_gain=ln1_gain, ln1_bias=ln1_bias, w_query=w_query, w_key=w_key, w_value=w_value, b_query=b_query, b_value=b_value, w_proj=w_proj, b_proj=b_proj, ln2_gain=ln2_gain, ln2_bias=ln2_bias, w_router=w_router, w_in=w_in, b_in=b_in, w_out=w_out, b_out=b_out, cotangent=cotangent)


@jax.custom_vjp
def low(v):
    return lax.optimization_barrier(v.astype(jnp.bfloat16)).astype(jnp.float32)

@jax.custom_vjp
def low_back(v):
    return v

def low_keep(v):
    return (low(v), None)

def low_pass(kept, grad):
    return (grad,)

def back_keep(v):
    return (v, None)

def back_low(kept, grad):
    return (low(grad),)
low.defvjp(low_keep, low_pass)
low_back.defvjp(back_keep, back_low)
HIGH = lax.Precision.HIGHEST
masked_fill = -1e+30

def matmul(left, right):
    return jnp.dot(left, right, precision=HIGH)

def layer_norm(values, gain, bias):
    center = values - lax.optimization_barrier(jnp.mean(values, -1, keepdims=True))
    inv_std = lax.rsqrt(lax.optimization_barrier(jnp.mean(center * center, -1, keepdims=True)) + 1e-06)
    return center * inv_std * gain + bias

def softmax_rows(scores):
    top = lax.optimization_barrier(jnp.max(scores, -1, keepdims=True))
    expo = jnp.exp(scores - top)
    return expo / lax.optimization_barrier(jnp.sum(expo, -1, keepdims=True))

def attend_images(h1_rows, key_mask, w_query, w_key, w_value, b_query, b_value):
    images = key_mask.shape[0]
    shape4 = (images, SEQ, HEADS, HEAD_DIM)
    query = low(low_back(matmul(h1_rows, w_query) + b_query)).reshape(shape4)
    keys = low(low_back(matmul(h1_rows, w_key))).reshape(shape4)
    values = low(low_back(matmul(h1_rows, w_value) + b_value)).reshape(shape4)
    raw = low_back(jnp.einsum('gqhd,gkhd->ghqk', query, keys, precision=HIGH))
    scores = jnp.where(key_mask[:, None, None, :] > 0, raw * HEAD_DIM ** (-0.5), masked_fill)
    probs = softmax_rows(scores)
    mixed = jnp.einsum('ghqk,gkhd->gqhd', low(probs), values, precision=HIGH)
    return low(low_back(mixed.reshape(images * SEQ, HEADS * HEAD_DIM)))

def expert_block(block):
    rows, w_in_one, b_in_one, w_out_one, b_out_one = block
    pre_act = low_back(matmul(rows, w_in_one) + b_in_one)
    hidden = low(jax.nn.gelu(pre_act, approximate=False))
    return matmul(hidden, w_out_one) + b_out_one

def reference(tokens_in, valid, routes, ln1_gain, ln1_bias, w_query, w_key, w_value, b_query, b_value, w_proj, b_proj, ln2_gain, ln2_bias, w_router, w_in, b_in, w_out, b_out, cotangent):
    flat_ids = routes.reshape(-1).astype(jnp.int32)
    grouped = routes.reshape(N_EXPERT, TOK_DEV * 2)
    onehot = (grouped[:, :, None] == jnp.arange(EXPERTS, dtype=jnp.int32)[None, None, :]).astype(jnp.int32)
    before = jnp.cumsum(onehot, 1) - onehot
    slot_pos = lax.optimization_barrier(jnp.sum(before * onehot, 2))
    slot_index = (jnp.arange(N_EXPERT, dtype=jnp.int32)[:, None] * CAP + slot_pos).reshape(-1).astype(jnp.int32)
    key_mask = valid.reshape(N_EXPERT, IMG_DEV, SEQ)

    def forward(x_in, gain_one, bias_one, wq_f, wk_f, wv_f, bq_f, bv_f, wp_f, bp_f, gain_two, bias_two, wr_f, wi_f, bi_f, wo_f, bo_f):
        h1_val = low(layer_norm(x_in, gain_one, bias_one))

        def one_group(block):
            return attend_images(block[0], block[1], wq_f, wk_f, wv_f, bq_f, bv_f)
        heads_out = lax.map(jax.checkpoint(one_group), (h1_val.reshape(N_EXPERT, TOK_DEV, D), key_mask))
        attn_out = low_back(matmul(heads_out.reshape(TOKENS, D), wp_f) + bp_f)
        middle = x_in + attn_out
        h2_val = low(layer_norm(middle, gain_two, bias_two))
        logits = low_back(matmul(h2_val, wr_f))
        route_probs = softmax_rows(logits)
        gates = jnp.take_along_axis(route_probs, routes, axis=1)
        rows = low_back(jnp.broadcast_to(h2_val[:, None, :], (TOKENS, 2, D)).reshape(TOKENS * 2, D))
        buffers = jnp.zeros((EXPERTS, N_EXPERT * CAP, D), jnp.float32).at[flat_ids, slot_index].set(rows)
        results = lax.map(jax.checkpoint(expert_block), (buffers, wi_f, bi_f, wo_f, bo_f))
        results = low(low_back(results))
        picked = results[flat_ids, slot_index].reshape(TOKENS, 2, D)
        moe_out = lax.optimization_barrier(jnp.sum(gates[:, :, None] * picked, 1))
        output = middle + moe_out
        return (output, (middle, attn_out, moe_out))
    inputs = (tokens_in, ln1_gain, ln1_bias, w_query.astype(jnp.float32), w_key.astype(jnp.float32), w_value.astype(jnp.float32), b_query, b_value, w_proj.astype(jnp.float32), b_proj, ln2_gain, ln2_bias, w_router.astype(jnp.float32), w_in.astype(jnp.float32), b_in, w_out.astype(jnp.float32), b_out)
    output, back_fn, extras = jax.vjp(forward, *inputs, has_aux=True)
    grads = back_fn(cotangent)
    middle, attn_out, moe_out = extras
    valid_rows = valid.reshape(TOKENS).astype(jnp.float32)[:, None]
    count = jnp.sum(valid_rows) * D
    rms_values = jnp.stack([jnp.sqrt(jnp.sum(valid_rows * field * field) / count) for field in (tokens_in, middle, output, attn_out, moe_out)])
    return (output, grads[0], grads[1], grads[2], grads[3], grads[4], grads[5], grads[6], grads[7], grads[8], grads[9], grads[10], grads[11], grads[12], grads[13], grads[14], grads[15], grads[16], rms_values)
```

```python
import functools

import jax
import jax.numpy as jnp
from jax import lax
from jax.experimental import pallas as pl
from jax.experimental.pallas import tpu as pltpu
from jax.sharding import PartitionSpec as P

HEAD_DIM = 64
LANES = 128
LOG2E = 1.4426950408889634
MASKED = -1e30
MESH = pl.DeviceIdType.MESH
VMEM_LIMIT = 60 << 20
f32 = jnp.float32
bf16 = jnp.bfloat16
i32 = jnp.int32


def up(value, step):
    return -(-value // step) * step


def params(**more):
    return pltpu.CompilerParams(vmem_limit_bytes=VMEM_LIMIT, **more)


def whole(shape):
    return pl.BlockSpec(shape, lambda *_: (0,) * len(shape))


def dot(a, b):
    return lax.dot_general(a, b, (((1,), (0,)), ((), ())), preferred_element_type=f32)


def dot_nt(a, b):
    return lax.dot_general(a, b, (((1,), (1,)), ((), ())), preferred_element_type=f32)


def dot_tn(a, b):
    return lax.dot_general(a, b, (((0,), (0,)), ((), ())), preferred_element_type=f32)


def lane_iota(shape):
    return lax.broadcasted_iota(i32, shape, len(shape) - 1)


def norm_parts(values):
    center = values - jnp.mean(values, -1, keepdims=True)
    inv_std = lax.rsqrt(jnp.mean(center * center, -1, keepdims=True) + 1e-06)
    return center * inv_std, inv_std


def norm_back(grad_out, normed, inv_std, gain):
    scaled = grad_out * gain
    return inv_std * (
        scaled
        - jnp.mean(scaled, -1, keepdims=True)
        - normed * jnp.mean(scaled * normed, -1, keepdims=True)
    )


def gelu_parts(x):
    z = jnp.abs(x) * 0.7071067811865476
    t = 1.0 / (1.0 + 0.3275911 * z)
    poly = t * (
        0.254829592 * 0.5
        + t
        * (
            -0.284496736 * 0.5
            + t * (1.421413741 * 0.5 + t * (-1.453152027 * 0.5 + t * (1.061405429 * 0.5)))
        )
    )
    e = jnp.exp2(x * x * (-0.5 * LOG2E))
    half = poly * e
    cdf = jnp.where(x >= 0, 1.0 - half, half)
    return x * cdf, cdf + x * e * 0.3989422804014327


def prep_kernel(dims, routes_ref, cot_ref, grow_ref, post_ref, fidx_ref, g16):
    images, seq, seq_pad, experts, cap_dev = dims
    tok_pad = images * seq_pad
    core = lax.axis_index("tensor")
    expert = lax.axis_index("expert")
    for i in range(images):
        rows = cot_ref[seq * i : seq * (i + 1), :].astype(bf16)
        g16[seq_pad * i : seq_pad * (i + 1), :] = jnp.zeros((seq_pad, rows.shape[1]), bf16)
        g16[seq_pad * i : seq_pad * i + seq, :] = rows
    r0 = routes_ref[:, 0:1]
    r1 = routes_ref[:, 1:2]
    lanes = lane_iota((tok_pad, LANES))
    named0 = r0 == lanes
    named1 = r1 == lanes
    named = jnp.where(named0 | named1, 1.0, 0.0)
    named_low = named.astype(bf16)
    lower = (
        lax.broadcasted_iota(i32, (seq_pad, seq_pad), 1)
        < lax.broadcasted_iota(i32, (seq_pad, seq_pad), 0)
    ).astype(f32).astype(bf16)
    run = jnp.zeros((1, LANES), f32)
    parts = []
    for i in range(images):
        rows = slice(seq_pad * i, seq_pad * (i + 1))
        parts.append(dot(lower, named_low[rows]) + run)
        run = run + jnp.sum(named[rows], 0, keepdims=True)
    before = jnp.concatenate(parts, 0) - (core * cap_dev).astype(f32)
    pos = jnp.where(named > 0, before, -1.0)
    groups, _, _, group = post_ref.shape
    for j in range(groups):
        turned = jnp.transpose(pos[group * j : group * (j + 1)], (1, 0))
        for e in range(experts):
            post_ref[j, e] = turned[e : e + 1]
    for k, named_k, r_k in ((0, named0, r0), (1, named1, r1)):
        slot = jnp.sum(jnp.where(named_k, before, 0.0), 1, keepdims=True)
        fits = (slot >= 0) & (slot < cap_dev) & (r_k >= 0)
        turn = lax.rem(r_k - expert + experts, experts)
        flat = turn.astype(f32) * cap_dev + slot
        fidx_ref[:, k : k + 1] = jnp.where(fits, flat, -1.0).astype(i32)
    slots = lax.broadcasted_iota(i32, (cap_dev, group), 0).astype(f32)
    for e in range(experts):
        total = None
        for j in range(groups):
            named_e = post_ref[j, lax.rem(expert + e, experts)]
            pick = jnp.where(named_e == slots, 1.0, 0.0).astype(bf16)
            term = dot(pick, g16[group * j : group * (j + 1), :])
            total = term if total is None else total + term
        grow_ref[e] = total.astype(bf16)


def combine_kernel(cap_dev, with_dots, rows_ref, gslot_ref, fidx_ref, *rest):
    if with_dots:
        grow_ref, own_ref, out_ref, own_dots_ref, dots_ref, scaled, spread = rest
    else:
        own_ref, out_ref, scaled = rest
    rows_all = rows_ref.shape[0]
    tile = LANES
    lanes = lane_iota((tile, LANES))
    for i in range(rows_all // tile):
        here = slice(tile * i, tile * (i + 1))
        rows = rows_ref[here, :].astype(f32)
        scaled[here, :] = (rows * gslot_ref[here, :]).astype(bf16)
        if with_dots:
            dots = jnp.sum(rows * grow_ref[here, :].astype(f32), 1, keepdims=True)
            owner = (lax.broadcasted_iota(i32, (tile, LANES), 0) + tile * i) // cap_dev
            owner = lax.rem(owner + lax.axis_index("expert"), lax.axis_size("expert"))
            spread[here, :] = jnp.where(lanes == owner, dots, 0.0).astype(bf16)
    group = own_ref.shape[0]
    n = out_ref.shape[0] + 1
    me = lax.axis_index("tensor")
    step = 208 if group % 208 == 0 else group
    lanes = lane_iota((step, rows_all))
    for k in range(n):
        base = lax.rem(me + k, n) * group
        for i in range(group // step):
            tok = pl.ds(pl.multiple_of(base + i * step, 16), step)
            hit = (fidx_ref[tok, 0:1] == lanes) | (fidx_ref[tok, 1:2] == lanes)
            pick = jnp.where(hit, 1.0, 0.0).astype(bf16)
            to = slice(i * step, (i + 1) * step)
            (own_ref if k == 0 else out_ref.at[k - 1])[to, :] = dot(pick, scaled[...]).astype(bf16)
            if with_dots:
                (own_dots_ref if k == 0 else dots_ref.at[k - 1])[to, :] = dot(
                    pick, spread[...]
                ).astype(bf16)


def piece(own_ref, rest_ref, j):
    return own_ref[...] if j == 0 else rest_ref[j - 1]


def read_image(dst, src, image, seq):
    for n in range(src.shape[0] // seq):

        @pl.when(image == n)
        def _(n=n):
            dst[0:seq, :] = src[seq * n : seq * (n + 1), :]


def write_image(dst, value, image, seq):
    for n in range(dst.shape[0] // seq):

        @pl.when(image == n)
        def _(n=n):
            dst[seq * n : seq * (n + 1), :] = value[:seq]


def attn_fwd_kernel(
    dims, tok_ref, valid_ref, mask_ref, g1_ref, b1_ref, wq, wqs, wk, wks, wv, wvs, wp, wps,
    bq_ref, bv_ref, bp_ref, g2_ref, b2_ref, wr_ref,
    h1_ref, q_ref, k_ref, v_ref, probs_ref, heads_ref, mid_ref, h2x_ref, acc_ref, x_s
):
    seq, seq_pad, key_pad, own, experts = dims
    width = tok_ref.shape[1]
    step = pl.program_id(0)
    image = lax.axis_index("tensor") * own + step
    x_s[...] = jnp.zeros_like(x_s)
    read_image(x_s, tok_ref, image, seq)
    x = x_s[...]
    normed, _ = norm_parts(x)
    h1 = (normed * g1_ref[...] + b1_ref[...]).astype(bf16)
    h1_ref[0] = h1
    k_ref[0, seq_pad:, :] = jnp.zeros((key_pad - seq_pad, width), bf16)
    v_ref[0, seq_pad:, :] = jnp.zeros((key_pad - seq_pad, width), bf16)
    shares = [slice(wq.shape[1] * j, wq.shape[1] * (j + 1)) for j in range(wqs.shape[0] + 1)]
    for j, cols in enumerate(shares):
        q_ref[0, :, cols] = (dot(h1, piece(wq, wqs, j)) + bq_ref[:, cols]).astype(bf16)
        k_ref[0, 0:seq_pad, cols] = dot(h1, piece(wk, wks, j)).astype(bf16)
        v_ref[0, 0:seq_pad, cols] = (dot(h1, piece(wv, wvs, j)) + bv_ref[:, cols]).astype(bf16)
    low_half = lane_iota((seq_pad, LANES)) < HEAD_DIM
    mask = mask_ref[0]
    for p in range(width // LANES):
        cols = slice(LANES * p, LANES * (p + 1))
        qp = q_ref[0, :, cols]
        zero = jnp.zeros_like(qp)
        qs = jnp.concatenate([jnp.where(low_half, qp, zero), jnp.where(low_half, zero, qp)], 0)
        s = dot_nt(qs, k_ref[0, :, cols]) * (HEAD_DIM**-0.5 * LOG2E) + mask
        e = jnp.exp2(s - jnp.max(s, -1, keepdims=True))
        prob = (e * (1.0 / jnp.sum(e, -1, keepdims=True))).astype(bf16)
        probs_ref[0, p] = prob
        o = dot(prob, v_ref[0, :, cols])
        heads_ref[0, :, cols] = jnp.where(low_half, o[:seq_pad], o[seq_pad:]).astype(bf16)
    attn = bp_ref[...]
    for j, cols in enumerate(shares):
        attn = attn + dot(heads_ref[0, :, cols], piece(wp, wps, j))
    middle = x + attn
    mid_ref[0] = middle
    ok = valid_ref[0]

    @pl.when(step == 0)
    def _():
        acc_ref[...] = jnp.zeros_like(acc_ref)

    for row, field in enumerate((x, middle, attn)):
        acc_ref[row : row + 1, :] += jnp.sum(ok * field * field, 0, keepdims=True)
    normed2, _ = norm_parts(middle)
    h2 = (normed2 * g2_ref[...] + b2_ref[...]).astype(bf16)
    h2x_ref[0, :, 0:width] = h2
    logits = dot(h2, wr_ref[...])
    logits = jnp.where(lane_iota(logits.shape) < experts, logits, MASKED)
    e = jnp.exp(logits - jnp.max(logits, -1, keepdims=True))
    prob = e / jnp.sum(e, -1, keepdims=True)
    high = prob.astype(bf16).astype(f32)
    h2x_ref[0, :, width:] = (high + pltpu.roll(prob - high, experts, 1)).astype(bf16)


def attn_bwd_kernel(
    dims, tok_ref, cot_ref, valid_ref, accf_ref, mid_ref, h2x_ref, h1_ref, q_ref, k_ref, v_ref, probs_ref,
    heads_ref, moe_own, moe_ref, dots_own, dots_ref, gmoe_own, gmoe_ref, g1_ref, g2_ref,
    wq, wqs, wk, wks, wv, wvs, wp, wps, wr_ref,
    out_ref, gin_ref, grad_own, grad_rest, acc_ref,
    x_s, c_s, gh_s, h1_s, heads_s, ga_s, dq_s, dk_s, dv_s
):
    seq, seq_pad, key_pad, own, experts = dims
    width = tok_ref.shape[1]
    step = pl.program_id(0)
    shares = [slice(wq.shape[1] * j, wq.shape[1] * (j + 1)) for j in range(wqs.shape[0] + 1)]
    small_b = small_base(len(shares))
    image = lax.axis_index("tensor") * own + step
    at = pl.multiple_of(step * seq_pad, 16)
    pad = jnp.zeros((seq_pad - seq + 8, width), f32)
    x_s[seq // 8 * 8 :, :] = pad[: seq_pad - seq // 8 * 8]
    c_s[seq // 8 * 8 :, :] = pad[: seq_pad - seq // 8 * 8]
    read_image(x_s, tok_ref, image, seq)
    read_image(c_s, cot_ref, image, seq)
    ok = valid_ref[0]

    @pl.when(step == 0)
    def _():
        acc_ref[...] = jnp.zeros_like(acc_ref)
        acc_ref[small_b : small_b + 8, :] = accf_ref[...]

    def add(row, value):
        acc_ref[row : row + 1, :] += jnp.sum(value, 0, keepdims=True)

    def total(own_ref, rest_ref):
        value = own_ref[0].astype(f32)
        for j in range(rest_ref.shape[0]):
            value = value + rest_ref[j, 0].astype(f32)
        return value

    middle = mid_ref[0]
    moe = total(moe_own, moe_ref)
    output = middle + moe
    write_image(out_ref, output, step, seq)
    add(0, ok * output * output)
    add(1, ok * moe * moe)
    h2 = h2x_ref[0, :, 0:width]
    pair = h2x_ref[0, :, width:].astype(f32)
    prob = jnp.where(
        lane_iota(pair.shape) < experts, pair + pltpu.roll(pair, LANES - experts, 1), 0.0
    )
    grad_probs = total(dots_own, dots_ref)
    grad_logits = (
        prob * (grad_probs - jnp.sum(grad_probs * prob, -1, keepdims=True))
    ).astype(bf16)
    acc_ref[small_b + 8 : small_b + 8 + experts, :] += dot_tn(grad_logits, h2)[:experts]
    grad_h2 = dot_nt(grad_logits, wr_ref[...]) + total(gmoe_own, gmoe_ref)
    normed2, inv2 = norm_parts(middle)
    add(2, grad_h2 * normed2)
    add(3, grad_h2)
    grad_middle = c_s[...] + norm_back(grad_h2, normed2, inv2, g2_ref[...])
    c_s[...] = grad_middle
    grad_attn = grad_middle.astype(bf16)
    add(4, grad_attn.astype(f32))
    ga_s[pl.ds(at, seq_pad), :] = grad_attn
    heads_s[pl.ds(at, seq_pad), :] = heads_ref[0]
    h1_s[pl.ds(at, seq_pad), :] = h1_ref[0]
    for j, cols in enumerate(shares):
        gh_s[:, cols] = dot_nt(grad_attn, piece(wp, wps, j)).astype(bf16)
    low_half = lane_iota((seq_pad, LANES)) < HEAD_DIM

    def split(value):
        zero = jnp.zeros_like(value)
        return jnp.concatenate(
            [jnp.where(low_half, value, zero), jnp.where(low_half, zero, value)], 0
        )

    for p in range(width // LANES):
        cols = slice(LANES * p, LANES * (p + 1))
        gs = split(gh_s[:, cols])
        qs = split(q_ref[0, :, cols])
        low_prob = probs_ref[0, p]
        weights = low_prob.astype(f32)
        mixed = weights * dot_nt(gs, v_ref[0, :, cols])
        ds = (
            (mixed - weights * jnp.sum(mixed, -1, keepdims=True)) * (HEAD_DIM**-0.5)
        ).astype(bf16)
        dq = dot(ds, k_ref[0, :, cols])
        dq_s[pl.ds(at, seq_pad), cols] = jnp.where(
            low_half, dq[:seq_pad], dq[seq_pad:]
        ).astype(bf16)
        dk_s[pl.ds(at, seq_pad), cols] = dot_tn(ds, qs)[:seq_pad].astype(bf16)
        dv_s[pl.ds(at, seq_pad), cols] = dot_tn(low_prob, gs)[:seq_pad].astype(bf16)
    dq = dq_s[pl.ds(at, seq_pad), :]
    dk = dk_s[pl.ds(at, seq_pad), :]
    dv = dv_s[pl.ds(at, seq_pad), :]
    which = lax.broadcasted_iota(i32, (small_b, shares[0].stop), 0)
    for j, cols in enumerate(shares):
        owner = lax.rem(lax.axis_index("tensor") + j, len(shares))
        for base, value in ((8, dq), (8 + len(shares), dv)):
            total_j = jnp.sum(value[:, cols].astype(f32), 0, keepdims=True)
            acc_ref[0:small_b, shares[0]] += jnp.where(which == base + owner, total_j, 0.0)
    grad_h1 = None
    for j, cols in enumerate(shares):
        for left, own_ref, rest_ref in ((dq, wq, wqs), (dk, wk, wks), (dv, wv, wvs)):
            term = dot_nt(left[:, cols], piece(own_ref, rest_ref, j))
            grad_h1 = term if grad_h1 is None else grad_h1 + term
    normed1, inv1 = norm_parts(x_s[...])
    add(5, grad_h1 * normed1)
    add(6, grad_h1)
    add(7, jnp.broadcast_to(ok, grad_h1.shape))
    grad_in = c_s[...] + norm_back(grad_h1, normed1, inv1, g1_ref[...])
    write_image(gin_ref, grad_in, step, seq)

    @pl.when(step == own - 1)
    def _():
        for n, part in enumerate((dq_s, dk_s, dv_s, heads_s)):
            rows = slice(width * n, width * (n + 1))
            left = ga_s if n == 3 else h1_s
            grad = dot_tn(left[...], part[...])
            grad_own[rows, :] = grad[:, shares[0]]
            for j, cols in enumerate(shares[1:]):
                grad_rest[j, rows, :] = grad[:, cols].astype(bf16)


def small_base(cores):
    return up(8 + 2 * cores, 8)


def view(own_ref, rest_ref, j):
    return own_ref if j == 0 else rest_ref.at[j - 1]


def chunk_of(hidden):
    for size in (512, 384, 256, 128):
        if hidden % size == 0:
            return size
    return hidden


def greet(peers):
    barrier = pltpu.get_barrier_semaphore()
    for peer in peers:
        pl.semaphore_signal(barrier, inc=1, device_id=peer, device_id_type=MESH)
    pl.semaphore_wait(barrier, len(peers))


def around(axis):
    n = lax.axis_size(axis)
    me = lax.axis_index(axis)
    return n, lambda k: {axis: lax.rem(me + n + k, n)}


def moe_kernel(
    h2x_ref, post_ref, grow_hbm, w_in, w_ins, b_in, b_ins, w_out, w_outs, b_out_ref,
    back_ref, gback_ref, gslot_ref, gin_own, gout_own, gin_rest, gout_rest,
    gbin_own, gbin_rest, gbout_ref,
    table, out_s, rows_s, hid, slope, grow_s, res_s, gate_out, gate_in, stage_in, stage_out,
    gbin_send, gbout_send,
    local_sem, tab_send, tab_recv, h_send, h_recv, c_send, c_recv, r_send, r_recv, g_send, g_recv,
    w_send, w_recv, own_sem
):
    experts, chip = around("expert")
    cores, core = around("tensor")
    me_e = lax.axis_index("expert")
    me_t = lax.axis_index("tensor")
    cap_dev, width = rows_s.shape[1:]
    group = table.shape[1]
    share = w_in.shape[1]
    size = chunk_of(share)
    per = share // size
    greet([chip(k) for k in range(1, experts)] + [core(k) for k in range(1, cores)])

    def remote(src, dst, send, recv, there):
        return pltpu.make_async_remote_copy(
            src_ref=src, dst_ref=dst, send_sem=send, recv_sem=recv,
            device_id=there, device_id_type=MESH,
        )

    grow_copy = pltpu.make_async_copy(grow_hbm, grow_s, local_sem.at[0])
    grow_copy.start()
    own_copy = pltpu.make_async_copy(h2x_ref, table.at[me_t], local_sem.at[1])
    own_copy.start()
    fills = [
        remote(h2x_ref, table.at[me_t], tab_send.at[k], tab_recv.at[k], core(k))
        for k in range(1, cores)
    ]
    for copy in fills:
        copy.start()
    own_copy.wait()
    for copy in fills:
        copy.wait()

    slots = lax.broadcasted_iota(i32, (cap_dev, group), 0).astype(f32)
    lanes = lane_iota((cap_dev, LANES))

    def select(k):
        e = lax.rem(me_e + k, experts)
        total = None
        for j in range(cores):
            pick = jnp.where(post_ref[j, e] == slots, 1.0, 0.0).astype(bf16)
            term = dot(pick, table[j])
            total = term if total is None else total + term
        mine = (lanes == e) | (lanes == e + experts)
        gate = jnp.sum(jnp.where(mine, total[:, width:], 0.0), 1, keepdims=True)
        gslot_ref[pl.ds(pl.multiple_of(cap_dev * k, 8), cap_dev), :] = gate
        spread = jnp.transpose(jnp.broadcast_to(gate, (cap_dev, LANES)), (1, 0))
        return total[:, :width].astype(bf16), spread[0:8]

    def h_copy(k):
        return remote(out_s.at[k], rows_s.at[k], h_send.at[k], h_recv.at[k], chip(k))

    def c_copy(k):
        return remote(gate_out.at[k], gate_in.at[k], c_send.at[k], c_recv.at[k], chip(k))

    def r_copy(k):
        return remote(res_s.at[k], back_ref.at[k], r_send.at[k], r_recv.at[k], chip(-k))

    def g_copy(k):
        return remote(out_s.at[k], gback_ref.at[k], g_send.at[k], g_recv.at[k], chip(-k))

    def send_rows(k, _):
        rows, gate = select(k)
        out_s[k] = rows
        gate_out[k] = gate
        h_copy(k).start()
        c_copy(k).start()
        return 0

    lax.fori_loop(1, experts, send_rows, 0)
    rows, gate = select(0)
    rows_s[0] = rows
    gate_in[0] = gate

    def forward(i):
        x = rows_s[pl.ds(2 * i, 2)].reshape(2 * cap_dev, width)
        here = pl.ds(pl.multiple_of(2 * cap_dev * i, 16), 2 * cap_dev)
        total = None
        for j in range(cores):
            for n in range(per):
                cols = slice(size * n, size * (n + 1))
                flat = slice(share * j + size * n, share * j + size * (n + 1))
                pre = dot(x, view(w_in, w_ins, j)[:, cols]) + view(b_in, b_ins, j)[:, cols]
                act, steep = gelu_parts(pre)
                act = act.astype(bf16)
                hid[here, flat] = act
                slope[here, flat] = steep.astype(bf16)
                term = dot(act, view(w_out, w_outs, j)[cols, :])
                total = term if total is None else total + term
        res = (total + b_out_ref[...]).astype(bf16)
        res_s[pl.ds(2 * i, 2)] = res.reshape(2, cap_dev, width)

    h_copy(1).wait_recv()
    forward(0)
    own_res = pltpu.make_async_copy(res_s.at[0], back_ref.at[0], own_sem.at[0])
    own_res.start()
    r_copy(1).start()

    def forward_step(i, _):
        h_copy(2 * i).wait_recv()
        h_copy(2 * i + 1).wait_recv()
        forward(i)
        r_copy(2 * i).start()
        r_copy(2 * i + 1).start()
        return 0

    lax.fori_loop(1, experts // 2, forward_step, 0)

    def sent_rows(k, _):
        h_copy(k).wait_send()
        return 0

    lax.fori_loop(1, experts, sent_rows, 0)
    grow_copy.wait()

    def backward(i):
        g = grow_s[pl.ds(2 * i, 2)].reshape(2 * cap_dev, width)
        here = pl.ds(pl.multiple_of(2 * cap_dev * i, 16), 2 * cap_dev)
        total = None
        for j in range(cores):
            for n in range(per):
                cols = slice(size * n, size * (n + 1))
                flat = slice(share * j + size * n, share * j + size * (n + 1))
                grad = dot_nt(g, view(w_out, w_outs, j)[cols, :])
                gpre = (grad * slope[here, flat].astype(f32)).astype(bf16)
                slope[here, flat] = gpre
                term = dot_nt(gpre, view(w_in, w_ins, j)[:, cols])
                total = term if total is None else total + term
        out_s[pl.ds(2 * i, 2)] = total.astype(bf16).reshape(2, cap_dev, width)

    backward(0)
    own_grad = pltpu.make_async_copy(out_s.at[0], gback_ref.at[0], own_sem.at[1])
    own_grad.start()
    g_copy(1).start()

    def backward_step(i, _):
        backward(i)
        g_copy(2 * i).start()
        g_copy(2 * i + 1).start()
        return 0

    lax.fori_loop(1, experts // 2, backward_step, 0)

    def gates_in(k, _):
        c_copy(k).wait()
        return 0

    lax.fori_loop(1, experts, gates_in, 0)

    def scale_rows(k, total):
        square = jnp.broadcast_to(gate_in[k, 0:1, :], (LANES, cap_dev))
        gate = jnp.transpose(square, (1, 0))[:, 0:1]
        rows_s[k] = (rows_s[k].astype(f32) * gate).astype(bf16)
        scaled = (grow_s[k].astype(f32) * gate).astype(bf16)
        grow_s[k] = scaled
        return total + jnp.sum(scaled.astype(f32), 0, keepdims=True)

    bias = lax.fori_loop(0, experts, scale_rows, jnp.zeros((1, width), f32))
    gbout_send[...] = jnp.broadcast_to(bias, gbout_send.shape)
    gbout_ref[me_t] = jnp.broadcast_to(bias, gbout_send.shape)
    rows_all = experts * cap_dev

    def grads(col):
        cols = pl.ds(pl.multiple_of(col, LANES), size)
        left = rows_s[...].reshape(rows_all, width)
        right = grow_s[...].reshape(rows_all, width)
        return dot_tn(left, slope[:, cols]), dot_tn(hid[:, cols], right)

    def column_sums(col):
        cols = pl.ds(pl.multiple_of(col, LANES), size)
        total = jnp.zeros((1, size), f32)
        for k in range(experts):
            square = jnp.broadcast_to(gate_in[k, 0:1, :], (LANES, cap_dev))
            gate = jnp.transpose(square, (1, 0))[:, 0:1]
            here = slice(cap_dev * k, cap_dev * (k + 1))
            total = total + jnp.sum(slope[here, cols].astype(f32) * gate, 0, keepdims=True)
        return total

    pending = []
    for j in list(range(1, cores)) + [0]:
        for n in range(per):
            cols = slice(size * n, size * (n + 1))
            slot = len(pending) % 2
            if len(pending) >= 2:
                for wait in pending[-2]:
                    wait()
            gw_in, gw_out = grads(share * j + size * n)
            stage_in[slot] = gw_in.astype(bf16)
            stage_out[slot] = gw_out.astype(bf16)
            sums = column_sums(share * j + size * n)
            if j == 0:
                gbin_own[:, cols] = sums
                a = pltpu.make_async_copy(stage_in.at[slot], gin_own.at[:, cols], own_sem.at[2 + slot])
                b = pltpu.make_async_copy(stage_out.at[slot], gout_own.at[cols, :], own_sem.at[4 + slot])
                a.start()
                b.start()
                pending.append((a.wait, b.wait))
            else:
                gbin_send[j - 1, :, cols] = sums
                at = (j - 1) * per + n
                a = remote(
                    stage_in.at[slot], gin_rest.at[j - 1, :, cols],
                    w_send.at[0, at], w_recv.at[0, at], core(j),
                )
                b = remote(
                    stage_out.at[slot], gout_rest.at[j - 1, cols, :],
                    w_send.at[1, at], w_recv.at[1, at], core(j),
                )
                a.start()
                b.start()
                pending.append((a.wait_send, b.wait_send))
        if j != 0:
            tail = [
                remote(
                    gbin_send.at[j - 1], gbin_rest.at[j - 1],
                    w_send.at[2, j - 1], w_recv.at[2, j - 1], core(j),
                ),
                remote(
                    gbout_send, gbout_ref.at[me_t],
                    w_send.at[3, j - 1], w_recv.at[3, j - 1], core(j),
                ),
            ]
            for copy in tail:
                copy.start()
    for waits in pending[-2:]:
        for wait in waits:
            wait()
    for j in range(1, cores):
        for n in range(per):
            cols = slice(size * n, size * (n + 1))
            at = (j - 1) * per + n
            remote(
                stage_in.at[0], gin_rest.at[j - 1, :, cols],
                w_send.at[0, at], w_recv.at[0, at], core(j),
            ).wait_recv()
            remote(
                stage_out.at[0], gout_rest.at[j - 1, cols, :],
                w_send.at[1, at], w_recv.at[1, at], core(j),
            ).wait_recv()
        remote(
            gbin_send.at[j - 1], gbin_rest.at[j - 1],
            w_send.at[2, j - 1], w_recv.at[2, j - 1], core(j),
        ).wait()
        remote(
            gbout_send, gbout_ref.at[me_t], w_send.at[3, j - 1], w_recv.at[3, j - 1], core(j)
        ).wait()

    def finish(k, _):
        r_copy(k).wait()
        g_copy(k).wait()
        return 0

    lax.fori_loop(1, experts, finish, 0)
    own_res.wait()
    own_grad.wait()


def swap_kernel(gather, count, *refs):
    srcs, dsts, (ssem, rsem) = refs[:count], refs[count : 2 * count], refs[2 * count :]
    n = lax.axis_size("tensor")
    me = lax.axis_index("tensor")
    barrier = pltpu.get_barrier_semaphore()
    for k in range(1, n):
        pl.semaphore_signal(
            barrier, inc=1, device_id={"tensor": lax.rem(me + k, n)}, device_id_type=MESH
        )
    pl.semaphore_wait(barrier, n - 1)
    copies = []
    for a, (src, dst) in enumerate(zip(srcs, dsts)):
        for k in range(1, n):
            copies.append(
                pltpu.make_async_remote_copy(
                    src_ref=src if gather else src.at[k - 1],
                    dst_ref=dst.at[k - 1],
                    send_sem=ssem.at[a, k],
                    recv_sem=rsem.at[a, k],
                    device_id={"tensor": lax.rem(me + (n - k if gather else k), n)},
                    device_id_type=MESH,
                )
            )
    for copy in copies:
        copy.start()
    for copy in copies:
        copy.wait()


def swap(ident, gather, *arrays):
    n = lax.axis_size("tensor")
    count = len(arrays)
    outs = [
        jax.ShapeDtypeStruct(((n - 1,) + a.shape) if gather else a.shape, a.dtype) for a in arrays
    ]
    anywhere = pl.BlockSpec(memory_space=pl.ANY)
    return pl.pallas_call(
        functools.partial(swap_kernel, gather, count),
        out_shape=outs,
        in_specs=[anywhere] * count,
        out_specs=[anywhere] * count,
        scratch_shapes=[pltpu.SemaphoreType.DMA((count, n)), pltpu.SemaphoreType.DMA((count, n))],
        compiler_params=pltpu.CompilerParams(collective_id=ident, has_side_effects=True),
        name="swap%d" % ident,
    )(*arrays)


def reduce_kernel(
    chunks, own_ref, rest_ref, small_ref, wqkv_ref, wproj_ref, small_out,
    rest_s, acc, send_s, recv_s, low, small_r, small_m, small_s, small_t,
    t_send, t_recv, x_send, x_recv, st_send, st_recv, sx_send, sx_recv, sg_send, sg_recv
):
    experts, _ = around("expert")
    cores, core = around("tensor")
    me_e = lax.axis_index("expert")
    me_t = lax.axis_index("tensor")
    bits = experts.bit_length() - 1
    rows_all = own_ref.shape[0]
    rows = rows_all // chunks
    piece_rows = small_r.shape[1]

    def my_bit(b):
        return lax.rem(me_e // (1 << b), 2)

    def partner(b):
        return {"expert": me_e + (1 << b) * (1 - 2 * my_bit(b))}

    def remote(src, dst, send, recv, there):
        return pltpu.make_async_remote_copy(
            src_ref=src, dst_ref=dst, send_sem=send, recv_sem=recv,
            device_id=there, device_id_type=MESH,
        )

    greet([partner(b) for b in range(bits)] + [core(k) for k in range(1, cores)])

    first = []
    for c in range(chunks):
        here = slice(rows * c, rows * (c + 1))
        first.append([
            remote(
                rest_ref.at[k - 1, here, :], rest_s.at[k - 1, here, :],
                t_send.at[k - 1, c], t_recv.at[k - 1, c], core(k),
            )
            for k in range(1, cores)
        ])
    smalls = [
        remote(
            small_ref.at[pl.ds(pl.multiple_of(lax.rem(me_t + k, cores) * piece_rows, 8), piece_rows), :],
            small_r.at[k - 1], st_send.at[k - 1], st_recv.at[k - 1], core(k),
        )
        for k in range(1, cores)
    ]
    for copy in smalls:
        copy.start()
    for group in first:
        for copy in group:
            copy.start()

    def gather_chunk(c):
        here = slice(rows * c, rows * (c + 1))
        for copy in first[c]:
            copy.wait()
        total = own_ref[here, :]
        for k in range(cores - 1):
            total = total + rest_s[k, here, :].astype(f32)
        acc[here, :] = total

    orders = []
    for c in range(chunks):
        order = list(range(bits))
        if c % 2 == 1 and bits > 1:
            order[0], order[1] = 1, 0
        orders.append(order)
    base = [0] * chunks
    live = {}

    def start(c, s):
        if s < bits:
            b = orders[c][s]
            half = rows >> (s + 1)
            off = rows - 2 * half
            away = pl.ds(pl.multiple_of(rows * c + base[c] + (1 - my_bit(b)) * half, 8), half)
            box = slice(off, off + half)
            send_s[c, box, :] = acc[away, :].astype(bf16)
            copy = remote(
                send_s.at[c, box, :], recv_s.at[c, box, :],
                x_send.at[c, s], x_recv.at[c, s], partner(b),
            )
        else:
            b = orders[c][2 * bits - 1 - s]
            size = rows >> (2 * bits - s)
            if s == bits:
                mine = pl.ds(pl.multiple_of(rows * c + base[c], 16), size)
                low[mine, :] = acc[mine, :].astype(bf16)
            mine = pl.ds(pl.multiple_of(rows * c + base[c], 16), size)
            copy = remote(
                low.at[mine, :], low.at[mine, :], x_send.at[c, s], x_recv.at[c, s], partner(b)
            )
        copy.start()
        live[c, s] = copy

    def finish(c, s):
        live[c, s].wait()
        if s < bits:
            b = orders[c][s]
            half = rows >> (s + 1)
            off = rows - 2 * half
            base[c] = base[c] + my_bit(b) * half
            keep = pl.ds(pl.multiple_of(rows * c + base[c], 8), half)
            acc[keep, :] += recv_s[c, off : off + half, :].astype(f32)
        else:
            b = orders[c][2 * bits - 1 - s]
            size = rows >> (2 * bits - s)
            base[c] = base[c] - my_bit(b) * size
            if s == 2 * bits - 1:
                width = rows_all // 4
                here = slice(rows * c, rows * (c + 1))
                if rows * (c + 1) <= 3 * width:
                    wqkv_ref[here, :] = low[here, :].astype(f32)
                else:
                    top = min(max(rows * c, 3 * width), rows * (c + 1))
                    if top > rows * c:
                        wqkv_ref[rows * c : top, :] = low[rows * c : top, :].astype(f32)
                    wproj_ref[:, top - 3 * width : rows * (c + 1) - 3 * width] = jnp.transpose(
                        low[top : rows * (c + 1), :].astype(f32), (1, 0)
                    )

    def small_start(s):
        small_s[s] = small_m[...]
        copy = remote(
            small_s.at[s], small_t.at[s], sx_send.at[s], sx_recv.at[s], partner(s)
        )
        copy.start()
        live["small", s] = copy

    def small_finish(s):
        live["small", s].wait()
        small_m[...] += small_t[s]

    pairs = max(chunks // 2, 1)
    members = [[c for c in (2 * p, 2 * p + 1) if c < chunks] for p in range(pairs)]
    stages = 2 * bits
    for t in range(stages + pairs):
        for p in range(pairs):
            s = t - p
            for c in members[p]:
                if s == 0:
                    gather_chunk(c)
                if 1 <= s <= stages:
                    finish(c, s - 1)
                if 0 <= s < stages:
                    start(c, s)
        if t == 0:
            for copy in smalls:
                copy.wait()
            total = small_ref[pl.ds(pl.multiple_of(me_t * piece_rows, 8), piece_rows), :]
            for k in range(cores - 1):
                total = total + small_r[k]
            small_m[...] = total
            small_start(0)
        elif t <= bits:
            small_finish(t - 1)
            if t < bits:
                small_start(t)
            else:
                mine = pl.ds(pl.multiple_of(me_t * piece_rows, 8), piece_rows)
                small_out[mine, :] = small_m[...]
                lasts = [
                    remote(
                        small_m, small_out.at[mine, :], sg_send.at[k - 1], sg_recv.at[k - 1], core(k)
                    )
                    for k in range(1, cores)
                ]
                for copy in lasts:
                    copy.start()
    for copy in lasts:
        copy.wait()


def on_device(
    tokens_in, valid, routes, ln1_gain, ln1_bias, w_query, w_key, w_value, b_query, b_value,
    w_proj, b_proj, ln2_gain, ln2_bias, w_router, w_in, b_in, w_out, b_out, cotangent,
):
    tok_rows, width = tokens_in.shape
    images, seq = valid.shape
    experts = lax.axis_size("expert")
    cores = lax.axis_size("tensor")
    core = lax.axis_index("tensor")
    capacity = (10 * tok_rows // (4 * experts) // 8 + 1) * 8
    cap_dev = up(up(capacity, cores) // cores, 16)
    rows_all = experts * cap_dev
    seq_pad = up(seq, 16)
    key_pad = up(seq_pad, LANES)
    own = images // cores
    tok_own = own * seq
    tok_pad = images * seq_pad
    pad_own = own * seq_pad
    share = w_in.shape[2]
    hidden = share * cores
    wide = width + LANES
    pairs = width // LANES
    S = jax.ShapeDtypeStruct

    def row(v):
        return v.reshape(1, -1)

    def a2a(rows):
        return lax.all_to_all(rows, "expert", split_axis=0, concat_axis=0, tiled=True)

    routes_p = jnp.pad(
        routes.reshape(images, seq, 2), ((0, 0), (0, seq_pad - seq), (0, 0)), constant_values=-1
    ).reshape(tok_pad, 2)
    send_g, post, fidx = pl.pallas_call(
        functools.partial(prep_kernel, (images, seq, seq_pad, experts, cap_dev)),
        out_shape=[
            S((experts, cap_dev, width), bf16),
            S((cores, experts, 1, pad_own), f32),
            S((tok_pad, 2), i32),
        ],
        scratch_shapes=[pltpu.VMEM((tok_pad, width), bf16)],
        compiler_params=params(),
        name="prep",
    )(routes_p, cotangent)
    def turn(x):
        return lax.rem(jnp.arange(experts), experts)

    me_e = lax.axis_index("expert")
    turned = (jnp.arange(experts) + experts - me_e) % experts
    grow = a2a(send_g[turned])
    grow = grow[(me_e + experts - jnp.arange(experts)) % experts]

    own_w = (w_query, w_key, w_value, w_proj)
    *rest_w, bqs, bvs = swap(1, True, *own_w, row(b_query), row(b_value))
    attn_w = [w for pair in zip(own_w, rest_w) for w in pair]
    bq = jnp.concatenate([row(b_query)] + [bqs[j] for j in range(cores - 1)], 1)
    bv = jnp.concatenate([row(b_value)] + [bvs[j] for j in range(cores - 1)], 1)
    w_ins, w_outs, b_ins = swap(7, True, w_in[0], w_out[0], b_in)
    wr = jnp.pad(w_router, ((0, 0), (0, LANES - experts)))
    valid_own = lax.dynamic_slice_in_dim(valid, core * own, own, 0)
    valid_col = jnp.pad(valid_own.astype(f32), ((0, 0), (0, seq_pad - seq)))[:, :, None]
    mask_row = jnp.where(
        jnp.pad(valid_own, ((0, 0), (0, key_pad - seq))) > 0, 0.0, MASKED
    ).astype(f32)[:, None, :]

    dims = (seq, seq_pad, key_pad, own, experts)

    def per_image(*shape):
        return pl.BlockSpec((1,) + shape, lambda i: (i,) + (0,) * len(shape))

    h1, q, k, v, probs, heads, middle, h2x, acc_f = pl.pallas_call(
        functools.partial(attn_fwd_kernel, dims),
        grid=(own,),
        in_specs=[
            whole(tokens_in.shape),
            per_image(seq_pad, 1),
            per_image(1, key_pad),
            whole((1, width)),
            whole((1, width)),
            *[whole(w.shape) for w in attn_w],
            whole((1, width)),
            whole((1, width)),
            whole((1, width)),
            whole((1, width)),
            whole((1, width)),
            whole((width, LANES)),
        ],
        out_specs=[
            per_image(seq_pad, width),
            per_image(seq_pad, width),
            per_image(key_pad, width),
            per_image(key_pad, width),
            per_image(pairs, 2 * seq_pad, key_pad),
            per_image(seq_pad, width),
            per_image(seq_pad, width),
            per_image(seq_pad, wide),
            whole((8, width)),
        ],
        out_shape=[
            S((own, seq_pad, width), bf16),
            S((own, seq_pad, width), bf16),
            S((own, key_pad, width), bf16),
            S((own, key_pad, width), bf16),
            S((own, pairs, 2 * seq_pad, key_pad), bf16),
            S((own, seq_pad, width), bf16),
            S((own, seq_pad, width), f32),
            S((own, seq_pad, wide), bf16),
            S((8, width), f32),
        ],
        scratch_shapes=[pltpu.VMEM((seq_pad, width), f32)],
        compiler_params=params(),
        cost_estimate=pl.CostEstimate(
            flops=2 * pad_own * width * (4 * width + 2 * key_pad),
            bytes_accessed=24 << 20,
            transcendentals=0,
        ),
        name="attn_fwd",
    )(
        tokens_in, valid_col, mask_row, row(ln1_gain), row(ln1_bias), *attn_w, bq, bv,
        row(b_proj), row(ln2_gain), row(ln2_bias), wr,
    )

    size = chunk_of(share)
    per = share // size
    anywhere = pl.BlockSpec(memory_space=pl.ANY)
    inside = pl.BlockSpec(memory_space=pltpu.VMEM)
    block = (experts, cap_dev, width)
    DMA = pltpu.SemaphoreType.DMA
    (
        res_back, grad_back, gslot, gin_w, gout_w, gin_rest, gout_rest, gbin_own, gbin_rest, gb_out,
    ) = pl.pallas_call(
        moe_kernel,
        in_specs=[anywhere, inside, anywhere] + [inside] * 7,
        out_specs=[anywhere, anywhere, inside] + [anywhere] * 4 + [inside] * 3,
        out_shape=[
            S(block, bf16),
            S(block, bf16),
            S((rows_all, 1), f32),
            S((width, share), bf16),
            S((share, width), bf16),
            S((cores - 1, width, share), bf16),
            S((cores - 1, share, width), bf16),
            S((1, share), f32),
            S((cores - 1, 1, share), f32),
            S((cores, 8, width), f32),
        ],
        scratch_shapes=[
            pltpu.VMEM((cores, pad_own, wide), bf16),
            pltpu.VMEM(block, bf16),
            pltpu.VMEM(block, bf16),
            pltpu.VMEM((rows_all, hidden), bf16),
            pltpu.VMEM((rows_all, hidden), bf16),
            pltpu.VMEM(block, bf16),
            pltpu.VMEM(block, bf16),
            pltpu.VMEM((experts, 8, cap_dev), f32),
            pltpu.VMEM((experts, 8, cap_dev), f32),
            pltpu.VMEM((2, width, size), bf16),
            pltpu.VMEM((2, size, width), bf16),
            pltpu.VMEM((cores - 1, 1, share), f32),
            pltpu.VMEM((8, width), f32),
            DMA((2,)),
            DMA((cores,)),
            DMA((cores,)),
            *[DMA((experts,))] * 8,
            DMA((4, (cores - 1) * per)),
            DMA((4, (cores - 1) * per)),
            DMA((6,)),
        ],
        compiler_params=params(collective_id=2, has_side_effects=True),
        name="moe",
    )(
        h2x.reshape(pad_own, wide), post, grow, w_in[0], w_ins, b_in, b_ins, w_out[0], w_outs, b_out
    )
    res_back = res_back.reshape(rows_all, width)
    grad_back = grad_back.reshape(rows_all, width)
    grad_w_in, grad_w_out = [
        (own_part.astype(f32) + jnp.sum(rest_part.astype(f32), 0))[None]
        for own_part, rest_part in ((gin_w, gin_rest), (gout_w, gout_rest))
    ]
    grad_b_in = gbin_own + jnp.sum(gbin_rest, 0)
    grad_b_out = jnp.sum(gb_out[:, 0, :], 0, keepdims=True)

    moe_own, moe_p, dots_own, dots_p = pl.pallas_call(
        functools.partial(combine_kernel, cap_dev, True),
        out_shape=[
            S((pad_own, width), bf16),
            S((cores - 1, pad_own, width), bf16),
            S((pad_own, LANES), bf16),
            S((cores - 1, pad_own, LANES), bf16),
        ],
        scratch_shapes=[pltpu.VMEM((rows_all, width), bf16), pltpu.VMEM((rows_all, LANES), bf16)],
        compiler_params=params(),
        name="combine_res",
    )(res_back, gslot, fidx, send_g.reshape(rows_all, width))
    moe, dots = swap(4, False, moe_p, dots_p)
    gmoe_own, gmoe_p = pl.pallas_call(
        functools.partial(combine_kernel, cap_dev, False),
        out_shape=[S((pad_own, width), bf16), S((cores - 1, pad_own, width), bf16)],
        scratch_shapes=[pltpu.VMEM((rows_all, width), bf16)],
        compiler_params=params(),
        name="combine_grad",
    )(grad_back, gslot, fidx)
    (gmoe,) = swap(5, False, gmoe_p)

    def pieces(n):
        return pl.BlockSpec((cores - 1, 1, seq_pad, n), lambda i: (0, i, 0, 0))

    def by_image(x):
        return x.reshape(x.shape[:-2] + (own, seq_pad, x.shape[-1]))

    head_share = w_query.shape[1]
    small_b = small_base(cores)
    small_rows = up(small_b + 8 + experts, 8 * cores)
    out_own, gin_own, grad_own, grad_rest, small = pl.pallas_call(
        functools.partial(attn_bwd_kernel, dims),
        grid=(own,),
        in_specs=[
            whole(tokens_in.shape),
            whole(cotangent.shape),
            per_image(seq_pad, 1),
            whole((8, width)),
            per_image(seq_pad, width),
            per_image(seq_pad, wide),
            per_image(seq_pad, width),
            per_image(seq_pad, width),
            per_image(key_pad, width),
            per_image(key_pad, width),
            per_image(pairs, 2 * seq_pad, key_pad),
            per_image(seq_pad, width),
            per_image(seq_pad, width),
            pieces(width),
            per_image(seq_pad, LANES),
            pieces(LANES),
            per_image(seq_pad, width),
            pieces(width),
            whole((1, width)),
            whole((1, width)),
            *[whole(w.shape) for w in attn_w],
            whole((width, LANES)),
        ],
        out_specs=[
            whole((tok_own, width)),
            whole((tok_own, width)),
            whole((4 * width, head_share)),
            whole((cores - 1, 4 * width, head_share)),
            whole((small_rows, width)),
        ],
        out_shape=[
            S((tok_own, width), f32),
            S((tok_own, width), f32),
            S((4 * width, head_share), f32),
            S((cores - 1, 4 * width, head_share), bf16),
            S((small_rows, width), f32),
        ],
        scratch_shapes=[pltpu.VMEM((seq_pad, width), f32)] * 2
        + [pltpu.VMEM((seq_pad, width), bf16)]
        + [pltpu.VMEM((pad_own, width), bf16)] * 6,
        compiler_params=params(),
        name="attn_bwd",
    )(
        tokens_in, cotangent, valid_col, acc_f, middle, h2x, h1, q, k, v, probs, heads,
        by_image(moe_own), by_image(moe), by_image(dots_own), by_image(dots),
        by_image(gmoe_own), by_image(gmoe), row(ln1_gain), row(ln2_gain), *attn_w, wr,
    )
    output = lax.all_gather(out_own, "tensor", axis=0, tiled=True)
    grad_input = lax.all_gather(gin_own, "tensor", axis=0, tiled=True)

    chunks = next(c for c in (4, 2, 1) if (4 * width // c // experts) % 16 == 0)
    bits = experts.bit_length() - 1
    piece_rows = small_rows // cores
    chunk_rows = 4 * width // chunks
    wqkv, grad_w_proj, small = pl.pallas_call(
        functools.partial(reduce_kernel, chunks),
        in_specs=[inside, anywhere, inside],
        out_specs=[inside] * 3,
        out_shape=[
            S((3 * width, head_share), f32),
            S((head_share, width), f32),
            S((small_rows, width), f32),
        ],
        scratch_shapes=[
            pltpu.VMEM((cores - 1, 4 * width, head_share), bf16),
            pltpu.VMEM((4 * width, head_share), f32),
            pltpu.VMEM((chunks, chunk_rows, head_share), bf16),
            pltpu.VMEM((chunks, chunk_rows, head_share), bf16),
            pltpu.VMEM((4 * width, head_share), bf16),
            pltpu.VMEM((cores - 1, piece_rows, width), f32),
            pltpu.VMEM((piece_rows, width), f32),
            pltpu.VMEM((bits, piece_rows, width), f32),
            pltpu.VMEM((bits, piece_rows, width), f32),
            DMA((cores - 1, chunks)),
            DMA((cores - 1, chunks)),
            DMA((chunks, 2 * bits)),
            DMA((chunks, 2 * bits)),
            DMA((cores - 1,)),
            DMA((cores - 1,)),
            DMA((bits,)),
            DMA((bits,)),
            DMA((cores - 1,)),
            DMA((cores - 1,)),
        ],
        compiler_params=params(collective_id=6, has_side_effects=True),
        name="reduce",
    )(grad_own, grad_rest, small)
    squares = jnp.sum(
        jnp.stack([small[small_b], small[small_b + 1], small[0], small[small_b + 2], small[1]]), -1
    )
    rms_values = jnp.sqrt(squares / (small[7, 0] * width))

    def mine(first):
        return lax.dynamic_slice(small, (first + core, 0), (1, head_share))[0]

    return (
        output,
        grad_input,
        small[5],
        small[6],
        wqkv[:width],
        wqkv[width : 2 * width],
        wqkv[2 * width :],
        mine(8),
        mine(8 + cores),
        grad_w_proj,
        small[4],
        small[2],
        small[3],
        jnp.transpose(small[small_b + 8 : small_b + 8 + experts]),
        grad_w_in,
        grad_b_in,
        grad_w_out,
        grad_b_out,
        rms_values,
    )


def solution(mesh):
    in_specs = (
        P("expert", None), P("expert", None), P("expert", None), P(), P(),
        P(None, "tensor"), P(None, "tensor"), P(None, "tensor"), P("tensor"), P("tensor"),
        P("tensor", None), P(), P(), P(), P(),
        P("expert", None, "tensor"), P("expert", "tensor"), P("expert", "tensor", None),
        P("expert", None), P("expert", None),
    )
    out_specs = (
        P("expert", None), P("expert", None), P(), P(),
        P(None, "tensor"), P(None, "tensor"), P(None, "tensor"), P("tensor"), P("tensor"),
        P("tensor", None), P(), P(), P(), P(),
        P("expert", None, "tensor"), P("expert", "tensor"), P("expert", "tensor", None),
        P("expert", None), P(),
    )
    return jax.shard_map(
        on_device, mesh=mesh, in_specs=in_specs, out_specs=out_specs, check_vma=False
    )
```

```python
import functools

import jax
import jax.numpy as jnp
from jax import lax
from jax.experimental import pallas as pl
from jax.experimental.pallas import tpu as pltpu
from jax.sharding import PartitionSpec as P

HEAD_DIM = 64
LANES = 128
LOG2E = 1.4426950408889634
MASKED = -1e30
MESH = pl.DeviceIdType.MESH
VMEM_LIMIT = 60 << 20
f32 = jnp.float32
bf16 = jnp.bfloat16
i32 = jnp.int32


def up(value, step):
    return -(-value // step) * step


def params(**more):
    return pltpu.CompilerParams(vmem_limit_bytes=VMEM_LIMIT, **more)


def whole(shape):
    return pl.BlockSpec(shape, lambda *_: (0,) * len(shape), pipeline_mode=pl.Buffered(1))


def dot(a, b):
    return lax.dot_general(a, b, (((1,), (0,)), ((), ())), preferred_element_type=f32)


def dot_nt(a, b):
    return lax.dot_general(a, b, (((1,), (1,)), ((), ())), preferred_element_type=f32)


def dot_tn(a, b):
    return lax.dot_general(a, b, (((0,), (0,)), ((), ())), preferred_element_type=f32)


def lane_iota(shape):
    return lax.broadcasted_iota(i32, shape, len(shape) - 1)


def norm_parts(values):
    center = values - jnp.mean(values, -1, keepdims=True)
    inv_std = lax.rsqrt(jnp.mean(center * center, -1, keepdims=True) + 1e-06)
    return center * inv_std, inv_std


def norm_back(grad_out, normed, inv_std, gain):
    scaled = grad_out * gain
    return inv_std * (
        scaled
        - jnp.mean(scaled, -1, keepdims=True)
        - normed * jnp.mean(scaled * normed, -1, keepdims=True)
    )


def gelu_parts(x):
    z = jnp.abs(x) * 0.7071067811865476
    t = 1.0 / (1.0 + 0.3275911 * z)
    poly = t * (
        0.254829592 * 0.5
        + t
        * (
            -0.284496736 * 0.5
            + t * (1.421413741 * 0.5 + t * (-1.453152027 * 0.5 + t * (1.061405429 * 0.5)))
        )
    )
    e = jnp.exp2(x * x * (-0.5 * LOG2E))
    half = poly * e
    cdf = jnp.where(x >= 0, 1.0 - half, half)
    return x * cdf, cdf + x * e * 0.3989422804014327


def prep_kernel(dims, routes_ref, cot_ref, grow_ref, post_ref, fidx_ref, g16):
    images, seq, seq_pad, experts, cap_dev = dims
    tok_pad = images * seq_pad
    core = lax.axis_index("tensor")
    expert = lax.axis_index("expert")
    for i in range(images):
        rows = cot_ref[seq * i : seq * (i + 1), :].astype(bf16)
        g16[seq_pad * i : seq_pad * (i + 1), :] = jnp.zeros((seq_pad, rows.shape[1]), bf16)
        g16[seq_pad * i : seq_pad * i + seq, :] = rows
    r0 = routes_ref[:, 0:1]
    r1 = routes_ref[:, 1:2]
    lanes = lane_iota((tok_pad, LANES))
    named0 = r0 == lanes
    named1 = r1 == lanes
    named = jnp.where(named0 | named1, 1.0, 0.0)
    named_low = named.astype(bf16)
    lower = (
        lax.broadcasted_iota(i32, (seq_pad, seq_pad), 1)
        < lax.broadcasted_iota(i32, (seq_pad, seq_pad), 0)
    ).astype(f32).astype(bf16)
    run = jnp.zeros((1, LANES), f32)
    parts = []
    for i in range(images):
        rows = slice(seq_pad * i, seq_pad * (i + 1))
        parts.append(dot(lower, named_low[rows]) + run)
        run = run + jnp.sum(named[rows], 0, keepdims=True)
    before = jnp.concatenate(parts, 0) - (core * cap_dev).astype(f32)
    pos = jnp.where(named > 0, before, -1.0)
    groups, _, _, group = post_ref.shape
    for j in range(groups):
        turned = jnp.transpose(pos[group * j : group * (j + 1)], (1, 0))
        for e in range(experts):
            post_ref[j, e] = turned[e : e + 1]
    for k, named_k, r_k in ((0, named0, r0), (1, named1, r1)):
        slot = jnp.sum(jnp.where(named_k, before, 0.0), 1, keepdims=True)
        fits = (slot >= 0) & (slot < cap_dev) & (r_k >= 0)
        turn = lax.rem(r_k - expert + experts, experts)
        flat = turn.astype(f32) * cap_dev + slot
        fidx_ref[:, k : k + 1] = jnp.where(fits, flat, -1.0).astype(i32)
    slots = lax.broadcasted_iota(i32, (cap_dev, group), 0).astype(f32)
    for e in range(experts):
        total = None
        for j in range(groups):
            named_e = post_ref[j, lax.rem(expert + e, experts)]
            pick = jnp.where(named_e == slots, 1.0, 0.0).astype(bf16)
            term = dot(pick, g16[group * j : group * (j + 1), :])
            total = term if total is None else total + term
        grow_ref[e] = total.astype(bf16)


def piece(own_ref, rest_ref, j):
    return own_ref[...] if j == 0 else rest_ref[j - 1]


def read_image(dst, src, image, seq):
    for n in range(src.shape[0] // seq):

        @pl.when(image == n)
        def _(n=n):
            dst[0:seq, :] = src[seq * n : seq * (n + 1), :]


def attn_fwd_kernel(
    dims, tok_ref, valid_ref, mask_ref, g1_ref, b1_ref, wq, wqs, wk, wks, wv, wvs, wp, wps,
    bq_ref, bv_ref, bp_ref, g2_ref, b2_ref, wr_ref,
    h1_ref, q_ref, k_ref, v_ref, probs_ref, heads_ref, mid_ref, h2x_ref, acc_ref, x_s
):
    seq, seq_pad, key_pad, own, experts = dims
    width = tok_ref.shape[1]
    step = pl.program_id(0)
    image = lax.axis_index("tensor") * own + step
    x_s[...] = jnp.zeros_like(x_s)
    read_image(x_s, tok_ref, image, seq)
    x = x_s[...]
    normed, _ = norm_parts(x)
    h1 = (normed * g1_ref[...] + b1_ref[...]).astype(bf16)
    h1_ref[0] = h1
    k_ref[0, seq_pad:, :] = jnp.zeros((key_pad - seq_pad, width), bf16)
    v_ref[0, seq_pad:, :] = jnp.zeros((key_pad - seq_pad, width), bf16)
    shares = [slice(wq.shape[1] * j, wq.shape[1] * (j + 1)) for j in range(wqs.shape[0] + 1)]
    for j, cols in enumerate(shares):
        q_ref[0, :, cols] = (dot(h1, piece(wq, wqs, j)) + bq_ref[:, cols]).astype(bf16)
        k_ref[0, 0:seq_pad, cols] = dot(h1, piece(wk, wks, j)).astype(bf16)
        v_ref[0, 0:seq_pad, cols] = (dot(h1, piece(wv, wvs, j)) + bv_ref[:, cols]).astype(bf16)
    low_half = lane_iota((seq_pad, LANES)) < HEAD_DIM
    mask = mask_ref[0]
    for p in range(width // LANES):
        cols = slice(LANES * p, LANES * (p + 1))
        qp = q_ref[0, :, cols]
        zero = jnp.zeros_like(qp)
        qs = jnp.concatenate([jnp.where(low_half, qp, zero), jnp.where(low_half, zero, qp)], 0)
        s = dot_nt(qs, k_ref[0, :, cols]) * (HEAD_DIM**-0.5 * LOG2E) + mask
        e = jnp.exp2(s - jnp.max(s, -1, keepdims=True))
        prob = (e * (1.0 / jnp.sum(e, -1, keepdims=True))).astype(bf16)
        probs_ref[0, p] = prob
        o = dot(prob, v_ref[0, :, cols])
        heads_ref[0, :, cols] = jnp.where(low_half, o[:seq_pad], o[seq_pad:]).astype(bf16)
    attn = bp_ref[...]
    for j, cols in enumerate(shares):
        attn = attn + dot(heads_ref[0, :, cols], piece(wp, wps, j))
    middle = x + attn
    mid_ref[0] = middle
    ok = valid_ref[0]

    @pl.when(step == 0)
    def _():
        acc_ref[...] = jnp.zeros_like(acc_ref)

    for row, field in enumerate((x, middle, attn)):
        acc_ref[row : row + 1, :] += jnp.sum(ok * field * field, 0, keepdims=True)
    normed2, _ = norm_parts(middle)
    h2 = (normed2 * g2_ref[...] + b2_ref[...]).astype(bf16)
    h2x_ref[0, :, 0:width] = h2
    logits = dot(h2, wr_ref[...])
    logits = jnp.where(lane_iota(logits.shape) < experts, logits, MASKED)
    e = jnp.exp(logits - jnp.max(logits, -1, keepdims=True))
    prob = e / jnp.sum(e, -1, keepdims=True)
    high = prob.astype(bf16).astype(f32)
    h2x_ref[0, :, width:] = (high + pltpu.roll(prob - high, experts, 1)).astype(bf16)


def attn_bwd_kernel(
    dims, tok_ref, cot_ref, valid_ref, accf_ref, mid_ref, h2x_ref, h1_ref, q_ref, k_ref, v_ref, probs_ref,
    heads_ref, moe_own, moe_ref, gmoe_own, gmoe_ref, gin_w, gin_ws, gout_w, gout_ws, g1_ref, g2_ref,
    wq, wqs, wk, wks, wv, wvs, wp, wps, wr_ref,
    out_ref, gin_ref, grad_own, grad_rest, acc_ref, gw_in_ref, gw_out_ref,
    x_s, c_s, gh_s, h1_s, heads_s, ga_s, dq_s, dk_s, dv_s
):
    seq, seq_pad, key_pad, own, experts = dims
    width = tok_ref.shape[1]
    step = pl.program_id(0)
    shares = [slice(wq.shape[1] * j, wq.shape[1] * (j + 1)) for j in range(wqs.shape[0] + 1)]
    small_b = small_base(len(shares))
    image = lax.axis_index("tensor") * own + step
    at = pl.multiple_of(step * seq_pad, 16)
    pad = jnp.zeros((seq_pad - seq + 8, width), f32)
    x_s[seq // 8 * 8 :, :] = pad[: seq_pad - seq // 8 * 8]
    c_s[seq // 8 * 8 :, :] = pad[: seq_pad - seq // 8 * 8]
    read_image(x_s, tok_ref, image, seq)
    read_image(c_s, cot_ref, image, seq)
    ok = valid_ref[0]

    @pl.when(step == 0)
    def _():
        acc_ref[...] = jnp.zeros_like(acc_ref)
        acc_ref[small_b : small_b + 8, :] = accf_ref[...]

    def add(row, value):
        acc_ref[row : row + 1, :] += jnp.sum(value, 0, keepdims=True)

    def total(own_ref, rest_ref, cols):
        value = own_ref[0, :, cols].astype(f32)
        for j in range(rest_ref.shape[0]):
            value = value + rest_ref[j, 0, :, cols].astype(f32)
        return value

    for sum_ref, own_ref, rest_ref in (
        (gw_in_ref, gin_w, gin_ws), (gw_out_ref, gout_w, gout_ws)
    ):
        value = own_ref[...].astype(f32)
        for j in range(rest_ref.shape[0]):
            value = value + rest_ref[j].astype(f32)
        sum_ref[0] = value

    middle = mid_ref[0]
    moe = total(moe_own, moe_ref, slice(0, width))
    output = middle + moe
    out_ref[0] = output
    add(0, ok * output * output)
    add(1, ok * moe * moe)
    h2 = h2x_ref[0, :, 0:width]
    pair = h2x_ref[0, :, width:].astype(f32)
    prob = jnp.where(
        lane_iota(pair.shape) < experts, pair + pltpu.roll(pair, LANES - experts, 1), 0.0
    )
    grad_probs = total(moe_own, moe_ref, slice(width, width + LANES))
    grad_logits = (
        prob * (grad_probs - jnp.sum(grad_probs * prob, -1, keepdims=True))
    ).astype(bf16)
    acc_ref[small_b + 8 : small_b + 8 + experts, :] += dot_tn(grad_logits, h2)[:experts]
    grad_h2 = dot_nt(grad_logits, wr_ref[...]) + total(gmoe_own, gmoe_ref, slice(0, width))
    normed2, inv2 = norm_parts(middle)
    add(2, grad_h2 * normed2)
    add(3, grad_h2)
    grad_middle = c_s[...] + norm_back(grad_h2, normed2, inv2, g2_ref[...])
    c_s[...] = grad_middle
    grad_attn = grad_middle.astype(bf16)
    add(4, grad_attn.astype(f32))
    ga_s[pl.ds(at, seq_pad), :] = grad_attn
    heads_s[pl.ds(at, seq_pad), :] = heads_ref[0]
    h1_s[pl.ds(at, seq_pad), :] = h1_ref[0]
    for j, cols in enumerate(shares):
        gh_s[:, cols] = dot_nt(grad_attn, piece(wp, wps, j)).astype(bf16)
    low_half = lane_iota((seq_pad, LANES)) < HEAD_DIM

    def split(value):
        zero = jnp.zeros_like(value)
        return jnp.concatenate(
            [jnp.where(low_half, value, zero), jnp.where(low_half, zero, value)], 0
        )

    for p in range(width // LANES):
        cols = slice(LANES * p, LANES * (p + 1))
        gs = split(gh_s[:, cols])
        qs = split(q_ref[0, :, cols])
        low_prob = probs_ref[0, p]
        weights = low_prob.astype(f32)
        mixed = weights * dot_nt(gs, v_ref[0, :, cols])
        ds = (
            (mixed - weights * jnp.sum(mixed, -1, keepdims=True)) * (HEAD_DIM**-0.5)
        ).astype(bf16)
        dq = dot(ds, k_ref[0, :, cols])
        dq_s[pl.ds(at, seq_pad), cols] = jnp.where(
            low_half, dq[:seq_pad], dq[seq_pad:]
        ).astype(bf16)
        dk_s[pl.ds(at, seq_pad), cols] = dot_tn(ds, qs)[:seq_pad].astype(bf16)
        dv_s[pl.ds(at, seq_pad), cols] = dot_tn(low_prob, gs)[:seq_pad].astype(bf16)
    dq = dq_s[pl.ds(at, seq_pad), :]
    dk = dk_s[pl.ds(at, seq_pad), :]
    dv = dv_s[pl.ds(at, seq_pad), :]
    which = lax.broadcasted_iota(i32, (small_b, shares[0].stop), 0)
    for j, cols in enumerate(shares):
        owner = lax.rem(lax.axis_index("tensor") + j, len(shares))
        for base, value in ((8, dq), (8 + len(shares), dv)):
            total_j = jnp.sum(value[:, cols].astype(f32), 0, keepdims=True)
            acc_ref[0:small_b, shares[0]] += jnp.where(which == base + owner, total_j, 0.0)
    grad_h1 = None
    for j, cols in enumerate(shares):
        for left, own_ref, rest_ref in ((dq, wq, wqs), (dk, wk, wks), (dv, wv, wvs)):
            term = dot_nt(left[:, cols], piece(own_ref, rest_ref, j))
            grad_h1 = term if grad_h1 is None else grad_h1 + term
    normed1, inv1 = norm_parts(x_s[...])
    add(5, grad_h1 * normed1)
    add(6, grad_h1)
    add(7, jnp.broadcast_to(ok, grad_h1.shape))
    grad_in = c_s[...] + norm_back(grad_h1, normed1, inv1, g1_ref[...])
    gin_ref[0] = grad_in

    @pl.when(step == own - 1)
    def _():
        for n, part in enumerate((dq_s, dk_s, dv_s, heads_s)):
            rows = slice(width * n, width * (n + 1))
            left = ga_s if n == 3 else h1_s
            grad = dot_tn(left[...], part[...])
            grad_own[rows, :] = grad[:, shares[0]]
            for j, cols in enumerate(shares[1:]):
                grad_rest[j, rows, :] = grad[:, cols].astype(bf16)


def small_base(cores):
    return up(8 + 2 * cores, 8)


def view(own_ref, rest_ref, j):
    return own_ref if j == 0 else rest_ref.at[j - 1]


def chunk_of(hidden):
    for size in (512, 384, 256, 128):
        if hidden % size == 0:
            return size
    return hidden


def greet(peers):
    barrier = pltpu.get_barrier_semaphore()
    for peer in peers:
        pl.semaphore_signal(barrier, inc=1, device_id=peer, device_id_type=MESH)
    pl.semaphore_wait(barrier, len(peers))


def around(axis):
    n = lax.axis_size(axis)
    me = lax.axis_index(axis)
    return n, lambda k: {axis: lax.rem(me + n + k, n)}


def moe_kernel(
    h2x_ref, post_ref, grow_hbm, sent_hbm, fidx_ref, w_in, w_ins, b_in, b_ins, w_out, w_outs,
    b_out_ref,
    back_ref, gback_ref, gin_own, gout_own, gin_rest, gout_rest,
    gbin_own, gbin_rest, gbout_ref, moe_own, moe_rest, gmoe_own, gmoe_rest,
    table, out_s, rows_s, grow_s, res_s, gate_out, gate_in, gslot_ref,
    gbin_send, gbout_send,
    m_send, m_recv, load_sem, local_sem, tab_send, tab_recv, h_send, h_recv, c_send, c_recv, r_send, r_recv, g_send, g_recv,
    w_send, w_recv, own_sem
):
    experts, chip = around("expert")
    cores, core = around("tensor")
    me_e = lax.axis_index("expert")
    me_t = lax.axis_index("tensor")
    cap_dev, width = rows_s.shape[1:]
    group = table.shape[1]
    share = w_in.shape[1]
    size = chunk_of(share)
    per = share // size
    greet([chip(k) for k in range(1, experts)] + [core(k) for k in range(1, cores)])

    def remote(src, dst, send, recv, there):
        return pltpu.make_async_remote_copy(
            src_ref=src, dst_ref=dst, send_sem=send, recv_sem=recv,
            device_id=there, device_id_type=MESH,
        )

    grow_copy = pltpu.make_async_copy(grow_hbm, grow_s, local_sem.at[0])
    grow_copy.start()
    own_copy = pltpu.make_async_copy(h2x_ref, table.at[me_t], local_sem.at[1])
    own_copy.start()
    fills = [
        remote(h2x_ref, table.at[me_t], tab_send.at[k], tab_recv.at[k], core(k))
        for k in range(1, cores)
    ]
    for copy in fills:
        copy.start()
    own_copy.wait()
    for copy in fills:
        copy.wait()

    slots = lax.broadcasted_iota(i32, (cap_dev, group), 0).astype(f32)
    lanes = lane_iota((cap_dev, LANES))

    def select(k):
        e = lax.rem(me_e + k, experts)
        total = None
        for j in range(cores):
            pick = jnp.where(post_ref[j, e] == slots, 1.0, 0.0).astype(bf16)
            term = dot(pick, table[j])
            total = term if total is None else total + term
        mine = (lanes == e) | (lanes == e + experts)
        gate = jnp.sum(jnp.where(mine, total[:, width:], 0.0), 1, keepdims=True)
        gslot_ref[pl.ds(pl.multiple_of(cap_dev * k, 8), cap_dev), :] = gate
        spread = jnp.transpose(jnp.broadcast_to(gate, (cap_dev, LANES)), (1, 0))
        return total[:, :width].astype(bf16), spread[0:8]

    def h_copy(k):
        return remote(out_s.at[k], rows_s.at[k], h_send.at[k], h_recv.at[k], chip(k))

    def c_copy(k):
        return remote(gate_out.at[k], gate_in.at[k], c_send.at[k], c_recv.at[k], chip(k))

    def r_copy(k):
        return remote(res_s.at[k], back_ref.at[k], r_send.at[k], r_recv.at[k], chip(-k))

    def g_copy(k):
        return remote(out_s.at[k], gback_ref.at[k], g_send.at[k], g_recv.at[k], chip(-k))

    def far(j):
        return lax.rem(j + experts // 2, experts)

    def send_rows(j, _):
        k = far(j)
        rows, gate = select(k)
        out_s[k] = rows
        gate_out[k] = gate

        @pl.when(k > 0)
        def _():
            h_copy(k).start()
            c_copy(k).start()

        return 0

    lax.fori_loop(0, experts, send_rows, 0)
    rows_s[0] = out_s[0]
    gate_in[0] = gate_out[0]
    pl.run_scoped(
        functools.partial(
            expert_phase, locals_of(
                experts=experts, cores=cores, core=core, me_t=me_t, width=width, cap_dev=cap_dev,
                share=share, size=size, per=per, w_in=w_in, w_ins=w_ins, b_in=b_in, b_ins=b_ins,
                w_out=w_out, w_outs=w_outs, b_out_ref=b_out_ref, rows_s=rows_s, res_s=res_s,
                back_ref=back_ref, own_sem=own_sem, h_copy=h_copy, r_copy=r_copy, c_copy=c_copy,
                g_copy=g_copy, grow_copy=grow_copy, grow_s=grow_s, out_s=out_s,
                gback_ref=gback_ref, gate_in=gate_in, gbout_send=gbout_send, gbout_ref=gbout_ref,
                gbin_own=gbin_own, gbin_send=gbin_send, gbin_rest=gbin_rest, gin_own=gin_own,
                gout_own=gout_own, gin_rest=gin_rest, gout_rest=gout_rest, w_send=w_send,
                w_recv=w_recv, remote=remote, far=far,
            ),
        ),
        pltpu.VMEM((experts * cap_dev, share * cores), bf16),
        pltpu.VMEM((experts * cap_dev, share * cores), bf16),
        pltpu.VMEM((2, width, size), bf16),
        pltpu.VMEM((2, size, width), bf16),
    )
    rows_all = experts * cap_dev
    wide = width + LANES

    def token_phase(picks, values, total):
        loads = [
            pltpu.make_async_copy(sent_hbm, grow_s, load_sem.at[0]),
            pltpu.make_async_copy(back_ref, rows_s, load_sem.at[1]),
        ]
        loads[0].start()

        def arrived(k, _):
            r_copy(k).wait()
            return 0

        lax.fori_loop(1, experts, arrived, 0)
        loads[1].start()
        step = 208 if group % 208 == 0 else group
        tiles = group // step
        slot_lanes = lane_iota((step, rows_all))

        def make_picks(i, _):
            tok = pl.ds(pl.multiple_of(i * step, 16), step)
            hit = (fidx_ref[tok, 0:1] == slot_lanes) | (fidx_ref[tok, 1:2] == slot_lanes)
            picks[tok, :] = jnp.where(hit, 1.0, 0.0).astype(bf16)
            return 0

        lax.fori_loop(0, cores * tiles, make_picks, 0)
        for copy in loads:
            copy.wait()

        def gated(k):
            return gslot_ref[pl.ds(pl.multiple_of(cap_dev * k, 8), cap_dev), :]

        def weigh(k, _):
            rows = rows_s[k].astype(f32)
            dots = jnp.sum(rows * grow_s[k].astype(f32), 1, keepdims=True)
            here = pl.ds(pl.multiple_of(cap_dev * k, 16), cap_dev)
            values[here, 0:width] = (rows * gated(k)).astype(bf16)
            mine = lanes == lax.rem(me_e + k, experts)
            values[here, width:] = jnp.where(mine, dots, 0.0).astype(bf16)
            return 0

        lax.fori_loop(0, experts, weigh, 0)

        def m_copy(kind, k):
            source = table.at[k] if kind == 0 else table.at[k, :, 0:width]
            return remote(
                source, (moe_rest, gmoe_rest)[kind].at[k - 1],
                m_send.at[kind, k - 1], m_recv.at[kind, k - 1], core(k),
            )

        keep_moe = pltpu.make_async_copy(table.at[0], moe_own, load_sem.at[0])
        keep_gmoe = pltpu.make_async_copy(table.at[0, :, 0:width], gmoe_own, load_sem.at[0])

        for k in list(range(1, cores)) + [0]:

            def sums(i, _, k=k):
                tok = pl.ds(
                    pl.multiple_of(lax.rem(me_t + k, cores) * group + i * step, 16), step
                )
                to = pl.ds(pl.multiple_of(i * step, 16), step)
                table[k, to, :] = dot(picks[tok, :], values[...]).astype(bf16)
                return 0

            lax.fori_loop(0, tiles, sums, 0)
            if k > 0:
                m_copy(0, k).start()
        keep_moe.start()
        keep_moe.wait()
        for k in range(1, cores):
            m_copy(0, k).wait()

        batch = 4
        batches = experts // batch
        for b in range(batches):
            first = (b * batch + experts // 2) % experts
            for k in range(first, first + batch):
                if k > 0:
                    g_copy(k).wait_recv()
                else:
                    own_grad.wait()
            box = pl.ds(first, batch)
            load = pltpu.make_async_copy(gback_ref.at[box], rows_s.at[box], load_sem.at[0])
            load.start()
            load.wait()
            cols = slice(cap_dev * first, cap_dev * (first + batch))
            for k in range(first, first + batch):
                rows_s[k] = (rows_s[k].astype(f32) * gated(k)).astype(bf16)
            for k in list(range(1, cores)) + [0]:

                def gsums(i, _, k=k, b=b, cols=cols, box=box):
                    tok = pl.ds(
                        pl.multiple_of(lax.rem(me_t + k, cores) * group + i * step, 16), step
                    )
                    to = pl.ds(pl.multiple_of(i * step, 16), step)
                    rows = rows_s[box].reshape(batch * cap_dev, width)
                    value = dot(picks[tok, cols], rows)
                    if b > 0:
                        value = value + total[tok, :]
                    if b < batches - 1:
                        total[tok, :] = value
                    else:
                        table[k, to, 0:width] = value.astype(bf16)
                    return 0

                lax.fori_loop(0, tiles, gsums, 0)
                if b == batches - 1 and k > 0:
                    m_copy(1, k).start()
        keep_gmoe.start()
        keep_gmoe.wait()
        for k in range(1, cores):
            m_copy(1, k).wait()

        def finish(k, _):
            g_copy(k).wait_send()
            return 0

        lax.fori_loop(1, experts, finish, 0)

    own_grad = pltpu.make_async_copy(out_s.at[0], gback_ref.at[0], own_sem.at[1])
    pl.run_scoped(
        token_phase,
        pltpu.VMEM((cores * group, rows_all), bf16),
        pltpu.VMEM((rows_all, wide), bf16),
        pltpu.VMEM((cores * group, width), f32),
    )


class Bag:
    pass


def locals_of(**names):
    bag = Bag()
    bag.__dict__.update(names)
    return bag


def expert_phase(at, hid, slope, stage_in, stage_out):
    experts, cores, core, me_t, width, cap_dev = (
        at.experts, at.cores, at.core, at.me_t, at.width, at.cap_dev
    )
    share, size, per, far, remote = at.share, at.size, at.per, at.far, at.remote
    w_in, w_ins, b_in, b_ins, w_out, w_outs = at.w_in, at.w_ins, at.b_in, at.b_ins, at.w_out, at.w_outs
    b_out_ref, rows_s, res_s, back_ref, own_sem = at.b_out_ref, at.rows_s, at.res_s, at.back_ref, at.own_sem
    h_copy, r_copy, c_copy, g_copy, grow_copy = at.h_copy, at.r_copy, at.c_copy, at.g_copy, at.grow_copy
    grow_s, out_s, gback_ref, gate_in = at.grow_s, at.out_s, at.gback_ref, at.gate_in
    gbout_send, gbout_ref, gbin_own, gbin_send, gbin_rest = (
        at.gbout_send, at.gbout_ref, at.gbin_own, at.gbin_send, at.gbin_rest
    )
    gin_own, gout_own, gin_rest, gout_rest = at.gin_own, at.gout_own, at.gin_rest, at.gout_rest
    w_send, w_recv = at.w_send, at.w_recv

    def forward(i):
        x = rows_s[pl.ds(2 * i, 2)].reshape(2 * cap_dev, width)
        here = pl.ds(pl.multiple_of(2 * cap_dev * i, 16), 2 * cap_dev)
        total = None
        for j in range(cores):
            for n in range(per):
                cols = slice(size * n, size * (n + 1))
                flat = slice(share * j + size * n, share * j + size * (n + 1))
                pre = dot(x, view(w_in, w_ins, j)[:, cols]) + view(b_in, b_ins, j)[:, cols]
                act, steep = gelu_parts(pre)
                act = act.astype(bf16)
                hid[here, flat] = act
                slope[here, flat] = steep.astype(bf16)
                term = dot(act, view(w_out, w_outs, j)[cols, :])
                total = term if total is None else total + term
        res = (total + b_out_ref[...]).astype(bf16)
        res_s[pl.ds(2 * i, 2)] = res.reshape(2, cap_dev, width)

    own_res = pltpu.make_async_copy(res_s.at[0], back_ref.at[0], own_sem.at[0])

    def forward_step(j, _):
        i = lax.rem(j + experts // 4, experts // 2)

        @pl.when(i > 0)
        def _():
            h_copy(2 * i).wait_recv()

        h_copy(2 * i + 1).wait_recv()
        forward(i)

        @pl.when(i > 0)
        def _():
            r_copy(2 * i).start()

        @pl.when(i == 0)
        def _():
            own_res.start()

        r_copy(2 * i + 1).start()
        return 0

    lax.fori_loop(0, experts // 2, forward_step, 0)

    def sent_rows(k, _):
        h_copy(k).wait_send()
        return 0

    lax.fori_loop(1, experts, sent_rows, 0)
    grow_copy.wait()

    def backward(i):
        g = grow_s[pl.ds(2 * i, 2)].reshape(2 * cap_dev, width)
        here = pl.ds(pl.multiple_of(2 * cap_dev * i, 16), 2 * cap_dev)
        total = None
        for j in range(cores):
            for n in range(per):
                cols = slice(size * n, size * (n + 1))
                flat = slice(share * j + size * n, share * j + size * (n + 1))
                grad = dot_nt(g, view(w_out, w_outs, j)[cols, :])
                gpre = (grad * slope[here, flat].astype(f32)).astype(bf16)
                slope[here, flat] = gpre
                term = dot_nt(gpre, view(w_in, w_ins, j)[:, cols])
                total = term if total is None else total + term
        out_s[pl.ds(2 * i, 2)] = total.astype(bf16).reshape(2, cap_dev, width)

    own_grad = pltpu.make_async_copy(out_s.at[0], gback_ref.at[0], own_sem.at[1])

    def backward_step(j, _):
        i = lax.rem(j + experts // 4, experts // 2)
        backward(i)

        @pl.when(i > 0)
        def _():
            g_copy(2 * i).start()

        @pl.when(i == 0)
        def _():
            own_grad.start()

        g_copy(2 * i + 1).start()
        return 0

    lax.fori_loop(0, experts // 2, backward_step, 0)

    def gates_in(k, _):
        c_copy(k).wait()
        return 0

    lax.fori_loop(1, experts, gates_in, 0)

    def scale_rows(k, total):
        square = jnp.broadcast_to(gate_in[k, 0:1, :], (LANES, cap_dev))
        gate = jnp.transpose(square, (1, 0))[:, 0:1]
        rows_s[k] = (rows_s[k].astype(f32) * gate).astype(bf16)
        scaled = (grow_s[k].astype(f32) * gate).astype(bf16)
        grow_s[k] = scaled
        return total + jnp.sum(scaled.astype(f32), 0, keepdims=True)

    bias = lax.fori_loop(0, experts, scale_rows, jnp.zeros((1, width), f32))
    gbout_send[...] = jnp.broadcast_to(bias, gbout_send.shape)
    gbout_ref[me_t] = jnp.broadcast_to(bias, gbout_send.shape)
    rows_all = experts * cap_dev

    def grads(col):
        cols = pl.ds(pl.multiple_of(col, LANES), size)
        left = rows_s[...].reshape(rows_all, width)
        right = grow_s[...].reshape(rows_all, width)
        return dot_tn(left, slope[:, cols]), dot_tn(hid[:, cols], right)

    def column_sums(col):
        cols = pl.ds(pl.multiple_of(col, LANES), size)
        total = jnp.zeros((1, size), f32)
        for k in range(experts):
            square = jnp.broadcast_to(gate_in[k, 0:1, :], (LANES, cap_dev))
            gate = jnp.transpose(square, (1, 0))[:, 0:1]
            here = slice(cap_dev * k, cap_dev * (k + 1))
            total = total + jnp.sum(slope[here, cols].astype(f32) * gate, 0, keepdims=True)
        return total

    pending = []
    for j in list(range(1, cores)) + [0]:
        for n in range(per):
            cols = slice(size * n, size * (n + 1))
            slot = len(pending) % 2
            if len(pending) >= 2:
                for wait in pending[-2]:
                    wait()
            gw_in, gw_out = grads(share * j + size * n)
            stage_in[slot] = gw_in.astype(bf16)
            stage_out[slot] = gw_out.astype(bf16)
            sums = column_sums(share * j + size * n)
            if j == 0:
                gbin_own[:, cols] = sums
                a = pltpu.make_async_copy(stage_in.at[slot], gin_own.at[:, cols], own_sem.at[2 + slot])
                b = pltpu.make_async_copy(stage_out.at[slot], gout_own.at[cols, :], own_sem.at[4 + slot])
                a.start()
                b.start()
                pending.append((a.wait, b.wait))
            else:
                gbin_send[j - 1, :, cols] = sums
                at = (j - 1) * per + n
                a = remote(
                    stage_in.at[slot], gin_rest.at[j - 1, :, cols],
                    w_send.at[0, at], w_recv.at[0, at], core(j),
                )
                b = remote(
                    stage_out.at[slot], gout_rest.at[j - 1, cols, :],
                    w_send.at[1, at], w_recv.at[1, at], core(j),
                )
                a.start()
                b.start()
                pending.append((a.wait_send, b.wait_send))
        if j != 0:
            tail = [
                remote(
                    gbin_send.at[j - 1], gbin_rest.at[j - 1],
                    w_send.at[2, j - 1], w_recv.at[2, j - 1], core(j),
                ),
                remote(
                    gbout_send, gbout_ref.at[me_t],
                    w_send.at[3, j - 1], w_recv.at[3, j - 1], core(j),
                ),
            ]
            for copy in tail:
                copy.start()
    for waits in pending[-2:]:
        for wait in waits:
            wait()
    for j in range(1, cores):
        for n in range(per):
            cols = slice(size * n, size * (n + 1))
            at = (j - 1) * per + n
            remote(
                stage_in.at[0], gin_rest.at[j - 1, :, cols],
                w_send.at[0, at], w_recv.at[0, at], core(j),
            ).wait_recv()
            remote(
                stage_out.at[0], gout_rest.at[j - 1, cols, :],
                w_send.at[1, at], w_recv.at[1, at], core(j),
            ).wait_recv()
        remote(
            gbin_send.at[j - 1], gbin_rest.at[j - 1],
            w_send.at[2, j - 1], w_recv.at[2, j - 1], core(j),
        ).wait()
        remote(
            gbout_send, gbout_ref.at[me_t], w_send.at[3, j - 1], w_recv.at[3, j - 1], core(j)
        ).wait()

    own_res.wait()


def swap_kernel(gather, count, *refs):
    srcs, dsts, (ssem, rsem) = refs[:count], refs[count : 2 * count], refs[2 * count :]
    n = lax.axis_size("tensor")
    me = lax.axis_index("tensor")
    barrier = pltpu.get_barrier_semaphore()
    for k in range(1, n):
        pl.semaphore_signal(
            barrier, inc=1, device_id={"tensor": lax.rem(me + k, n)}, device_id_type=MESH
        )
    pl.semaphore_wait(barrier, n - 1)
    copies = []
    for a, (src, dst) in enumerate(zip(srcs, dsts)):
        for k in range(1, n):
            copies.append(
                pltpu.make_async_remote_copy(
                    src_ref=src if gather else src.at[k - 1],
                    dst_ref=dst.at[k - 1],
                    send_sem=ssem.at[a, k],
                    recv_sem=rsem.at[a, k],
                    device_id={"tensor": lax.rem(me + (n - k if gather else k), n)},
                    device_id_type=MESH,
                )
            )
    for copy in copies:
        copy.start()
    for copy in copies:
        copy.wait()


def swap(ident, gather, *arrays):
    n = lax.axis_size("tensor")
    count = len(arrays)
    outs = [
        jax.ShapeDtypeStruct(((n - 1,) + a.shape) if gather else a.shape, a.dtype) for a in arrays
    ]
    anywhere = pl.BlockSpec(memory_space=pl.ANY)
    return pl.pallas_call(
        functools.partial(swap_kernel, gather, count),
        out_shape=outs,
        in_specs=[anywhere] * count,
        out_specs=[anywhere] * count,
        scratch_shapes=[pltpu.SemaphoreType.DMA((count, n)), pltpu.SemaphoreType.DMA((count, n))],
        compiler_params=pltpu.CompilerParams(collective_id=ident, has_side_effects=True),
        name="swap%d" % ident,
    )(*arrays)


def reduce_kernel(
    chunks, own_ref, rest_ref, small_ref, out_ref, gin_ref, low, small_out, outs_ref, gins_ref,
    rest_s, acc, send_s, recv_s, small_r, small_m, small_s, small_t,
    t_send, t_recv, x_send, x_recv, st_send, st_recv, sx_send, sx_recv, sg_send, sg_recv,
    o_send, o_recv
):
    experts, _ = around("expert")
    cores, core = around("tensor")
    me_e = lax.axis_index("expert")
    me_t = lax.axis_index("tensor")
    bits = experts.bit_length() - 1
    rows_all = own_ref.shape[0]
    rows = rows_all // chunks
    piece_rows = small_r.shape[1]

    def my_bit(b):
        return lax.rem(me_e // (1 << b), 2)

    def partner(b):
        return {"expert": me_e + (1 << b) * (1 - 2 * my_bit(b))}

    def remote(src, dst, send, recv, there):
        return pltpu.make_async_remote_copy(
            src_ref=src, dst_ref=dst, send_sem=send, recv_sem=recv,
            device_id=there, device_id_type=MESH,
        )

    greet([partner(b) for b in range(bits)] + [core(k) for k in range(1, cores)])

    first = []
    for c in range(chunks):
        here = slice(rows * c, rows * (c + 1))
        first.append([
            remote(
                rest_ref.at[k - 1, here, :], rest_s.at[k - 1, here, :],
                t_send.at[k - 1, c], t_recv.at[k - 1, c], core(k),
            )
            for k in range(1, cores)
        ])
    smalls = [
        remote(
            small_ref.at[pl.ds(pl.multiple_of(lax.rem(me_t + k, cores) * piece_rows, 8), piece_rows), :],
            small_r.at[k - 1], st_send.at[k - 1], st_recv.at[k - 1], core(k),
        )
        for k in range(1, cores)
    ]
    for copy in smalls:
        copy.start()
    for group in first:
        for copy in group:
            copy.start()

    tokens = [
        remote(src, dst.at[k - 1], o_send.at[n, k - 1], o_recv.at[n, k - 1], core(k))
        for k in range(1, cores)
        for n, (src, dst) in enumerate(((gin_ref, gins_ref), (out_ref, outs_ref)))
    ]
    for copy in tokens:
        copy.start()

    def gather_chunk(c):
        here = slice(rows * c, rows * (c + 1))
        for copy in first[c]:
            copy.wait()
        total = own_ref[here, :]
        for k in range(cores - 1):
            total = total + rest_s[k, here, :].astype(f32)
        acc[here, :] = total

    orders = []
    for c in range(chunks):
        order = list(range(bits))
        if c % 2 == 1 and bits > 1:
            order[0], order[1] = 1, 0
        orders.append(order)
    base = [0] * chunks
    live = {}

    def start(c, s):
        if s < bits:
            b = orders[c][s]
            half = rows >> (s + 1)
            off = rows - 2 * half
            away = pl.ds(pl.multiple_of(rows * c + base[c] + (1 - my_bit(b)) * half, 8), half)
            box = slice(off, off + half)
            send_s[c, box, :] = acc[away, :].astype(bf16)
            copy = remote(
                send_s.at[c, box, :], recv_s.at[c, box, :],
                x_send.at[c, s], x_recv.at[c, s], partner(b),
            )
        else:
            b = orders[c][2 * bits - 1 - s]
            size = rows >> (2 * bits - s)
            if s == bits:
                mine = pl.ds(pl.multiple_of(rows * c + base[c], 16), size)
                low[mine, :] = acc[mine, :].astype(bf16)
            mine = pl.ds(pl.multiple_of(rows * c + base[c], 16), size)
            copy = remote(
                low.at[mine, :], low.at[mine, :], x_send.at[c, s], x_recv.at[c, s], partner(b)
            )
        copy.start()
        live[c, s] = copy

    def finish(c, s):
        live[c, s].wait()
        if s < bits:
            b = orders[c][s]
            half = rows >> (s + 1)
            off = rows - 2 * half
            base[c] = base[c] + my_bit(b) * half
            keep = pl.ds(pl.multiple_of(rows * c + base[c], 8), half)
            acc[keep, :] += recv_s[c, off : off + half, :].astype(f32)
        else:
            b = orders[c][2 * bits - 1 - s]
            size = rows >> (2 * bits - s)
            base[c] = base[c] - my_bit(b) * size

    def small_start(s):
        small_s[s] = small_m[...]
        copy = remote(
            small_s.at[s], small_t.at[s], sx_send.at[s], sx_recv.at[s], partner(s)
        )
        copy.start()
        live["small", s] = copy

    def small_finish(s):
        live["small", s].wait()
        small_m[...] += small_t[s]

    pairs = max(chunks // 2, 1)
    members = [[c for c in (2 * p, 2 * p + 1) if c < chunks] for p in range(pairs)]
    stages = 2 * bits
    for t in range(stages + pairs):
        for p in range(pairs):
            s = t - p
            for c in members[p]:
                if s == 0:
                    gather_chunk(c)
                if 1 <= s <= stages:
                    finish(c, s - 1)
                if 0 <= s < stages:
                    start(c, s)
        if t == 0:
            for copy in smalls:
                copy.wait()
            total = small_ref[pl.ds(pl.multiple_of(me_t * piece_rows, 8), piece_rows), :]
            for k in range(cores - 1):
                total = total + small_r[k]
            small_m[...] = total
            small_start(0)
        elif t <= bits:
            small_finish(t - 1)
            if t < bits:
                small_start(t)
            else:
                mine = pl.ds(pl.multiple_of(me_t * piece_rows, 8), piece_rows)
                small_out[mine, :] = small_m[...]
                lasts = [
                    remote(
                        small_m, small_out.at[mine, :], sg_send.at[k - 1], sg_recv.at[k - 1], core(k)
                    )
                    for k in range(1, cores)
                ]
                for copy in lasts:
                    copy.start()
    for copy in lasts + tokens:
        copy.wait()


def finish_kernel(
    seq, low_ref, small_ref, gbin_own, gbin_rest, gbout_ref, out_own, out_rest, gin_own, gin_rest,
    out_hbm, gin_hbm, gl1, bl1, gq, gk, gv, gbq, gbv, gwp, gbp, gl2, bl2, grout, gbin, gbout, rms,
    out_s, gin_s, in_sem, to_sem
):
    cores, own, seq_pad, width = (out_rest.shape[0] + 1,) + out_rest.shape[1:]
    me_t = lax.axis_index("tensor")
    images = cores * own
    share = gbq.shape[0]
    experts = grout.shape[1]
    jobs = []
    for n, (mine, rest, full, hbm) in enumerate(
        ((out_own, out_rest, out_s, out_hbm), (gin_own, gin_rest, gin_s, gin_hbm))
    ):
        jobs.append((n, mine, rest, full, hbm))
    rows_all = images * seq

    def place(c):
        for n, mine, rest, full, hbm in jobs:
            done = 0
            for im in range(images):
                p = (im // own - c) % cores
                src = mine.at[im % own] if p == 0 else rest.at[p - 1, im % own]
                full[seq * im : seq * (im + 1), :] = src[0:seq, :]
                upto = rows_all if im == images - 1 else seq * (im + 1) // 8 * 8
                pltpu.make_async_copy(
                    full.at[done:upto, :], hbm.at[done:upto, :], to_sem.at[n, im]
                ).start()
                done = upto

    for c in range(cores):

        @pl.when(me_t == c)
        def _(c=c):
            place(c)

    for n, grad in enumerate((gq, gk, gv)):
        grad[...] = low_ref[width * n : width * (n + 1), :].astype(f32)
    gwp[...] = jnp.transpose(low_ref[3 * width : 4 * width, :].astype(f32), (1, 0))
    base = small_base(cores)
    for dst, row in ((gl1, 5), (bl1, 6), (gbp, 4), (gl2, 2), (bl2, 3)):
        dst[...] = small_ref[row]
    which = lax.broadcasted_iota(i32, (base, share), 0)
    for dst, row in ((gbq, 8), (gbv, 8 + cores)):
        dst[...] = jnp.sum(jnp.where(which == row + me_t, small_ref[0:base, 0:share], 0.0), 0)
    grout[...] = jnp.transpose(small_ref[base + 8 : base + 8 + up(experts, 8), :], (1, 0))[:, :experts]
    value = gbin_own[...]
    for k in range(cores - 1):
        value = value + gbin_rest[k]
    gbin[...] = value
    value = gbout_ref[0, 0:1, :]
    for k in range(1, cores):
        value = value + gbout_ref[k, 0:1, :]
    gbout[...] = value
    count = small_ref[7:8, :] * width
    for n, row in enumerate((base, base + 1, 0, base + 2, 1)):
        square = jnp.sum(small_ref[row : row + 1, :], 1, keepdims=True)
        rms[n : n + 1, :] = jnp.sqrt(square / count[:, 0:LANES])
    done = [0] * 2
    for im in range(images):
        upto = rows_all if im == images - 1 else seq * (im + 1) // 8 * 8
        for n, mine, rest, full, hbm in jobs:
            pltpu.make_async_copy(
                full.at[done[n] : upto, :], hbm.at[done[n] : upto, :], to_sem.at[n, im]
            ).wait()
            done[n] = upto


def on_device(
    tokens_in, valid, routes, ln1_gain, ln1_bias, w_query, w_key, w_value, b_query, b_value,
    w_proj, b_proj, ln2_gain, ln2_bias, w_router, w_in, b_in, w_out, b_out, cotangent,
):
    tok_rows, width = tokens_in.shape
    images, seq = valid.shape
    experts = lax.axis_size("expert")
    cores = lax.axis_size("tensor")
    core = lax.axis_index("tensor")
    capacity = (10 * tok_rows // (4 * experts) // 8 + 1) * 8
    cap_dev = up(up(capacity, cores) // cores, 16)
    rows_all = experts * cap_dev
    seq_pad = up(seq, 16)
    key_pad = up(seq_pad, LANES)
    own = images // cores
    tok_own = own * seq
    tok_pad = images * seq_pad
    pad_own = own * seq_pad
    share = w_in.shape[2]
    hidden = share * cores
    wide = width + LANES
    pairs = width // LANES
    S = jax.ShapeDtypeStruct

    def row(v):
        return v.reshape(1, -1)

    def a2a(rows):
        return lax.all_to_all(rows, "expert", split_axis=0, concat_axis=0, tiled=True)

    routes_p = jnp.pad(
        routes.reshape(images, seq, 2), ((0, 0), (0, seq_pad - seq), (0, 0)), constant_values=-1
    ).reshape(tok_pad, 2)
    send_g, post, fidx = pl.pallas_call(
        functools.partial(prep_kernel, (images, seq, seq_pad, experts, cap_dev)),
        out_shape=[
            S((experts, cap_dev, width), bf16),
            S((cores, experts, 1, pad_own), f32),
            S((tok_pad, 2), i32),
        ],
        scratch_shapes=[pltpu.VMEM((tok_pad, width), bf16)],
        compiler_params=params(),
        name="prep",
    )(routes_p, cotangent)
    def turn(x):
        return lax.rem(jnp.arange(experts), experts)

    me_e = lax.axis_index("expert")
    turned = (jnp.arange(experts) + experts - me_e) % experts
    grow = a2a(send_g[turned])
    grow = grow[(me_e + experts - jnp.arange(experts)) % experts]

    own_w = (w_query, w_key, w_value, w_proj)
    *rest_w, bqs, bvs = swap(1, True, *own_w, row(b_query), row(b_value))
    attn_w = [w for pair in zip(own_w, rest_w) for w in pair]
    bq = jnp.concatenate([row(b_query)] + [bqs[j] for j in range(cores - 1)], 1)
    bv = jnp.concatenate([row(b_value)] + [bvs[j] for j in range(cores - 1)], 1)
    w_ins, w_outs, b_ins = swap(7, True, w_in[0], w_out[0], b_in)
    wr = jnp.pad(w_router, ((0, 0), (0, LANES - experts)))
    valid_own = lax.dynamic_slice_in_dim(valid, core * own, own, 0)
    valid_col = jnp.pad(valid_own.astype(f32), ((0, 0), (0, seq_pad - seq)))[:, :, None]
    mask_row = jnp.where(
        jnp.pad(valid_own, ((0, 0), (0, key_pad - seq))) > 0, 0.0, MASKED
    ).astype(f32)[:, None, :]

    dims = (seq, seq_pad, key_pad, own, experts)

    def per_image(*shape):
        return pl.BlockSpec((1,) + shape, lambda i: (i,) + (0,) * len(shape))

    h1, q, k, v, probs, heads, middle, h2x, acc_f = pl.pallas_call(
        functools.partial(attn_fwd_kernel, dims),
        grid=(own,),
        in_specs=[
            whole(tokens_in.shape),
            per_image(seq_pad, 1),
            per_image(1, key_pad),
            whole((1, width)),
            whole((1, width)),
            *[whole(w.shape) for w in attn_w],
            whole((1, width)),
            whole((1, width)),
            whole((1, width)),
            whole((1, width)),
            whole((1, width)),
            whole((width, LANES)),
        ],
        out_specs=[
            per_image(seq_pad, width),
            per_image(seq_pad, width),
            per_image(key_pad, width),
            per_image(key_pad, width),
            per_image(pairs, 2 * seq_pad, key_pad),
            per_image(seq_pad, width),
            per_image(seq_pad, width),
            per_image(seq_pad, wide),
            whole((8, width)),
        ],
        out_shape=[
            S((own, seq_pad, width), bf16),
            S((own, seq_pad, width), bf16),
            S((own, key_pad, width), bf16),
            S((own, key_pad, width), bf16),
            S((own, pairs, 2 * seq_pad, key_pad), bf16),
            S((own, seq_pad, width), bf16),
            S((own, seq_pad, width), f32),
            S((own, seq_pad, wide), bf16),
            S((8, width), f32),
        ],
        scratch_shapes=[pltpu.VMEM((seq_pad, width), f32)],
        compiler_params=params(),
        cost_estimate=pl.CostEstimate(
            flops=2 * pad_own * width * (4 * width + 2 * key_pad),
            bytes_accessed=24 << 20,
            transcendentals=0,
        ),
        name="attn_fwd",
    )(
        tokens_in, valid_col, mask_row, row(ln1_gain), row(ln1_bias), *attn_w, bq, bv,
        row(b_proj), row(ln2_gain), row(ln2_bias), wr,
    )

    size = chunk_of(share)
    per = share // size
    anywhere = pl.BlockSpec(memory_space=pl.ANY)
    inside = pl.BlockSpec(memory_space=pltpu.VMEM)
    block = (experts, cap_dev, width)
    DMA = pltpu.SemaphoreType.DMA
    (
        _, _, gin_w, gout_w, gin_rest, gout_rest, gbin_own, gbin_rest, gb_out,
        moe_own, moe_rest, gmoe_own, gmoe_rest,
    ) = pl.pallas_call(
        moe_kernel,
        in_specs=[anywhere, inside, anywhere, anywhere] + [inside] * 8,
        out_specs=[anywhere] * 6 + [inside] * 3 + [anywhere] * 4,
        out_shape=[
            S(block, bf16),
            S(block, bf16),
            S((width, share), bf16),
            S((share, width), bf16),
            S((cores - 1, width, share), bf16),
            S((cores - 1, share, width), bf16),
            S((1, share), f32),
            S((cores - 1, 1, share), f32),
            S((cores, 8, width), f32),
            S((pad_own, wide), bf16),
            S((cores - 1, pad_own, wide), bf16),
            S((pad_own, width), bf16),
            S((cores - 1, pad_own, width), bf16),
        ],
        scratch_shapes=[
            pltpu.VMEM((cores, pad_own, wide), bf16),
            pltpu.VMEM(block, bf16),
            pltpu.VMEM(block, bf16),
            pltpu.VMEM(block, bf16),
            pltpu.VMEM(block, bf16),
            pltpu.VMEM((experts, 8, cap_dev), f32),
            pltpu.VMEM((experts, 8, cap_dev), f32),
            pltpu.VMEM((rows_all, 1), f32),
            pltpu.VMEM((cores - 1, 1, share), f32),
            pltpu.VMEM((8, width), f32),
            DMA((2, cores - 1)),
            DMA((2, cores - 1)),
            DMA((2,)),
            DMA((2,)),
            DMA((cores,)),
            DMA((cores,)),
            *[DMA((experts,))] * 8,
            DMA((4, (cores - 1) * per)),
            DMA((4, (cores - 1) * per)),
            DMA((6,)),
        ],
        compiler_params=params(collective_id=2, has_side_effects=True),
        name="moe",
    )(
        h2x.reshape(pad_own, wide), post, grow, send_g, fidx, w_in[0], w_ins, b_in, b_ins, w_out[0], w_outs, b_out
    )
    def pieces(n):
        return pl.BlockSpec((cores - 1, 1, seq_pad, n), lambda i: (0, i, 0, 0))

    def by_image(x):
        return x.reshape(x.shape[:-2] + (own, seq_pad, x.shape[-1]))

    head_share = w_query.shape[1]
    buffers = {"pipeline_mode": pl.Buffered(1)} if cores > 2 else {}
    small_b = small_base(cores)
    small_rows = up(small_b + 8 + experts, 8 * cores)
    out_own, gin_own, grad_own, grad_rest, small, grad_w_in, grad_w_out = pl.pallas_call(
        functools.partial(attn_bwd_kernel, dims),
        grid=(own,),
        in_specs=[
            whole(tokens_in.shape),
            whole(cotangent.shape),
            per_image(seq_pad, 1),
            whole((8, width)),
            per_image(seq_pad, width),
            per_image(seq_pad, wide),
            per_image(seq_pad, width),
            per_image(seq_pad, width),
            per_image(key_pad, width),
            per_image(key_pad, width),
            per_image(pairs, 2 * seq_pad, key_pad),
            per_image(seq_pad, width),
            per_image(seq_pad, wide),
            pieces(wide),
            per_image(seq_pad, width),
            pieces(width),
            pl.BlockSpec((width // own, share), lambda i: (i, 0)),
            pl.BlockSpec((cores - 1, width // own, share), lambda i: (0, i, 0), **buffers),
            pl.BlockSpec((share // own, width), lambda i: (i, 0)),
            pl.BlockSpec((cores - 1, share // own, width), lambda i: (0, i, 0), **buffers),
            whole((1, width)),
            whole((1, width)),
            *[whole(w.shape) for w in attn_w],
            whole((width, LANES)),
        ],
        out_specs=[
            per_image(seq_pad, width),
            per_image(seq_pad, width),
            whole((4 * width, head_share)),
            whole((cores - 1, 4 * width, head_share)),
            whole((small_rows, width)),
            pl.BlockSpec((1, width // own, share), lambda i: (0, i, 0)),
            pl.BlockSpec((1, share // own, width), lambda i: (0, i, 0)),
        ],
        out_shape=[
            S((own, seq_pad, width), f32),
            S((own, seq_pad, width), f32),
            S((4 * width, head_share), f32),
            S((cores - 1, 4 * width, head_share), bf16),
            S((small_rows, width), f32),
            S((1, width, share), f32),
            S((1, share, width), f32),
        ],
        scratch_shapes=[pltpu.VMEM((seq_pad, width), f32)] * 2
        + [pltpu.VMEM((seq_pad, width), bf16)]
        + [pltpu.VMEM((pad_own, width), bf16)] * 6,
        compiler_params=params(),
        name="attn_bwd",
    )(
        tokens_in, cotangent, valid_col, acc_f, middle, h2x, h1, q, k, v, probs, heads,
        by_image(moe_own), by_image(moe_rest), by_image(gmoe_own), by_image(gmoe_rest),
        gin_w, gin_rest, gout_w, gout_rest, row(ln1_gain), row(ln2_gain), *attn_w, wr,
    )
    chunks = next(c for c in (4, 2, 1) if (4 * width // c // experts) % 16 == 0)
    bits = experts.bit_length() - 1
    piece_rows = small_rows // cores
    chunk_rows = 4 * width // chunks
    low, small, out_rest, gin_tok = pl.pallas_call(
        functools.partial(reduce_kernel, chunks),
        in_specs=[inside, anywhere, inside, anywhere, anywhere],
        out_specs=[inside, inside, anywhere, anywhere],
        out_shape=[
            S((4 * width, head_share), bf16),
            S((small_rows, width), f32),
            S((cores - 1, own, seq_pad, width), f32),
            S((cores - 1, own, seq_pad, width), f32),
        ],
        scratch_shapes=[
            pltpu.VMEM((cores - 1, 4 * width, head_share), bf16),
            pltpu.VMEM((4 * width, head_share), f32),
            pltpu.VMEM((chunks, chunk_rows, head_share), bf16),
            pltpu.VMEM((chunks, chunk_rows, head_share), bf16),
            pltpu.VMEM((cores - 1, piece_rows, width), f32),
            pltpu.VMEM((piece_rows, width), f32),
            pltpu.VMEM((bits, piece_rows, width), f32),
            pltpu.VMEM((bits, piece_rows, width), f32),
            DMA((cores - 1, chunks)),
            DMA((cores - 1, chunks)),
            DMA((chunks, 2 * bits)),
            DMA((chunks, 2 * bits)),
            DMA((cores - 1,)),
            DMA((cores - 1,)),
            DMA((bits,)),
            DMA((bits,)),
            DMA((cores - 1,)),
            DMA((cores - 1,)),
            DMA((2, cores - 1)),
            DMA((2, cores - 1)),
        ],
        compiler_params=params(collective_id=6, has_side_effects=True),
        name="reduce",
    )(grad_own, grad_rest, small, out_own, gin_own)
    vector = S((width,), f32)
    part = S((head_share,), f32)
    square = S((width, head_share), f32)
    (
        output, grad_input, gl1, bl1, gq, gk, gv, gbq, gbv, gwp, gbp, gl2, bl2, grout,
        grad_b_in, grad_b_out, rms,
    ) = pl.pallas_call(
        functools.partial(finish_kernel, seq),
        in_specs=[inside] * 9,
        out_specs=[anywhere] * 2 + [inside] * 15,
        out_shape=[
            S(tokens_in.shape, f32), S(tokens_in.shape, f32), vector, vector, square, square, square,
            part, part, S((head_share, width), f32), vector, vector, vector,
            S((width, experts), f32), S((1, share), f32), S((1, width), f32), S((8, LANES), f32),
        ],
        scratch_shapes=[
            pltpu.VMEM(tokens_in.shape, f32),
            pltpu.VMEM(tokens_in.shape, f32),
            DMA((2, images)),
            DMA((2, images)),
        ],
        compiler_params=params(),
        name="finish",
    )(low, small, gbin_own, gbin_rest, gb_out, out_own, out_rest, gin_own, gin_tok)
    return (
        output, grad_input, gl1, bl1, gq, gk, gv, gbq, gbv, gwp, gbp, gl2, bl2, grout,
        grad_w_in, grad_b_in, grad_w_out, grad_b_out, rms[:5, 0],
    )


def solution(mesh):
    in_specs = (
        P("expert", None), P("expert", None), P("expert", None), P(), P(),
        P(None, "tensor"), P(None, "tensor"), P(None, "tensor"), P("tensor"), P("tensor"),
        P("tensor", None), P(), P(), P(), P(),
        P("expert", None, "tensor"), P("expert", "tensor"), P("expert", "tensor", None),
        P("expert", None), P("expert", None),
    )
    out_specs = (
        P("expert", None), P("expert", None), P(), P(),
        P(None, "tensor"), P(None, "tensor"), P(None, "tensor"), P("tensor"), P("tensor"),
        P("tensor", None), P(), P(), P(), P(),
        P("expert", None, "tensor"), P("expert", "tensor"), P("expert", "tensor", None),
        P("expert", None), P(),
    )
    return jax.shard_map(
        on_device, mesh=mesh, in_specs=in_specs, out_specs=out_specs, check_vma=False
    )
```

```python
import functools

import jax
import jax.numpy as jnp
from jax import lax
from jax.experimental import pallas as pl
from jax.experimental.pallas import tpu as pltpu
from jax.sharding import PartitionSpec as P

HEAD_DIM = 64
LANES = 128
LOG2E = 1.4426950408889634
MASKED = -1e30
MESH = pl.DeviceIdType.MESH
VMEM_LIMIT = 60 << 20
f32 = jnp.float32
bf16 = jnp.bfloat16
i32 = jnp.int32


def up(value, step):
    return -(-value // step) * step


def params(**more):
    return pltpu.CompilerParams(vmem_limit_bytes=VMEM_LIMIT, **more)


def whole(shape):
    return pl.BlockSpec(shape, lambda *_: (0,) * len(shape), pipeline_mode=pl.Buffered(1))


def dot(a, b):
    return lax.dot_general(a, b, (((1,), (0,)), ((), ())), preferred_element_type=f32)


def dot_nt(a, b):
    return lax.dot_general(a, b, (((1,), (1,)), ((), ())), preferred_element_type=f32)


def dot_tn(a, b):
    return lax.dot_general(a, b, (((0,), (0,)), ((), ())), preferred_element_type=f32)


def lane_iota(shape):
    return lax.broadcasted_iota(i32, shape, len(shape) - 1)


def norm_parts(values):
    center = values - jnp.mean(values, -1, keepdims=True)
    inv_std = lax.rsqrt(jnp.mean(center * center, -1, keepdims=True) + 1e-06)
    return center * inv_std, inv_std


def norm_back(grad_out, normed, inv_std, gain):
    scaled = grad_out * gain
    return inv_std * (
        scaled
        - jnp.mean(scaled, -1, keepdims=True)
        - normed * jnp.mean(scaled * normed, -1, keepdims=True)
    )


def gelu_parts(x):
    z = jnp.abs(x) * 0.7071067811865476
    t = 1.0 / (1.0 + 0.3275911 * z)
    poly = t * (
        0.254829592 * 0.5
        + t
        * (
            -0.284496736 * 0.5
            + t * (1.421413741 * 0.5 + t * (-1.453152027 * 0.5 + t * (1.061405429 * 0.5)))
        )
    )
    e = jnp.exp2(x * x * (-0.5 * LOG2E))
    half = poly * e
    cdf = jnp.where(x >= 0, 1.0 - half, half)
    return x * cdf, cdf + x * e * 0.3989422804014327


def piece(own_ref, rest_ref, j):
    return own_ref[...] if j == 0 else rest_ref[j - 1]


def read_image(dst, src, image, seq):
    for n in range(src.shape[0] // seq):

        @pl.when(image == n)
        def _(n=n):
            dst[0:seq, :] = src[seq * n : seq * (n + 1), :]


def route_rows(dims, expert, core, routes_ref, cot_ref, routes_s, post_ref, fidx_ref, g16):
    images, seq, seq_pad, experts, cap_dev = dims
    tok_pad = images * seq_pad
    wide_s, routes_s = routes_s
    routes_s[...] = jnp.full(routes_s.shape, -1.0, f32)
    wide_s[...] = jnp.zeros_like(wide_s)
    wide_s[0:2, 0 : images * seq] = routes_ref[...].astype(f32)
    turned = jnp.transpose(wide_s[...], (1, 0))
    for i in range(images):
        rows = slice(seq_pad * i, seq_pad * i + seq)
        routes_s[rows, :] = turned[seq * i : seq * (i + 1), :]
        g16[seq_pad * i : seq_pad * (i + 1), :] = jnp.zeros((seq_pad, g16.shape[1]), bf16)
        g16[rows, :] = cot_ref[seq * i : seq * (i + 1), :].astype(bf16)
    r0 = routes_s[:, 0:1].astype(i32)
    r1 = routes_s[:, 1:2].astype(i32)
    lanes = lane_iota((tok_pad, LANES))
    named0 = r0 == lanes
    named1 = r1 == lanes
    named = jnp.where(named0 | named1, 1.0, 0.0)
    named_low = named.astype(bf16)
    lower = (
        lax.broadcasted_iota(i32, (seq_pad, seq_pad), 1)
        < lax.broadcasted_iota(i32, (seq_pad, seq_pad), 0)
    ).astype(f32).astype(bf16)
    run = jnp.zeros((1, LANES), f32)
    parts = []
    for i in range(images):
        rows = slice(seq_pad * i, seq_pad * (i + 1))
        parts.append(dot(lower, named_low[rows]) + run)
        run = run + jnp.sum(named[rows], 0, keepdims=True)
    before = jnp.concatenate(parts, 0) - (core * cap_dev).astype(f32)
    pos = jnp.where(named > 0, before, -1.0)
    groups, _, _, group = post_ref.shape
    for j in range(groups):
        turned = jnp.transpose(pos[group * j : group * (j + 1)], (1, 0))
        for e in range(experts):
            post_ref[j, e] = turned[e : e + 1]
    for k, named_k, r_k in ((0, named0, r0), (1, named1, r1)):
        slot = jnp.sum(jnp.where(named_k, before, 0.0), 1, keepdims=True)
        fits = (slot >= 0) & (slot < cap_dev) & (r_k >= 0)
        turn = lax.rem(r_k - expert + experts, experts)
        half = experts // 2
        far = jnp.where(turn >= half, 1, 0)
        flat = ((turn - far * half) * 2 + far).astype(f32) * cap_dev + slot
        fidx_ref[:, k : k + 1] = jnp.where(fits, flat, -1.0).astype(i32)


def vec(ref):
    return ref[...].reshape(1, -1)


def attn_fwd_kernel(
    dims, tok_ref, cot_ref, valid_ref, routes_ref, g1_ref, b1_ref, wq, wk, wv, wp, bq, bv,
    bp_ref, g2_ref, b2_ref, wr_ref, w_in_hbm, w_out_hbm, b_in_hbm,
    h1_ref, q_ref, k_ref, v_ref, probs_ref, heads_ref, mid_ref, ok_ref, x_ref,
    h2x_ref, acc_ref, sent_ref, post_ref, fidx_ref, wr_pad,
    wqs_hbm, wks_hbm, wvs_hbm, wps_hbm, grow_ref, h2x_rest, w_ins, w_outs, b_ins,
    wqs, wks, wvs, wps, g16, wide_s, routes_s, valid_s, bias_s, bias_in,
    w_send, w_recv, b_send, b_recv, h_send, h_recv, g_send, g_recv, own_sem, keep_sem
):
    images, seq, seq_pad, key_pad, own, cap_dev = dims
    width = tok_ref.shape[1]
    step = pl.program_id(0)
    experts, chip = around("expert")
    cores, core = around("tensor")
    me_e = lax.axis_index("expert")
    me_t = lax.axis_index("tensor")
    image = me_t * own + step
    group = own * seq_pad
    shares = shares_of(wq, wqs)
    share = wq.shape[1]

    def remote(src, dst, send, recv, there):
        return pltpu.make_async_remote_copy(
            src_ref=src, dst_ref=dst, send_sem=send, recv_sem=recv,
            device_id=there, device_id_type=MESH,
        )

    def weight_copy(n, k):
        src, dst = (
            (wq, wqs), (wk, wks), (wv, wvs), (wp, wps),
            (w_in_hbm, w_ins), (w_out_hbm, w_outs), (b_in_hbm, b_ins),
        )[n]
        return remote(src, dst.at[k - 1], w_send.at[n, k - 1], w_recv.at[n, k - 1], core(-k))

    def bias_copy(k):
        return remote(
            bias_s, bias_in.at[k - 1], b_send.at[k - 1], b_recv.at[k - 1], core(-k)
        )

    def h_copy(i, k):
        return remote(
            h2x_ref.at[i], h2x_rest.at[k - 1, i], h_send.at[i, k - 1], h_recv.at[i, k - 1], core(-k)
        )

    def g_copy(k):
        there = chip(offset_at(k, experts))
        return remote(sent_ref.at[k], grow_ref.at[k], g_send.at[k], g_recv.at[k], there)

    own_rows = pltpu.make_async_copy(sent_ref.at[0], grow_ref.at[0], own_sem)
    keeps = [
        pltpu.make_async_copy(src, dst, keep_sem.at[n])
        for n, (src, dst) in enumerate(
            ((wqs, wqs_hbm), (wks, wks_hbm), (wvs, wvs_hbm), (wps, wps_hbm))
        )
    ]

    @pl.when(step == 0)
    def _():
        peers = [core(k) for k in range(1, cores)] + [chip(k) for k in range(1, experts)]
        greet_start(peers)
        route_rows(
            (images, seq, seq_pad, experts, cap_dev), me_e, me_t,
            routes_ref, cot_ref, (wide_s, routes_s), post_ref, fidx_ref, g16,
        )
        greet_end(peers)
        bias_s[0:1, :] = vec(bq)
        bias_s[1:2, :] = vec(bv)
        for k in range(1, cores):
            bias_copy(k).start()
            for n in range(4):
                weight_copy(n, k).start()
        slots = lax.broadcasted_iota(i32, (cap_dev, group), 0).astype(f32)

        def send_rows(n, _):
            k = lax.rem(n + 1, experts)
            total = None
            for j in range(cores):
                named_e = post_ref[j, lax.rem(me_e + offset_at(k, experts), experts)]
                pick = jnp.where(named_e == slots, 1.0, 0.0).astype(bf16)
                term = dot(pick, g16[group * j : group * (j + 1), :])
                total = term if total is None else total + term
            sent_ref[k] = total.astype(bf16)

            @pl.when(k > 0)
            def _():
                g_copy(k).start()

            return 0

        lax.fori_loop(0, experts, send_rows, 0)
        own_rows.start()
        valid_s[...] = jnp.zeros_like(valid_s)
        valid_s[:, 0:seq] = valid_ref[...].astype(f32)
        wr_pad[...] = jnp.zeros_like(wr_pad)
        wr_pad[0:experts, :] = wr_ref[...]
        acc_ref[...] = jnp.zeros_like(acc_ref)
        for k in range(1, cores):
            bias_copy(k).wait()
            for n in range(4):
                weight_copy(n, k).wait()
            for n in range(4, 7):
                weight_copy(n, k).start()
        for copy in keeps:
            copy.start()

    x_ref[...] = jnp.zeros_like(x_ref)
    read_image(x_ref.at[0], tok_ref, image, seq)
    x = x_ref[0]
    normed, _ = norm_parts(x)
    h1 = (normed * vec(g1_ref) + vec(b1_ref)).astype(bf16)
    h1_ref[0] = h1
    k_ref[0, seq_pad:, :] = jnp.zeros((key_pad - seq_pad, width), bf16)
    v_ref[0, seq_pad:, :] = jnp.zeros((key_pad - seq_pad, width), bf16)
    for j, cols in enumerate(shares):
        bias = bias_s if j == 0 else bias_in.at[j - 1]
        q_ref[0, :, cols] = (dot(h1, piece(wq, wqs, j)) + bias[0:1, :]).astype(bf16)
        k_ref[0, 0:seq_pad, cols] = dot(h1, piece(wk, wks, j)).astype(bf16)
        v_ref[0, 0:seq_pad, cols] = (dot(h1, piece(wv, wvs, j)) + bias[1:2, :]).astype(bf16)
    low_half = lane_iota((seq_pad, LANES)) < HEAD_DIM
    which = lax.broadcasted_iota(i32, valid_s.shape, 0)
    ok_row = jnp.sum(jnp.where(which == image, valid_s[...], 0.0), 0, keepdims=True)
    ok_col = jnp.transpose(jnp.broadcast_to(ok_row, (LANES, key_pad)), (1, 0))[:seq_pad, 0:1]
    ok_ref[0] = ok_col
    mask = jnp.where(ok_row > 0, 0.0, MASKED)
    for p in range(width // LANES):
        cols = slice(LANES * p, LANES * (p + 1))
        qs = split_heads(q_ref[0, :, cols])
        s = dot_nt(qs, k_ref[0, :, cols]) * (HEAD_DIM**-0.5 * LOG2E) + mask
        e = jnp.exp2(s - jnp.max(s, -1, keepdims=True))
        prob = (e * (1.0 / jnp.sum(e, -1, keepdims=True))).astype(bf16)
        probs_ref[0, p] = prob
        o = dot(prob, v_ref[0, :, cols])
        heads_ref[0, :, cols] = jnp.where(low_half, o[:seq_pad], o[seq_pad:]).astype(bf16)
    attn = vec(bp_ref)
    for j, cols in enumerate(shares):
        attn = attn + dot(heads_ref[0, :, cols], piece(wp, wps, j))
    middle = x + attn
    mid_ref[0] = middle
    for row, field in enumerate((x, middle, attn)):
        acc_ref[row : row + 1, :] += jnp.sum(ok_col * field * field, 0, keepdims=True)
    normed2, _ = norm_parts(middle)
    h2 = (normed2 * vec(g2_ref) + vec(b2_ref)).astype(bf16)
    h2x_ref[step, :, 0:width] = h2
    logits = dot_nt(h2, wr_pad[...])
    logits = jnp.where(lane_iota(logits.shape) < experts, logits, MASKED)
    e = jnp.exp(logits - jnp.max(logits, -1, keepdims=True))
    prob = e / jnp.sum(e, -1, keepdims=True)
    high = prob.astype(bf16).astype(f32)
    h2x_ref[step, :, width:] = (high + pltpu.roll(prob - high, experts, 1)).astype(bf16)
    for k in range(1, cores):
        h_copy(step, k).start()

    @pl.when(step == own - 1)
    def _():
        for k in range(1, cores):
            for n in range(4, 7):
                weight_copy(n, k).wait()
            for i in range(own):
                h_copy(i, k).wait()

        def arrived(k, _):
            g_copy(k).wait()
            return 0

        lax.fori_loop(1, experts, arrived, 0)
        own_rows.wait()
        for copy in keeps:
            copy.wait()


def split_heads(value):
    low_half = lane_iota(value.shape) < HEAD_DIM
    zero = jnp.zeros_like(value)
    return jnp.concatenate([jnp.where(low_half, value, zero), jnp.where(low_half, zero, value)], 0)


def shares_of(own_ref, rest_ref):
    share = own_ref.shape[1]
    return [slice(share * j, share * (j + 1)) for j in range(rest_ref.shape[0] + 1)]


def add_parts(acc_ref, base, shares, value):
    rows = small_base(len(shares))
    which = lax.broadcasted_iota(i32, (rows, shares[0].stop), 0)
    for j, cols in enumerate(shares):
        owner = lax.rem(lax.axis_index("tensor") + j, len(shares))
        total = jnp.sum(value[:, cols].astype(f32), 0, keepdims=True)
        acc_ref[0:rows, shares[0]] += jnp.where(which == base + owner, total, 0.0)


def attn_bwd_a_kernel(
    dims, cot_ref, valid_ref, accf_ref, mid_ref, h2x_ref, h1_ref, probs_ref, heads_ref,
    moe_own, moe_ref, gmoe_own, gmoe_ref, gin_w, gin_ws, gout_w, gout_ws, g2_ref, wq, wp, wps, wr_ref,
    out_ref, gm_ref, gh_ref, dv_ref, grad_own, grad_rest, acc_ref, gw_in_ref, gw_out_ref,
    c_s, h1_s, heads_s, ga_s, dv_s
):
    seq, seq_pad, key_pad, own, experts = dims
    width = cot_ref.shape[1]
    step = pl.program_id(0)
    shares = shares_of(wq, wps)
    small_b = small_base(len(shares))
    image = lax.axis_index("tensor") * own + step
    at = pl.multiple_of(step * seq_pad, 16)
    c_s[seq // 8 * 8 :, :] = jnp.zeros((seq_pad - seq // 8 * 8, width), f32)
    read_image(c_s, cot_ref, image, seq)
    ok = valid_ref[0]

    @pl.when(step == 0)
    def _():
        acc_ref[...] = jnp.zeros_like(acc_ref)
        acc_ref[small_b : small_b + 8, :] = accf_ref[...]

    def add(row, value):
        acc_ref[row : row + 1, :] += jnp.sum(value, 0, keepdims=True)

    def total(own_ref, rest_ref, cols):
        value = own_ref[0, :, cols].astype(f32)
        for j in range(rest_ref.shape[0]):
            value = value + rest_ref[j, 0, :, cols].astype(f32)
        return value

    for sum_ref, own_ref, rest_ref in (
        (gw_in_ref, gin_w, gin_ws), (gw_out_ref, gout_w, gout_ws)
    ):
        value = own_ref[...].astype(f32)
        for j in range(rest_ref.shape[0]):
            value = value + rest_ref[j].astype(f32)
        sum_ref[0] = value
    middle = mid_ref[0]
    moe = total(moe_own, moe_ref, slice(0, width))
    output = middle + moe
    out_ref[0] = output
    add(0, ok * output * output)
    add(1, ok * moe * moe)
    h2 = h2x_ref[0, :, 0:width]
    pair = h2x_ref[0, :, width:].astype(f32)
    prob = jnp.where(
        lane_iota(pair.shape) < experts, pair + pltpu.roll(pair, LANES - experts, 1), 0.0
    )
    grad_probs = total(moe_own, moe_ref, slice(width, width + LANES))
    grad_logits = (
        prob * (grad_probs - jnp.sum(grad_probs * prob, -1, keepdims=True))
    ).astype(bf16)
    acc_ref[small_b + 8 : small_b + 8 + experts, :] += dot_tn(grad_logits, h2)[:experts]
    grad_h2 = dot(grad_logits, wr_ref[...]) + total(gmoe_own, gmoe_ref, slice(0, width))
    normed2, inv2 = norm_parts(middle)
    add(2, grad_h2 * normed2)
    add(3, grad_h2)
    add(7, jnp.broadcast_to(ok, grad_h2.shape))
    grad_middle = c_s[...] + norm_back(grad_h2, normed2, inv2, vec(g2_ref))
    gm_ref[0] = grad_middle
    grad_attn = grad_middle.astype(bf16)
    add(4, grad_attn.astype(f32))
    here = pl.ds(at, seq_pad)
    ga_s[here, :] = grad_attn
    heads_s[here, :] = heads_ref[0]
    h1_s[here, :] = h1_ref[0]
    for j, cols in enumerate(shares):
        gh_ref[0, :, cols] = dot_nt(grad_attn, piece(wp, wps, j)).astype(bf16)
    for p in range(width // LANES):
        cols = slice(LANES * p, LANES * (p + 1))
        gs = split_heads(gh_ref[0, :, cols])
        dv_s[here, cols] = dot_tn(probs_ref[0, p], gs)[:seq_pad].astype(bf16)
    dv = dv_s[here, :]
    dv_ref[0] = dv
    add_parts(acc_ref, 8 + len(shares), shares, dv)

    @pl.when(step == own - 1)
    def _():
        for n, (left, right) in enumerate(((ga_s, heads_s), (h1_s, dv_s))):
            rows = slice(width * n, width * (n + 1))
            grad = dot_tn(left[...], right[...])
            put_chunks(grad_own, grad_rest, rows, shares, grad)


def put_chunks(own_ref, rest_ref, rows, shares, grad):
    lanes = own_ref.shape[2]
    for j, cols in enumerate(shares):
        for c in range(own_ref.shape[0]):
            value = grad[:, cols.start + lanes * c : cols.start + lanes * (c + 1)]
            if j == 0:
                own_ref[c, rows, :] = value
            else:
                rest_ref[j - 1, c, rows, :] = value.astype(bf16)


def attn_bwd_b_kernel(
    dims, q_ref, k_ref, v_ref, probs_ref, gh_ref, first_own, first_rest, small_ref, g1_ref,
    wq, wqs, wk, wks, wv, wvs, x_hbm, gm_hbm, dv_hbm, h1_hbm, out_hbm,
    low_hbm, small_hbm, gin_ref, outs_ref, gins_ref,
    low, small_out, dq_s, dk_s, x_s, gm_s, dv_s, h1_s, rest_out, rest_s, acc, send_s, recv_s,
    small_a, small_r, small_m, small_s, small_t,
    load_sem, t_send, t_recv, x_send, x_recv, st_send, st_recv, sx_send, sx_recv, sg_send, sg_recv,
    o_send, o_recv, i_send, i_recv
):
    seq, seq_pad, key_pad, own, _ = dims
    width = q_ref.shape[2]
    step = pl.program_id(0)
    shares = shares_of(wq, wqs)
    at = pl.multiple_of(step * seq_pad, 16)
    here = pl.ds(at, seq_pad)
    experts, _ = around("expert")
    cores, core = around("tensor")
    me_e = lax.axis_index("expert")
    me_t = lax.axis_index("tensor")
    bits = experts.bit_length() - 1
    chunks, rows, _ = acc.shape[1:]
    piece_rows = small_r.shape[1]
    low_half = lane_iota((seq_pad, LANES)) < HEAD_DIM

    def my_bit(b):
        return lax.rem(me_e // (1 << b), 2)

    def partner(b):
        return {"expert": me_e + (1 << b) * (1 - 2 * my_bit(b))}

    def remote(src, dst, send, recv, there):
        return pltpu.make_async_remote_copy(
            src_ref=src, dst_ref=dst, send_sem=send, recv_sem=recv,
            device_id=there, device_id_type=MESH,
        )

    orders = []
    for c in range(chunks):
        order = list(range(bits))
        if c == 1:
            order = [1, 0] + order[2:]
        elif c == 2:
            order = order[2:] + order[:2]
        orders.append(order)

    def base_at(c, s):
        value = 0
        for n in range(s):
            value = value + my_bit(orders[c][n]) * (rows >> (n + 1))
        return value

    def inner(phase, c, k):
        source = first_rest if phase == 0 else rest_out
        return remote(
            source.at[k - 1, c], rest_s.at[phase, k - 1, c],
            t_send.at[phase, k - 1, c], t_recv.at[phase, k - 1, c], core(k),
        )

    def across(phase, c, s):
        sems = (x_send.at[phase, c, s], x_recv.at[phase, c, s])
        if s < bits:
            half = rows >> (s + 1)
            box = slice(rows - 2 * half, rows - half)
            return remote(
                send_s.at[phase, c, box, :], recv_s.at[phase, c, box, :], *sems,
                partner(orders[c][s]),
            )
        size = rows >> (2 * bits - s)
        mine = pl.ds(pl.multiple_of(base_at(c, 2 * bits - s), 16), size)
        return remote(
            low.at[phase, c, mine, :], low.at[phase, c, mine, :], *sems,
            partner(orders[c][2 * bits - 1 - s]),
        )

    def send_stage(phase, c, s):
        if s < bits:
            half = rows >> (s + 1)
            away = pl.ds(
                pl.multiple_of(base_at(c, s) + (1 - my_bit(orders[c][s])) * half, 16), half
            )
            send_s[phase, c, rows - 2 * half : rows - half, :] = acc[phase, c, away, :].astype(bf16)
        elif s == bits:
            mine = pl.ds(pl.multiple_of(base_at(c, bits), 16), rows >> bits)
            low[phase, c, mine, :] = acc[phase, c, mine, :].astype(bf16)
        across(phase, c, s).start()

    def end_stage(phase, c, s):
        across(phase, c, s).wait()
        if s < bits:
            half = rows >> (s + 1)
            keep = pl.ds(pl.multiple_of(base_at(c, s + 1), 16), half)
            acc[phase, c, keep, :] += recv_s[phase, c, rows - 2 * half : rows - half, :].astype(f32)

    def point(phase, s):
        for c in range(chunks):
            if s == 0:
                for k in range(1, cores):
                    inner(phase, c, k).wait()
                value = first_own[c] if phase == 0 else acc[phase, c]
                for k in range(cores - 1):
                    value = value + rest_s[phase, k, c].astype(f32)
                acc[phase, c] = value
            else:
                end_stage(phase, c, s - 1)
            if s < 2 * bits:
                send_stage(phase, c, s)

    def out_copy(k):
        return remote(out_hbm, outs_ref.at[k - 1], o_send.at[k - 1], o_recv.at[k - 1], core(k))

    def gin_copy(i, k):
        return remote(
            gin_ref.at[i], gins_ref.at[k - 1, i], i_send.at[i, k - 1], i_recv.at[i, k - 1], core(k)
        )

    loads = [
        pltpu.make_async_copy(src, dst, load_sem.at[n])
        for n, (src, dst) in enumerate(
            ((x_hbm, x_s), (gm_hbm, gm_s), (dv_hbm, dv_s), (h1_hbm, h1_s))
        )
    ]

    @pl.when(step == 0)
    def _():
        peers = [partner(b) for b in range(bits)] + [core(k) for k in range(1, cores)]
        greet_start(peers)
        for copy in loads:
            copy.start()
        greet_end(peers)
        for c in range(chunks):
            for k in range(1, cores):
                inner(0, c, k).start()

    pairs = width // LANES
    points = {}
    hidden_points = min(7, 2 * bits + 1)
    for n in range(hidden_points):
        turn = 4 + (n * (own * pairs - 5)) // max(hidden_points - 1, 1)
        points.setdefault((turn // pairs, turn % pairs), []).append(n)

    for p in range(pairs):
        cols = slice(LANES * p, LANES * (p + 1))
        gs = split_heads(gh_ref[0, :, cols])
        qs = split_heads(q_ref[0, :, cols])
        weights = probs_ref[0, p].astype(f32)
        mixed = weights * dot_nt(gs, v_ref[0, :, cols])
        ds = (
            (mixed - weights * jnp.sum(mixed, -1, keepdims=True)) * (HEAD_DIM**-0.5)
        ).astype(bf16)
        dq = dot(ds, k_ref[0, :, cols])
        dq_s[here, cols] = jnp.where(low_half, dq[:seq_pad], dq[seq_pad:]).astype(bf16)
        dk_s[here, cols] = dot_tn(ds, qs)[:seq_pad].astype(bf16)
        for i in range(own):
            if (i, p) in points:

                @pl.when(step == i)
                def _(i=i, p=p):
                    for n in points[i, p]:
                        point(0, n)
                        if n == 0:
                            for k in range(1, cores):
                                out_copy(k).start()

    @pl.when(step == own - 1)
    def _():
        for copy in loads:
            copy.wait()
        for n, part in enumerate((dq_s, dk_s)):
            box = slice(width * n, width * (n + 1))
            grad = dot_tn(h1_s[...].reshape(own * seq_pad, width), part[...])
            put_chunks(acc.at[1], rest_out, box, shares, grad)
        for c in range(chunks):
            for k in range(1, cores):
                inner(1, c, k).start()
        small_a[...] = small_ref[...]
        add_parts(small_a, 8, shares, dq_s[...])

        def first_norm(i):
            box = slice(seq_pad * i, seq_pad * (i + 1))
            grad_h1 = None
            for j, cols in enumerate(shares):
                for left, own_ref, rest_ref in (
                    (dq_s[box, cols], wq, wqs), (dk_s[box, cols], wk, wks), (dv_s[i, :, cols], wv, wvs)
                ):
                    term = dot_nt(left, piece(own_ref, rest_ref, j))
                    grad_h1 = term if grad_h1 is None else grad_h1 + term
            normed1, inv1 = norm_parts(x_s[i])
            for row, value in ((5, grad_h1 * normed1), (6, grad_h1)):
                small_a[row : row + 1, :] += jnp.sum(value, 0, keepdims=True)
            gin_ref[i] = gm_s[i] + norm_back(grad_h1, normed1, inv1, vec(g1_ref))
            for k in range(1, cores):
                gin_copy(i, k).start()

        def small_piece(k):
            mine = pl.ds(
                pl.multiple_of(lax.rem(me_t + k, cores) * piece_rows, 8), piece_rows
            )
            return remote(
                small_a.at[mine, :], small_r.at[k - 1], st_send.at[k - 1], st_recv.at[k - 1], core(k)
            )

        def small_across(n):
            return remote(small_s.at[n], small_t.at[n], sx_send.at[n], sx_recv.at[n], partner(n))

        mine = pl.ds(pl.multiple_of(me_t * piece_rows, 8), piece_rows)

        def small_back(k):
            return remote(
                small_m, small_out.at[mine, :], sg_send.at[k - 1], sg_recv.at[k - 1], core(k)
            )

        def small_point(n):
            if n == 0:
                for k in range(1, cores):
                    small_piece(k).wait()
                total = small_a[mine, :]
                for k in range(cores - 1):
                    total = total + small_r[k]
                small_m[...] = total
            else:
                small_across(n - 1).wait()
                small_m[...] += small_t[n - 1]
            if n < bits:
                small_s[n] = small_m[...]
                small_across(n).start()
            else:
                small_out[mine, :] = small_m[...]
                for k in range(1, cores):
                    small_back(k).start()

        older = list(range(hidden_points, 2 * bits + 1))
        newer = list(range(2 * bits + 1))
        norms = list(range(own))
        smalls = []
        while older or newer or norms or smalls:
            if norms:
                first_norm(norms.pop(0))
                if not norms:
                    for k in range(1, cores):
                        small_piece(k).start()
                    smalls = list(range(bits + 1))
            elif smalls:
                small_point(smalls.pop(0))
            if older:
                point(0, older.pop(0))
            if newer:
                point(1, newer.pop(0))
        keeps = [pltpu.make_async_copy(low, low_hbm, load_sem.at[0])]
        keeps[0].start()
        for k in range(1, cores):
            small_back(k).wait()
        keeps.append(pltpu.make_async_copy(small_out, small_hbm, load_sem.at[1]))
        keeps[1].start()
        for k in range(1, cores):
            out_copy(k).wait()
            for i in range(own):
                gin_copy(i, k).wait()
        for copy in keeps:
            copy.wait()


def small_base(cores):
    return up(8 + 2 * cores, 8)


def view(own_ref, rest_ref, j):
    return own_ref if j == 0 else rest_ref.at[j - 1]


def chunk_of(hidden):
    for size in (512, 384, 256, 128):
        if hidden % size == 0:
            return size
    return hidden


def greet_start(peers):
    barrier = pltpu.get_barrier_semaphore()
    for peer in peers:
        pl.semaphore_signal(barrier, inc=1, device_id=peer, device_id_type=MESH)


def greet_end(peers):
    pl.semaphore_wait(pltpu.get_barrier_semaphore(), len(peers))


def offset_at(place, experts):
    return place // 2 + lax.rem(place, 2) * (experts // 2)


def around(axis):
    n = lax.axis_size(axis)
    me = lax.axis_index(axis)
    return n, lambda k: {axis: lax.rem(me + n + k, n)}


def moe_kernel(
    h2x_ref, h2x_rest, post_ref, grow_hbm, sent_hbm, fidx_ref, w_in, w_ins, b_in, b_ins, w_out, w_outs,
    b_out_ref,
    back_ref, gback_ref, gin_own, gout_own, gin_rest, gout_rest,
    gbin_own, gbin_rest, gbout_ref, moe_own, moe_rest, gmoe_own, gmoe_rest,
    table, out_s, rows_s, grow_s, res_s, gate_out, gate_in, gslot_ref,
    gbin_send, gbout_send,
    m_send, m_recv, load_sem, local_sem, h_send, h_recv, c_send, c_recv, r_send, r_recv, g_send, g_recv,
    w_send, w_recv, own_sem
):
    experts, chip = around("expert")
    cores, core = around("tensor")
    me_e = lax.axis_index("expert")
    me_t = lax.axis_index("tensor")
    cap_dev, width = rows_s.shape[1:]
    group = table.shape[1]
    share = w_in.shape[1]
    size = chunk_of(share)
    per = share // size
    peers = [chip(k) for k in range(1, experts)] + [core(k) for k in range(1, cores)]
    greet_start(peers)

    def remote(src, dst, send, recv, there):
        return pltpu.make_async_remote_copy(
            src_ref=src, dst_ref=dst, send_sem=send, recv_sem=recv,
            device_id=there, device_id_type=MESH,
        )

    grow_copy = pltpu.make_async_copy(grow_hbm, grow_s, local_sem.at[0])
    grow_copy.start()
    fills = [
        pltpu.make_async_copy(
            h2x_ref if k == 0 else h2x_rest.at[k - 1],
            table.at[lax.rem(me_t + k, cores)], local_sem.at[1 + k],
        )
        for k in range(cores)
    ]
    for copy in fills:
        copy.start()
    for copy in fills:
        copy.wait()
    greet_end(peers)

    slots = lax.broadcasted_iota(i32, (cap_dev, group), 0).astype(f32)
    lanes = lane_iota((cap_dev, LANES))

    def select(k):
        e = lax.rem(me_e + offset_at(k, experts), experts)
        total = None
        for j in range(cores):
            pick = jnp.where(post_ref[j, e] == slots, 1.0, 0.0).astype(bf16)
            term = dot(pick, table[j])
            total = term if total is None else total + term
        mine = (lanes == e) | (lanes == e + experts)
        gate = jnp.sum(jnp.where(mine, total[:, width:], 0.0), 1, keepdims=True)
        gslot_ref[pl.ds(pl.multiple_of(cap_dev * k, 8), cap_dev), :] = gate
        spread = jnp.transpose(jnp.broadcast_to(gate, (cap_dev, LANES)), (1, 0))
        return total[:, :width].astype(bf16), spread[0:8]

    def h_copy(k):
        there = chip(offset_at(k, experts))
        return remote(out_s.at[k], rows_s.at[k], h_send.at[k], h_recv.at[k], there)

    def c_copy(k):
        there = chip(offset_at(k, experts))
        return remote(gate_out.at[k], gate_in.at[k], c_send.at[k], c_recv.at[k], there)

    def r_copy(k):
        there = chip(-offset_at(k, experts))
        return remote(res_s.at[k], back_ref.at[k], r_send.at[k], r_recv.at[k], there)

    def g_copy(k):
        there = chip(-offset_at(k, experts))
        return remote(out_s.at[k], gback_ref.at[k], g_send.at[k], g_recv.at[k], there)

    def send_rows(j, _):
        k = lax.rem(j + 1, experts)
        rows, gate = select(k)
        out_s[k] = rows
        gate_out[k] = gate

        @pl.when(k > 0)
        def _():
            h_copy(k).start()
            c_copy(k).start()

        return 0

    lax.fori_loop(0, experts, send_rows, 0)
    rows_s[0] = out_s[0]
    gate_in[0] = gate_out[0]
    pl.run_scoped(
        functools.partial(
            expert_phase, locals_of(
                experts=experts, cores=cores, core=core, me_t=me_t, width=width, cap_dev=cap_dev,
                share=share, size=size, per=per, w_in=w_in, w_ins=w_ins, b_in=b_in, b_ins=b_ins,
                w_out=w_out, w_outs=w_outs, b_out_ref=b_out_ref, rows_s=rows_s, res_s=res_s,
                back_ref=back_ref, own_sem=own_sem, h_copy=h_copy, r_copy=r_copy, c_copy=c_copy,
                g_copy=g_copy, grow_copy=grow_copy, grow_s=grow_s, out_s=out_s,
                gback_ref=gback_ref, gate_in=gate_in, gbout_send=gbout_send, gbout_ref=gbout_ref,
                gbin_own=gbin_own, gbin_send=gbin_send, gbin_rest=gbin_rest, gin_own=gin_own,
                gout_own=gout_own, gin_rest=gin_rest, gout_rest=gout_rest, w_send=w_send,
                w_recv=w_recv, remote=remote,
            ),
        ),
        pltpu.VMEM((experts * cap_dev, share * cores), bf16),
        pltpu.VMEM((experts * cap_dev, share * cores), bf16),
        pltpu.VMEM((2, width, size), bf16),
        pltpu.VMEM((2, size, width), bf16),
    )
    rows_all = experts * cap_dev
    wide = width + LANES

    def token_phase(picks, values, total):
        loads = [
            pltpu.make_async_copy(sent_hbm, grow_s, load_sem.at[0]),
            pltpu.make_async_copy(back_ref, rows_s, load_sem.at[1]),
        ]
        loads[0].start()

        def arrived(k, _):
            r_copy(k).wait()
            return 0

        lax.fori_loop(1, experts, arrived, 0)
        loads[1].start()
        step = 208 if group % 208 == 0 else group
        tiles = group // step
        slot_lanes = lane_iota((step, rows_all))

        def make_picks(i, _):
            tok = pl.ds(pl.multiple_of(i * step, 16), step)
            hit = (fidx_ref[tok, 0:1] == slot_lanes) | (fidx_ref[tok, 1:2] == slot_lanes)
            picks[tok, :] = jnp.where(hit, 1.0, 0.0).astype(bf16)
            return 0

        lax.fori_loop(0, cores * tiles, make_picks, 0)
        for copy in loads:
            copy.wait()

        def gated(k):
            return gslot_ref[pl.ds(pl.multiple_of(cap_dev * k, 8), cap_dev), :]

        def weigh(k, _):
            rows = rows_s[k].astype(f32)
            dots = jnp.sum(rows * grow_s[k].astype(f32), 1, keepdims=True)
            here = pl.ds(pl.multiple_of(cap_dev * k, 16), cap_dev)
            values[here, 0:width] = (rows * gated(k)).astype(bf16)
            mine = lanes == lax.rem(me_e + offset_at(k, experts), experts)
            values[here, width:] = jnp.where(mine, dots, 0.0).astype(bf16)
            return 0

        lax.fori_loop(0, experts, weigh, 0)

        def m_copy(kind, k):
            source = table.at[k] if kind == 0 else table.at[k, :, 0:width]
            return remote(
                source, (moe_rest, gmoe_rest)[kind].at[k - 1],
                m_send.at[kind, k - 1], m_recv.at[kind, k - 1], core(k),
            )

        keep_moe = pltpu.make_async_copy(table.at[0], moe_own, load_sem.at[0])
        keep_gmoe = pltpu.make_async_copy(table.at[0, :, 0:width], gmoe_own, load_sem.at[0])

        for k in list(range(1, cores)) + [0]:

            def sums(i, _, k=k):
                tok = pl.ds(
                    pl.multiple_of(lax.rem(me_t + k, cores) * group + i * step, 16), step
                )
                to = pl.ds(pl.multiple_of(i * step, 16), step)
                table[k, to, :] = dot(picks[tok, :], values[...]).astype(bf16)
                return 0

            lax.fori_loop(0, tiles, sums, 0)
            if k > 0:
                m_copy(0, k).start()
        keep_moe.start()
        keep_moe.wait()
        for k in range(1, cores):
            m_copy(0, k).wait()

        batch = 4
        batches = experts // batch
        for b in range(batches):
            first = b * batch
            for k in range(first, first + batch):
                if k > 0:
                    g_copy(k).wait_recv()
                else:
                    own_grad.wait()
            box = pl.ds(first, batch)
            load = pltpu.make_async_copy(gback_ref.at[box], rows_s.at[box], load_sem.at[0])
            load.start()
            load.wait()
            cols = slice(cap_dev * first, cap_dev * (first + batch))
            for k in range(first, first + batch):
                rows_s[k] = (rows_s[k].astype(f32) * gated(k)).astype(bf16)
            for k in list(range(1, cores)) + [0]:

                def gsums(i, _, k=k, b=b, cols=cols, box=box):
                    tok = pl.ds(
                        pl.multiple_of(lax.rem(me_t + k, cores) * group + i * step, 16), step
                    )
                    to = pl.ds(pl.multiple_of(i * step, 16), step)
                    rows = rows_s[box].reshape(batch * cap_dev, width)
                    value = dot(picks[tok, cols], rows)
                    if b > 0:
                        value = value + total[tok, :]
                    if b < batches - 1:
                        total[tok, :] = value
                    else:
                        table[k, to, 0:width] = value.astype(bf16)
                    return 0

                lax.fori_loop(0, tiles, gsums, 0)
                if b == batches - 1 and k > 0:
                    m_copy(1, k).start()
        keep_gmoe.start()
        keep_gmoe.wait()
        for k in range(1, cores):
            m_copy(1, k).wait()

        def finish(k, _):
            g_copy(k).wait_send()
            return 0

        lax.fori_loop(1, experts, finish, 0)

    own_grad = pltpu.make_async_copy(out_s.at[0], gback_ref.at[0], own_sem.at[1])
    pl.run_scoped(
        token_phase,
        pltpu.VMEM((cores * group, rows_all), bf16),
        pltpu.VMEM((rows_all, wide), bf16),
        pltpu.VMEM((cores * group, width), f32),
    )


class Bag:
    pass


def locals_of(**names):
    bag = Bag()
    bag.__dict__.update(names)
    return bag


def expert_phase(at, hid, slope, stage_in, stage_out):
    experts, cores, core, me_t, width, cap_dev = (
        at.experts, at.cores, at.core, at.me_t, at.width, at.cap_dev
    )
    share, size, per, remote = at.share, at.size, at.per, at.remote
    w_in, w_ins, b_in, b_ins, w_out, w_outs = at.w_in, at.w_ins, at.b_in, at.b_ins, at.w_out, at.w_outs
    b_out_ref, rows_s, res_s, back_ref, own_sem = at.b_out_ref, at.rows_s, at.res_s, at.back_ref, at.own_sem
    h_copy, r_copy, c_copy, g_copy, grow_copy = at.h_copy, at.r_copy, at.c_copy, at.g_copy, at.grow_copy
    grow_s, out_s, gback_ref, gate_in = at.grow_s, at.out_s, at.gback_ref, at.gate_in
    gbout_send, gbout_ref, gbin_own, gbin_send, gbin_rest = (
        at.gbout_send, at.gbout_ref, at.gbin_own, at.gbin_send, at.gbin_rest
    )
    gin_own, gout_own, gin_rest, gout_rest = at.gin_own, at.gout_own, at.gin_rest, at.gout_rest
    w_send, w_recv = at.w_send, at.w_recv

    def forward(i):
        x = rows_s[pl.ds(2 * i, 2)].reshape(2 * cap_dev, width)
        here = pl.ds(pl.multiple_of(2 * cap_dev * i, 16), 2 * cap_dev)
        total = None
        for j in range(cores):
            for n in range(per):
                cols = slice(size * n, size * (n + 1))
                flat = slice(share * j + size * n, share * j + size * (n + 1))
                pre = dot(x, view(w_in, w_ins, j)[:, cols]) + view(b_in, b_ins, j)[:, cols]
                act, steep = gelu_parts(pre)
                act = act.astype(bf16)
                hid[here, flat] = act
                slope[here, flat] = steep.astype(bf16)
                term = dot(act, view(w_out, w_outs, j)[cols, :])
                total = term if total is None else total + term
        res = (total + b_out_ref[...]).astype(bf16)
        res_s[pl.ds(2 * i, 2)] = res.reshape(2, cap_dev, width)

    own_res = pltpu.make_async_copy(res_s.at[0], back_ref.at[0], own_sem.at[0])

    def forward_step(i, _):

        @pl.when(i > 0)
        def _():
            h_copy(2 * i).wait_recv()

        h_copy(2 * i + 1).wait_recv()
        forward(i)

        @pl.when(i > 0)
        def _():
            r_copy(2 * i).start()

        @pl.when(i == 0)
        def _():
            own_res.start()

        r_copy(2 * i + 1).start()
        return 0

    lax.fori_loop(0, experts // 2, forward_step, 0)

    def sent_rows(k, _):
        h_copy(k).wait_send()
        return 0

    lax.fori_loop(1, experts, sent_rows, 0)
    grow_copy.wait()

    def backward(i):
        g = grow_s[pl.ds(2 * i, 2)].reshape(2 * cap_dev, width)
        here = pl.ds(pl.multiple_of(2 * cap_dev * i, 16), 2 * cap_dev)
        total = None
        for j in range(cores):
            for n in range(per):
                cols = slice(size * n, size * (n + 1))
                flat = slice(share * j + size * n, share * j + size * (n + 1))
                grad = dot_nt(g, view(w_out, w_outs, j)[cols, :])
                gpre = (grad * slope[here, flat].astype(f32)).astype(bf16)
                slope[here, flat] = gpre
                term = dot_nt(gpre, view(w_in, w_ins, j)[:, cols])
                total = term if total is None else total + term
        out_s[pl.ds(2 * i, 2)] = total.astype(bf16).reshape(2, cap_dev, width)

    own_grad = pltpu.make_async_copy(out_s.at[0], gback_ref.at[0], own_sem.at[1])

    def backward_step(i, _):
        backward(i)

        @pl.when(i > 0)
        def _():
            g_copy(2 * i).start()

        @pl.when(i == 0)
        def _():
            own_grad.start()

        g_copy(2 * i + 1).start()
        return 0

    lax.fori_loop(0, experts // 2, backward_step, 0)

    def gates_in(k, _):
        c_copy(k).wait()
        return 0

    lax.fori_loop(1, experts, gates_in, 0)

    def scale_rows(k, total):
        square = jnp.broadcast_to(gate_in[k, 0:1, :], (LANES, cap_dev))
        gate = jnp.transpose(square, (1, 0))[:, 0:1]
        rows_s[k] = (rows_s[k].astype(f32) * gate).astype(bf16)
        scaled = (grow_s[k].astype(f32) * gate).astype(bf16)
        grow_s[k] = scaled
        return total + jnp.sum(scaled.astype(f32), 0, keepdims=True)

    bias = lax.fori_loop(0, experts, scale_rows, jnp.zeros((1, width), f32))
    gbout_send[...] = jnp.broadcast_to(bias, gbout_send.shape)
    gbout_ref[me_t] = jnp.broadcast_to(bias, gbout_send.shape)
    rows_all = experts * cap_dev

    def grads(col):
        cols = pl.ds(pl.multiple_of(col, LANES), size)
        left = rows_s[...].reshape(rows_all, width)
        right = grow_s[...].reshape(rows_all, width)
        return dot_tn(left, slope[:, cols]), dot_tn(hid[:, cols], right)

    def column_sums(col):
        cols = pl.ds(pl.multiple_of(col, LANES), size)
        total = jnp.zeros((1, size), f32)
        for k in range(experts):
            square = jnp.broadcast_to(gate_in[k, 0:1, :], (LANES, cap_dev))
            gate = jnp.transpose(square, (1, 0))[:, 0:1]
            here = slice(cap_dev * k, cap_dev * (k + 1))
            total = total + jnp.sum(slope[here, cols].astype(f32) * gate, 0, keepdims=True)
        return total

    pending = []
    for j in list(range(1, cores)) + [0]:
        for n in range(per):
            cols = slice(size * n, size * (n + 1))
            slot = len(pending) % 2
            if len(pending) >= 2:
                for wait in pending[-2]:
                    wait()
            gw_in, gw_out = grads(share * j + size * n)
            stage_in[slot] = gw_in.astype(bf16)
            stage_out[slot] = gw_out.astype(bf16)
            sums = column_sums(share * j + size * n)
            if j == 0:
                gbin_own[:, cols] = sums
                a = pltpu.make_async_copy(stage_in.at[slot], gin_own.at[:, cols], own_sem.at[2 + slot])
                b = pltpu.make_async_copy(stage_out.at[slot], gout_own.at[cols, :], own_sem.at[4 + slot])
                a.start()
                b.start()
                pending.append((a.wait, b.wait))
            else:
                gbin_send[j - 1, :, cols] = sums
                at = (j - 1) * per + n
                a = remote(
                    stage_in.at[slot], gin_rest.at[j - 1, :, cols],
                    w_send.at[0, at], w_recv.at[0, at], core(j),
                )
                b = remote(
                    stage_out.at[slot], gout_rest.at[j - 1, cols, :],
                    w_send.at[1, at], w_recv.at[1, at], core(j),
                )
                a.start()
                b.start()
                pending.append((a.wait_send, b.wait_send))
        if j != 0:
            tail = [
                remote(
                    gbin_send.at[j - 1], gbin_rest.at[j - 1],
                    w_send.at[2, j - 1], w_recv.at[2, j - 1], core(j),
                ),
                remote(
                    gbout_send, gbout_ref.at[me_t],
                    w_send.at[3, j - 1], w_recv.at[3, j - 1], core(j),
                ),
            ]
            for copy in tail:
                copy.start()
    for waits in pending[-2:]:
        for wait in waits:
            wait()
    for j in range(1, cores):
        for n in range(per):
            cols = slice(size * n, size * (n + 1))
            at = (j - 1) * per + n
            remote(
                stage_in.at[0], gin_rest.at[j - 1, :, cols],
                w_send.at[0, at], w_recv.at[0, at], core(j),
            ).wait_recv()
            remote(
                stage_out.at[0], gout_rest.at[j - 1, cols, :],
                w_send.at[1, at], w_recv.at[1, at], core(j),
            ).wait_recv()
        remote(
            gbin_send.at[j - 1], gbin_rest.at[j - 1],
            w_send.at[2, j - 1], w_recv.at[2, j - 1], core(j),
        ).wait()
        remote(
            gbout_send, gbout_ref.at[me_t], w_send.at[3, j - 1], w_recv.at[3, j - 1], core(j)
        ).wait()

    own_res.wait()


def finish_kernel(
    seq, low_ref, small_ref, gbin_own, gbin_rest, gbout_ref, out_own, out_rest, gin_own, gin_rest,
    out_hbm, gin_hbm, gl1, bl1, gq, gk, gv, gbq, gbv, gwp, gbp, gl2, bl2, grout, gbin, gbout, rms,
    out_s, gin_s, in_sem, to_sem
):
    cores, own, seq_pad, width = (out_rest.shape[0] + 1,) + out_rest.shape[1:]
    me_t = lax.axis_index("tensor")
    images = cores * own
    share = gbq.shape[0]
    experts = grout.shape[0]
    jobs = []
    for n, (mine, rest, full, hbm) in enumerate(
        ((out_own, out_rest, out_s, out_hbm), (gin_own, gin_rest, gin_s, gin_hbm))
    ):
        jobs.append((n, mine, rest, full, hbm))
    rows_all = images * seq

    def place(c):
        for n, mine, rest, full, hbm in jobs:
            done = 0
            for im in range(images):
                p = (im // own - c) % cores
                src = mine.at[im % own] if p == 0 else rest.at[p - 1, im % own]
                full[seq * im : seq * (im + 1), :] = src[0:seq, :]
                upto = rows_all if im == images - 1 else seq * (im + 1) // 8 * 8
                pltpu.make_async_copy(
                    full.at[done:upto, :], hbm.at[done:upto, :], to_sem.at[n, im]
                ).start()
                done = upto

    for c in range(cores):

        @pl.when(me_t == c)
        def _(c=c):
            place(c)

    lanes = low_ref.shape[3]
    for c in range(low_ref.shape[1]):
        cols = slice(lanes * c, lanes * (c + 1))
        for grad, phase, n in ((gv, 0, 1), (gq, 1, 0), (gk, 1, 1)):
            grad[:, cols] = low_ref[phase, c, width * n : width * (n + 1), :].astype(f32)
        gwp[cols, :] = jnp.transpose(low_ref[0, c, 0:width, :].astype(f32), (1, 0))
    base = small_base(cores)
    for dst, row in ((gl1, 5), (bl1, 6), (gbp, 4), (gl2, 2), (bl2, 3)):
        dst[...] = small_ref[row]
    which = lax.broadcasted_iota(i32, (base, share), 0)
    for dst, row in ((gbq, 8), (gbv, 8 + cores)):
        dst[...] = jnp.sum(jnp.where(which == row + me_t, small_ref[0:base, 0:share], 0.0), 0)
    grout[...] = small_ref[base + 8 : base + 8 + experts, :]
    value = gbin_own[...]
    for k in range(cores - 1):
        value = value + gbin_rest[k]
    gbin[...] = value
    value = gbout_ref[0, 0:1, :]
    for k in range(1, cores):
        value = value + gbout_ref[k, 0:1, :]
    gbout[...] = value
    count = small_ref[7:8, 0:1] * width
    lanes = lane_iota((1, LANES))
    value = jnp.zeros((1, LANES), f32)
    for n, row in enumerate((base, base + 1, 0, base + 2, 1)):
        square = jnp.sum(small_ref[row : row + 1, :], 1, keepdims=True)
        value = jnp.where(lanes == n, jnp.sqrt(square / count), value)
    rms[...] = value[0, 0:5]
    done = [0] * 2
    for im in range(images):
        upto = rows_all if im == images - 1 else seq * (im + 1) // 8 * 8
        for n, mine, rest, full, hbm in jobs:
            pltpu.make_async_copy(
                full.at[done[n] : upto, :], hbm.at[done[n] : upto, :], to_sem.at[n, im]
            ).wait()
            done[n] = upto


def on_device(
    tokens_in, valid, routes, ln1_gain, ln1_bias, w_query, w_key, w_value, b_query, b_value,
    w_proj, b_proj, ln2_gain, ln2_bias, w_router, w_in, b_in, w_out, b_out, cotangent,
):
    tok_rows, width = tokens_in.shape
    images, seq = valid.shape
    experts = lax.axis_size("expert")
    cores = lax.axis_size("tensor")
    core = lax.axis_index("tensor")
    capacity = (10 * tok_rows // (4 * experts) // 8 + 1) * 8
    cap_dev = up(up(capacity, cores) // cores, 16)
    rows_all = experts * cap_dev
    seq_pad = up(seq, 16)
    key_pad = up(seq_pad, LANES)
    own = images // cores
    tok_own = own * seq
    tok_pad = images * seq_pad
    pad_own = own * seq_pad
    share = w_in.shape[2]
    hidden = share * cores
    wide = width + LANES
    pairs = width // LANES
    S = jax.ShapeDtypeStruct

    dims = (seq, seq_pad, key_pad, own, experts)

    def per_image(*shape):
        return pl.BlockSpec((1,) + shape, lambda i: (i,) + (0,) * len(shape))

    anywhere = pl.BlockSpec(memory_space=pl.ANY)
    inside = pl.BlockSpec(memory_space=pltpu.VMEM)
    block = (experts, cap_dev, width)
    DMA = pltpu.SemaphoreType.DMA
    (
        h1, q, k, v, probs, heads, middle, valid_col, x_pad, h2x, acc_f, send_g, post, fidx,
        wr, wqs, wks, wvs, wps, grow, h2x_rest, w_ins, w_outs, b_ins,
    ) = pl.pallas_call(
        functools.partial(attn_fwd_kernel, (images, seq, seq_pad, key_pad, own, cap_dev)),
        grid=(own,),
        in_specs=[
            *[
                whole(a.shape)
                for a in (
                    tokens_in, cotangent, valid, routes.T, ln1_gain, ln1_bias, w_query, w_key,
                    w_value, w_proj, b_query, b_value, b_proj, ln2_gain, ln2_bias, w_router.T,
                )
            ],
            *[anywhere] * 3,
        ],
        out_specs=[
            per_image(seq_pad, width),
            per_image(seq_pad, width),
            per_image(key_pad, width),
            per_image(key_pad, width),
            per_image(pairs, 2 * seq_pad, key_pad),
            per_image(seq_pad, width),
            per_image(seq_pad, width),
            per_image(seq_pad, 1),
            per_image(seq_pad, width),
            whole((own, seq_pad, wide)),
            whole((8, width)),
            whole(block),
            whole((cores, experts, 1, pad_own)),
            whole((tok_pad, 2)),
            whole((LANES, width)),
            *[anywhere] * 9,
        ],
        out_shape=[
            S((own, seq_pad, width), bf16),
            S((own, seq_pad, width), bf16),
            S((own, key_pad, width), bf16),
            S((own, key_pad, width), bf16),
            S((own, pairs, 2 * seq_pad, key_pad), bf16),
            S((own, seq_pad, width), bf16),
            S((own, seq_pad, width), f32),
            S((own, seq_pad, 1), f32),
            S((own, seq_pad, width), f32),
            S((own, seq_pad, wide), bf16),
            S((8, width), f32),
            S(block, bf16),
            S((cores, experts, 1, pad_own), f32),
            S((tok_pad, 2), i32),
            S((LANES, width), bf16),
            *[S((cores - 1,) + w.shape, bf16) for w in (w_query, w_key, w_value, w_proj)],
            S(block, bf16),
            S((cores - 1, own, seq_pad, wide), bf16),
            S((cores - 1, width, share), bf16),
            S((cores - 1, share, width), bf16),
            S((cores - 1, 1, share), f32),
        ],
        scratch_shapes=[
            *[
                pltpu.VMEM((cores - 1,) + w.shape, bf16)
                for w in (w_query, w_key, w_value, w_proj)
            ],
            pltpu.VMEM((tok_pad, width), bf16),
            pltpu.VMEM((8, up(tok_rows, LANES)), f32),
            pltpu.VMEM((tok_pad, 8), f32),
            pltpu.VMEM((images, key_pad), f32),
            pltpu.VMEM((8, w_query.shape[1]), f32),
            pltpu.VMEM((cores - 1, 8, w_query.shape[1]), f32),
            DMA((7, cores - 1)),
            DMA((7, cores - 1)),
            DMA((cores - 1,)),
            DMA((cores - 1,)),
            DMA((own, cores - 1)),
            DMA((own, cores - 1)),
            DMA((experts,)),
            DMA((experts,)),
            DMA,
            DMA((4,)),
        ],
        compiler_params=params(collective_id=1, has_side_effects=True),
        name="attn_fwd",
    )(
        tokens_in, cotangent, valid, routes.T, ln1_gain, ln1_bias, w_query, w_key, w_value, w_proj,
        b_query, b_value, b_proj, ln2_gain, ln2_bias, w_router.T, w_in[0], w_out[0], b_in,
    )
    attn_w = [w_query, wqs, w_key, wks, w_value, wvs, w_proj, wps]

    size = chunk_of(share)
    per = share // size
    (
        _, _, gin_w, gout_w, gin_rest, gout_rest, gbin_own, gbin_rest, gb_out,
        moe_own, moe_rest, gmoe_own, gmoe_rest,
    ) = pl.pallas_call(
        moe_kernel,
        in_specs=[anywhere, anywhere, inside, anywhere, anywhere] + [inside] * 8,
        out_specs=[anywhere] * 6 + [inside] * 3 + [anywhere] * 4,
        out_shape=[
            S(block, bf16),
            S(block, bf16),
            S((width, share), bf16),
            S((share, width), bf16),
            S((cores - 1, width, share), bf16),
            S((cores - 1, share, width), bf16),
            S((1, share), f32),
            S((cores - 1, 1, share), f32),
            S((cores, 8, width), f32),
            S((pad_own, wide), bf16),
            S((cores - 1, pad_own, wide), bf16),
            S((pad_own, width), bf16),
            S((cores - 1, pad_own, width), bf16),
        ],
        scratch_shapes=[
            pltpu.VMEM((cores, pad_own, wide), bf16),
            pltpu.VMEM(block, bf16),
            pltpu.VMEM(block, bf16),
            pltpu.VMEM(block, bf16),
            pltpu.VMEM(block, bf16),
            pltpu.VMEM((experts, 8, cap_dev), f32),
            pltpu.VMEM((experts, 8, cap_dev), f32),
            pltpu.VMEM((rows_all, 1), f32),
            pltpu.VMEM((cores - 1, 1, share), f32),
            pltpu.VMEM((8, width), f32),
            DMA((2, cores - 1)),
            DMA((2, cores - 1)),
            DMA((2,)),
            DMA((1 + cores,)),
            *[DMA((experts,))] * 8,
            DMA((4, (cores - 1) * per)),
            DMA((4, (cores - 1) * per)),
            DMA((6,)),
        ],
        compiler_params=params(collective_id=2, has_side_effects=True),
        name="moe",
    )(
        h2x.reshape(pad_own, wide), h2x_rest.reshape(cores - 1, pad_own, wide), post, grow, send_g, fidx, w_in[0], w_ins, b_in, b_ins, w_out[0], w_outs, b_out
    )
    def pieces(n):
        return pl.BlockSpec((cores - 1, 1, seq_pad, n), lambda i: (0, i, 0, 0))

    def by_image(x):
        return x.reshape(x.shape[:-2] + (own, seq_pad, x.shape[-1]))

    head_share = w_query.shape[1]
    chunks = 3 if head_share == 3 * LANES else 1
    lanes = head_share // chunks
    buffers = {"pipeline_mode": pl.Buffered(1)} if cores > 2 else {}
    small_b = small_base(cores)
    small_rows = up(small_b + 8 + experts, 8 * cores)
    (
        out_own, gm, gh, dv, first_own, first_rest, small, grad_w_in, grad_w_out,
    ) = pl.pallas_call(
        functools.partial(attn_bwd_a_kernel, dims),
        grid=(own,),
        in_specs=[
            whole(cotangent.shape),
            per_image(seq_pad, 1),
            whole((8, width)),
            per_image(seq_pad, width),
            per_image(seq_pad, wide),
            per_image(seq_pad, width),
            per_image(pairs, 2 * seq_pad, key_pad),
            per_image(seq_pad, width),
            per_image(seq_pad, wide),
            pieces(wide),
            per_image(seq_pad, width),
            pieces(width),
            pl.BlockSpec((width // own, share), lambda i: (i, 0)),
            pl.BlockSpec((cores - 1, width // own, share), lambda i: (0, i, 0), **buffers),
            pl.BlockSpec((share // own, width), lambda i: (i, 0)),
            pl.BlockSpec((cores - 1, share // own, width), lambda i: (0, i, 0), **buffers),
            whole((width,)),
            whole(w_query.shape),
            *[whole(w.shape) for w in attn_w[6:]],
            whole((LANES, width)),
        ],
        out_specs=[
            per_image(seq_pad, width),
            per_image(seq_pad, width),
            per_image(seq_pad, width),
            per_image(seq_pad, width),
            whole((chunks, 2 * width, lanes)),
            whole((cores - 1, chunks, 2 * width, lanes)),
            whole((small_rows, width)),
            pl.BlockSpec((1, width // own, share), lambda i: (0, i, 0)),
            pl.BlockSpec((1, share // own, width), lambda i: (0, i, 0)),
        ],
        out_shape=[
            S((own, seq_pad, width), f32),
            S((own, seq_pad, width), f32),
            S((own, seq_pad, width), bf16),
            S((own, seq_pad, width), bf16),
            S((chunks, 2 * width, lanes), f32),
            S((cores - 1, chunks, 2 * width, lanes), bf16),
            S((small_rows, width), f32),
            S((1, width, share), f32),
            S((1, share, width), f32),
        ],
        scratch_shapes=[pltpu.VMEM((seq_pad, width), f32)]
        + [pltpu.VMEM((pad_own, width), bf16)] * 4,
        compiler_params=params(),
        name="attn_bwd_a",
    )(
        cotangent, valid_col, acc_f, middle, h2x, h1, probs, heads,
        by_image(moe_own), by_image(moe_rest), by_image(gmoe_own), by_image(gmoe_rest),
        gin_w, gin_rest, gout_w, gout_rest, ln2_gain, w_query, *attn_w[6:], wr,
    )
    bits = experts.bit_length() - 1
    piece_rows = small_rows // cores
    low, small, gin_own, out_rest, gin_tok = pl.pallas_call(
        functools.partial(attn_bwd_b_kernel, dims),
        grid=(own,),
        in_specs=[
            per_image(seq_pad, width),
            per_image(key_pad, width),
            per_image(key_pad, width),
            per_image(pairs, 2 * seq_pad, key_pad),
            per_image(seq_pad, width),
            whole((chunks, 2 * width, lanes)),
            anywhere,
            whole((small_rows, width)),
            whole((width,)),
            *[whole(w.shape) for w in attn_w[:6]],
            *[anywhere] * 5,
        ],
        out_specs=[
            anywhere,
            anywhere,
            whole((own, seq_pad, width)),
            anywhere,
            anywhere,
        ],
        out_shape=[
            S((2, chunks, 2 * width, lanes), bf16),
            S((small_rows, width), f32),
            S((own, seq_pad, width), f32),
            S((cores - 1, own, seq_pad, width), f32),
            S((cores - 1, own, seq_pad, width), f32),
        ],
        scratch_shapes=[
            pltpu.VMEM((2, chunks, 2 * width, lanes), bf16),
            pltpu.VMEM((small_rows, width), f32),
            pltpu.VMEM((pad_own, width), bf16),
            pltpu.VMEM((pad_own, width), bf16),
            pltpu.VMEM((own, seq_pad, width), f32),
            pltpu.VMEM((own, seq_pad, width), f32),
            pltpu.VMEM((own, seq_pad, width), bf16),
            pltpu.VMEM((own, seq_pad, width), bf16),
            pltpu.VMEM((cores - 1, chunks, 2 * width, lanes), bf16),
            pltpu.VMEM((2, cores - 1, chunks, 2 * width, lanes), bf16),
            pltpu.VMEM((2, chunks, 2 * width, lanes), f32),
            pltpu.VMEM((2, chunks, 2 * width, lanes), bf16),
            pltpu.VMEM((2, chunks, 2 * width, lanes), bf16),
            pltpu.VMEM((small_rows, width), f32),
            pltpu.VMEM((cores - 1, piece_rows, width), f32),
            pltpu.VMEM((piece_rows, width), f32),
            pltpu.VMEM((bits, piece_rows, width), f32),
            pltpu.VMEM((bits, piece_rows, width), f32),
            DMA((4,)),
            DMA((2, cores - 1, chunks)),
            DMA((2, cores - 1, chunks)),
            DMA((2, chunks, 2 * bits)),
            DMA((2, chunks, 2 * bits)),
            DMA((cores - 1,)),
            DMA((cores - 1,)),
            DMA((bits,)),
            DMA((bits,)),
            DMA((cores - 1,)),
            DMA((cores - 1,)),
            DMA((cores - 1,)),
            DMA((cores - 1,)),
            DMA((own, cores - 1)),
            DMA((own, cores - 1)),
        ],
        compiler_params=params(collective_id=6, has_side_effects=True),
        name="attn_bwd_b",
    )(
        q, k, v, probs, gh, first_own, first_rest, small, ln1_gain, *attn_w[:6],
        x_pad, gm, dv, h1, out_own,
    )
    vector = S((width,), f32)
    part = S((head_share,), f32)
    square = S((width, head_share), f32)
    (
        output, grad_input, gl1, bl1, gq, gk, gv, gbq, gbv, gwp, gbp, gl2, bl2, grout,
        grad_b_in, grad_b_out, rms,
    ) = pl.pallas_call(
        functools.partial(finish_kernel, seq),
        in_specs=[inside] * 9,
        out_specs=[anywhere] * 2 + [inside] * 15,
        out_shape=[
            S(tokens_in.shape, f32), S(tokens_in.shape, f32), vector, vector, square, square, square,
            part, part, S((head_share, width), f32), vector, vector, vector,
            S((experts, width), f32), S((1, share), f32), S((1, width), f32), S((5,), f32),
        ],
        scratch_shapes=[
            pltpu.VMEM(tokens_in.shape, f32),
            pltpu.VMEM(tokens_in.shape, f32),
            DMA((2, images)),
            DMA((2, images)),
        ],
        compiler_params=params(),
        name="finish",
    )(low, small, gbin_own, gbin_rest, gb_out, out_own, out_rest, gin_own, gin_tok)
    return (
        output, grad_input, gl1, bl1, gq, gk, gv, gbq, gbv, gwp, gbp, gl2, bl2, grout.T,
        grad_w_in, grad_b_in, grad_w_out, grad_b_out, rms,
    )


def solution(mesh):
    in_specs = (
        P("expert", None), P("expert", None), P("expert", None), P(), P(),
        P(None, "tensor"), P(None, "tensor"), P(None, "tensor"), P("tensor"), P("tensor"),
        P("tensor", None), P(), P(), P(), P(),
        P("expert", None, "tensor"), P("expert", "tensor"), P("expert", "tensor", None),
        P("expert", None), P("expert", None),
    )
    out_specs = (
        P("expert", None), P("expert", None), P(), P(),
        P(None, "tensor"), P(None, "tensor"), P(None, "tensor"), P("tensor"), P("tensor"),
        P("tensor", None), P(), P(), P(), P(),
        P("expert", None, "tensor"), P("expert", "tensor"), P("expert", "tensor", None),
        P("expert", None), P(),
    )
    return jax.shard_map(
        on_device, mesh=mesh, in_specs=in_specs, out_specs=out_specs, check_vma=False
    )
```

```python
import functools

import jax
import jax.numpy as jnp
from jax import lax
from jax.experimental import pallas as pl
from jax.experimental.pallas import tpu as pltpu
from jax.sharding import PartitionSpec as P

HEAD_DIM = 64
LANES = 128
LOG2E = 1.4426950408889634
MASKED = -1e30
MESH = pl.DeviceIdType.MESH
VMEM_LIMIT = 60 << 20
f32 = jnp.float32
bf16 = jnp.bfloat16
i32 = jnp.int32


def up(value, step):
    return -(-value // step) * step


def params(**more):
    return pltpu.CompilerParams(vmem_limit_bytes=VMEM_LIMIT, **more)


def whole(shape):
    return pl.BlockSpec(shape, lambda *_: (0,) * len(shape), pipeline_mode=pl.Buffered(1))


def dot(a, b):
    return lax.dot_general(a, b, (((1,), (0,)), ((), ())), preferred_element_type=f32)


def dot_nt(a, b):
    return lax.dot_general(a, b, (((1,), (1,)), ((), ())), preferred_element_type=f32)


def dot_tn(a, b):
    return lax.dot_general(a, b, (((0,), (0,)), ((), ())), preferred_element_type=f32)


def lane_iota(shape):
    return lax.broadcasted_iota(i32, shape, len(shape) - 1)


def norm_parts(values):
    center = values - jnp.mean(values, -1, keepdims=True)
    inv_std = lax.rsqrt(jnp.mean(center * center, -1, keepdims=True) + 1e-06)
    return center * inv_std, inv_std


def norm_back(grad_out, normed, inv_std, gain):
    scaled = grad_out * gain
    return inv_std * (
        scaled
        - jnp.mean(scaled, -1, keepdims=True)
        - normed * jnp.mean(scaled * normed, -1, keepdims=True)
    )


def gelu_parts(x):
    z = jnp.abs(x) * 0.7071067811865476
    t = 1.0 / (1.0 + 0.3275911 * z)
    poly = t * (
        0.254829592 * 0.5
        + t
        * (
            -0.284496736 * 0.5
            + t * (1.421413741 * 0.5 + t * (-1.453152027 * 0.5 + t * (1.061405429 * 0.5)))
        )
    )
    e = jnp.exp2(x * x * (-0.5 * LOG2E))
    half = poly * e
    cdf = jnp.where(x >= 0, 1.0 - half, half)
    return x * cdf, cdf + x * e * 0.3989422804014327


def piece(own_ref, rest_ref, j):
    return own_ref[...] if j == 0 else rest_ref[j - 1]


def read_image(dst, src, image, seq):
    for n in range(src.shape[0] // seq):

        @pl.when(image == n)
        def _(n=n):
            dst[0:seq, :] = src[seq * n : seq * (n + 1), :]


def route_rows(dims, expert, core, routes_ref, cot_ref, routes_s, post_ref, fidx_ref, g16):
    images, seq, seq_pad, experts, cap_dev = dims
    tok_pad = images * seq_pad
    wide_s, routes_s = routes_s
    routes_s[...] = jnp.full(routes_s.shape, -1.0, f32)
    wide_s[...] = jnp.zeros_like(wide_s)
    wide_s[0:2, 0 : images * seq] = routes_ref[...].astype(f32)
    turned = jnp.transpose(wide_s[...], (1, 0))
    for i in range(images):
        rows = slice(seq_pad * i, seq_pad * i + seq)
        routes_s[rows, :] = turned[seq * i : seq * (i + 1), :]
        g16[seq_pad * i : seq_pad * (i + 1), :] = jnp.zeros((seq_pad, g16.shape[1]), bf16)
        g16[rows, :] = cot_ref[seq * i : seq * (i + 1), :].astype(bf16)
    r0 = routes_s[:, 0:1].astype(i32)
    r1 = routes_s[:, 1:2].astype(i32)
    lanes = lane_iota((tok_pad, LANES))
    named0 = r0 == lanes
    named1 = r1 == lanes
    named = jnp.where(named0 | named1, 1.0, 0.0)
    named_low = named.astype(bf16)
    lower = (
        lax.broadcasted_iota(i32, (seq_pad, seq_pad), 1)
        < lax.broadcasted_iota(i32, (seq_pad, seq_pad), 0)
    ).astype(f32).astype(bf16)
    run = jnp.zeros((1, LANES), f32)
    parts = []
    for i in range(images):
        rows = slice(seq_pad * i, seq_pad * (i + 1))
        parts.append(dot(lower, named_low[rows]) + run)
        run = run + jnp.sum(named[rows], 0, keepdims=True)
    before = jnp.concatenate(parts, 0) - (core * cap_dev).astype(f32)
    pos = jnp.where(named > 0, before, -1.0)
    groups, _, _, group = post_ref.shape
    for j in range(groups):
        turned = jnp.transpose(pos[group * j : group * (j + 1)], (1, 0))
        for e in range(experts):
            post_ref[j, e] = turned[e : e + 1]
    for k, named_k, r_k in ((0, named0, r0), (1, named1, r1)):
        slot = jnp.sum(jnp.where(named_k, before, 0.0), 1, keepdims=True)
        fits = (slot >= 0) & (slot < cap_dev) & (r_k >= 0)
        turn = jnp.bitwise_xor(r_k, expert)
        half = experts // 2
        far = jnp.where(turn >= half, 1, 0)
        flat = ((turn - far * half) * 2 + far).astype(f32) * cap_dev + slot
        fidx_ref[:, k : k + 1] = jnp.where(fits, flat, -1.0).astype(i32)


def vec(ref):
    return ref[...].reshape(1, -1)


def attn_fwd_kernel(
    dims, tok_ref, cot_ref, valid_ref, routes_ref, g1_ref, b1_ref, wq, wk, wv, wp, bq, bv,
    bp_ref, g2_ref, b2_ref, wr_ref, w_in_hbm, w_out_hbm, b_in_hbm,
    h1_ref, q_ref, k_ref, v_ref, probs_ref, heads_ref, mid_ref, ok_ref, x_ref,
    h2x_ref, acc_ref, sent_ref, post_ref, fidx_ref, wr_pad,
    wqs_hbm, wks_hbm, wvs_hbm, wps_hbm, grow_ref, h2x_rest, w_ins, w_outs, b_ins,
    wqs, wks, wvs, wps, g16, wide_s, routes_s, valid_s, bias_s, bias_in,
    w_send, w_recv, b_send, b_recv, h_send, h_recv, g_send, g_recv, own_sem, keep_sem
):
    images, seq, seq_pad, key_pad, own, cap_dev = dims
    width = tok_ref.shape[1]
    step = pl.program_id(0)
    experts, chip = around("expert")
    cores, core = around("tensor")
    me_e = lax.axis_index("expert")
    me_t = lax.axis_index("tensor")
    image = me_t * own + step
    group = own * seq_pad
    shares = shares_of(wq, wqs)
    share = wq.shape[1]

    def remote(src, dst, send, recv, there):
        return pltpu.make_async_remote_copy(
            src_ref=src, dst_ref=dst, send_sem=send, recv_sem=recv,
            device_id=there, device_id_type=MESH,
        )

    def weight_copy(n, k):
        src, dst = (
            (wq, wqs), (wk, wks), (wv, wvs), (wp, wps),
            (w_in_hbm, w_ins), (w_out_hbm, w_outs), (b_in_hbm, b_ins),
        )[n]
        return remote(src, dst.at[k - 1], w_send.at[n, k - 1], w_recv.at[n, k - 1], core(-k))

    def bias_copy(k):
        return remote(
            bias_s, bias_in.at[k - 1], b_send.at[k - 1], b_recv.at[k - 1], core(-k)
        )

    def h_copy(i, k):
        return remote(
            h2x_ref.at[i], h2x_rest.at[k - 1, i], h_send.at[i, k - 1], h_recv.at[i, k - 1], core(-k)
        )

    def g_copy(k):
        there = {"expert": chip_at(k, experts)}
        return remote(sent_ref.at[k], grow_ref.at[k], g_send.at[k], g_recv.at[k], there)

    own_rows = pltpu.make_async_copy(sent_ref.at[0], grow_ref.at[0], own_sem)
    keeps = [
        pltpu.make_async_copy(src, dst, keep_sem.at[n])
        for n, (src, dst) in enumerate(
            ((wqs, wqs_hbm), (wks, wks_hbm), (wvs, wvs_hbm), (wps, wps_hbm))
        )
    ]

    @pl.when(step == 0)
    def _():
        peers = [core(k) for k in range(1, cores)] + [chip(k) for k in range(1, experts)]
        greet_start(peers)
        route_rows(
            (images, seq, seq_pad, experts, cap_dev), me_e, me_t,
            routes_ref, cot_ref, (wide_s, routes_s), post_ref, fidx_ref, g16,
        )
        greet_end(peers)
        bias_s[0:1, :] = vec(bq)
        bias_s[1:2, :] = vec(bv)
        for k in range(1, cores):
            bias_copy(k).start()
            for n in range(4):
                weight_copy(n, k).start()
        slots = lax.broadcasted_iota(i32, (cap_dev, group), 0).astype(f32)

        def send_rows(n, _):
            k = lax.rem(n + 1, experts)
            total = None
            for j in range(cores):
                named_e = post_ref[j, chip_at(k, experts)]
                pick = jnp.where(named_e == slots, 1.0, 0.0).astype(bf16)
                term = dot(pick, g16[group * j : group * (j + 1), :])
                total = term if total is None else total + term
            sent_ref[k] = total.astype(bf16)

            @pl.when((k > 0) & (k < early_places(experts)))
            def _():
                g_copy(k).start()

            return 0

        lax.fori_loop(0, experts, send_rows, 0)
        own_rows.start()
        valid_s[...] = jnp.zeros_like(valid_s)
        valid_s[:, 0:seq] = valid_ref[...].astype(f32)
        wr_pad[...] = jnp.zeros_like(wr_pad)
        wr_pad[0:experts, :] = wr_ref[...]
        acc_ref[...] = jnp.zeros_like(acc_ref)
        for k in range(1, cores):
            bias_copy(k).wait()
            for n in range(4):
                weight_copy(n, k).wait()
            for n in range(4, 7):
                weight_copy(n, k).start()
        for copy in keeps:
            copy.start()

    x_ref[...] = jnp.zeros_like(x_ref)
    read_image(x_ref.at[0], tok_ref, image, seq)
    x = x_ref[0]
    normed, _ = norm_parts(x)
    h1 = (normed * vec(g1_ref) + vec(b1_ref)).astype(bf16)
    h1_ref[0] = h1
    k_ref[0, seq_pad:, :] = jnp.zeros((key_pad - seq_pad, width), bf16)
    v_ref[0, seq_pad:, :] = jnp.zeros((key_pad - seq_pad, width), bf16)
    for j, cols in enumerate(shares):
        bias = bias_s if j == 0 else bias_in.at[j - 1]
        q_ref[0, :, cols] = (dot(h1, piece(wq, wqs, j)) + bias[0:1, :]).astype(bf16)
        k_ref[0, 0:seq_pad, cols] = dot(h1, piece(wk, wks, j)).astype(bf16)
        v_ref[0, 0:seq_pad, cols] = (dot(h1, piece(wv, wvs, j)) + bias[1:2, :]).astype(bf16)
    low_half = lane_iota((seq_pad, LANES)) < HEAD_DIM
    which = lax.broadcasted_iota(i32, valid_s.shape, 0)
    ok_row = jnp.sum(jnp.where(which == image, valid_s[...], 0.0), 0, keepdims=True)
    ok_col = jnp.transpose(jnp.broadcast_to(ok_row, (LANES, key_pad)), (1, 0))[:seq_pad, 0:1]
    ok_ref[0] = ok_col
    mask = jnp.where(ok_row > 0, 0.0, MASKED)
    for p in range(width // LANES):
        cols = slice(LANES * p, LANES * (p + 1))
        qs = split_heads(q_ref[0, :, cols])
        s = dot_nt(qs, k_ref[0, :, cols]) * (HEAD_DIM**-0.5 * LOG2E) + mask
        e = jnp.exp2(s - jnp.max(s, -1, keepdims=True))
        prob = (e * (1.0 / jnp.sum(e, -1, keepdims=True))).astype(bf16)
        probs_ref[0, p] = prob
        o = dot(prob, v_ref[0, :, cols])
        heads_ref[0, :, cols] = jnp.where(low_half, o[:seq_pad], o[seq_pad:]).astype(bf16)
    attn = vec(bp_ref)
    for j, cols in enumerate(shares):
        attn = attn + dot(heads_ref[0, :, cols], piece(wp, wps, j))
    middle = x + attn
    mid_ref[0] = middle
    for row, field in enumerate((x, middle, attn)):
        acc_ref[row : row + 1, :] += jnp.sum(ok_col * field * field, 0, keepdims=True)
    normed2, _ = norm_parts(middle)
    h2 = (normed2 * vec(g2_ref) + vec(b2_ref)).astype(bf16)
    h2x_ref[step, :, 0:width] = h2
    logits = dot_nt(h2, wr_pad[...])
    logits = jnp.where(lane_iota(logits.shape) < experts, logits, MASKED)
    e = jnp.exp(logits - jnp.max(logits, -1, keepdims=True))
    prob = e / jnp.sum(e, -1, keepdims=True)
    high = prob.astype(bf16).astype(f32)
    h2x_ref[step, :, width:] = (high + pltpu.roll(prob - high, experts, 1)).astype(bf16)
    for k in range(1, cores):
        h_copy(step, k).start()

    @pl.when(step == own - 1)
    def _():
        for k in range(1, cores):
            for n in range(4, 7):
                weight_copy(n, k).wait()
            for i in range(own):
                h_copy(i, k).wait()

        def arrived(k, _):
            g_copy(k).wait()
            return 0

        lax.fori_loop(1, early_places(experts), arrived, 0)
        own_rows.wait()
        for copy in keeps:
            copy.wait()


def split_heads(value):
    low_half = lane_iota(value.shape) < HEAD_DIM
    zero = jnp.zeros_like(value)
    return jnp.concatenate([jnp.where(low_half, value, zero), jnp.where(low_half, zero, value)], 0)


def shares_of(own_ref, rest_ref):
    share = own_ref.shape[1]
    return [slice(share * j, share * (j + 1)) for j in range(rest_ref.shape[0] + 1)]


def add_parts(acc_ref, base, shares, value):
    rows = small_base(len(shares))
    which = lax.broadcasted_iota(i32, (rows, shares[0].stop), 0)
    for j, cols in enumerate(shares):
        owner = lax.rem(lax.axis_index("tensor") + j, len(shares))
        total = jnp.sum(value[:, cols].astype(f32), 0, keepdims=True)
        acc_ref[0:rows, shares[0]] += jnp.where(which == base + owner, total, 0.0)


def attn_bwd_a_kernel(
    dims, cot_ref, valid_ref, accf_ref, mid_ref, h2x_ref, h1_ref, probs_ref, heads_ref,
    moe_own, moe_ref, gmoe_own, gmoe_ref, gin_w, gin_ws, gout_w, gout_ws, g2_ref, wq, wp, wps, wr_ref,
    out_ref, gm_ref, gh_ref, dv_ref, grad_own, grad_rest, acc_ref, gw_in_ref, gw_out_ref,
    c_s, h1_s, heads_s, ga_s, dv_s
):
    seq, seq_pad, key_pad, own, experts = dims
    width = cot_ref.shape[1]
    step = pl.program_id(0)
    shares = shares_of(wq, wps)
    small_b = small_base(len(shares))
    image = lax.axis_index("tensor") * own + step
    at = pl.multiple_of(step * seq_pad, 16)
    c_s[seq // 8 * 8 :, :] = jnp.zeros((seq_pad - seq // 8 * 8, width), f32)
    read_image(c_s, cot_ref, image, seq)
    ok = valid_ref[0]

    @pl.when(step == 0)
    def _():
        acc_ref[...] = jnp.zeros_like(acc_ref)
        acc_ref[small_b : small_b + 8, :] = accf_ref[...]

    def add(row, value):
        acc_ref[row : row + 1, :] += jnp.sum(value, 0, keepdims=True)

    def total(own_ref, rest_ref, cols):
        value = own_ref[0, :, cols].astype(f32)
        for j in range(rest_ref.shape[0]):
            value = value + rest_ref[j, 0, :, cols].astype(f32)
        return value

    for sum_ref, own_ref, rest_ref in (
        (gw_in_ref, gin_w, gin_ws), (gw_out_ref, gout_w, gout_ws)
    ):
        value = own_ref[...].astype(f32)
        for j in range(rest_ref.shape[0]):
            value = value + rest_ref[j].astype(f32)
        sum_ref[0] = value
    middle = mid_ref[0]
    moe = total(moe_own, moe_ref, slice(0, width))
    output = middle + moe
    out_ref[0] = output
    add(0, ok * output * output)
    add(1, ok * moe * moe)
    h2 = h2x_ref[0, :, 0:width]
    pair = h2x_ref[0, :, width:].astype(f32)
    prob = jnp.where(
        lane_iota(pair.shape) < experts, pair + pltpu.roll(pair, LANES - experts, 1), 0.0
    )
    grad_probs = total(moe_own, moe_ref, slice(width, width + LANES))
    grad_logits = (
        prob * (grad_probs - jnp.sum(grad_probs * prob, -1, keepdims=True))
    ).astype(bf16)
    acc_ref[small_b + 8 : small_b + 8 + experts, :] += dot_tn(grad_logits, h2)[:experts]
    grad_h2 = dot(grad_logits, wr_ref[...]) + total(gmoe_own, gmoe_ref, slice(0, width))
    normed2, inv2 = norm_parts(middle)
    add(2, grad_h2 * normed2)
    add(3, grad_h2)
    add(7, jnp.broadcast_to(ok, grad_h2.shape))
    grad_middle = c_s[...] + norm_back(grad_h2, normed2, inv2, vec(g2_ref))
    gm_ref[0] = grad_middle
    grad_attn = grad_middle.astype(bf16)
    add(4, grad_attn.astype(f32))
    here = pl.ds(at, seq_pad)
    ga_s[here, :] = grad_attn
    heads_s[here, :] = heads_ref[0]
    h1_s[here, :] = h1_ref[0]
    for j, cols in enumerate(shares):
        gh_ref[0, :, cols] = dot_nt(grad_attn, piece(wp, wps, j)).astype(bf16)
    for p in range(width // LANES):
        cols = slice(LANES * p, LANES * (p + 1))
        gs = split_heads(gh_ref[0, :, cols])
        dv_s[here, cols] = dot_tn(probs_ref[0, p], gs)[:seq_pad].astype(bf16)
    dv = dv_s[here, :]
    dv_ref[0] = dv
    add_parts(acc_ref, 8 + len(shares), shares, dv)

    @pl.when(step == own - 1)
    def _():
        for n, (left, right) in enumerate(((ga_s, heads_s), (h1_s, dv_s))):
            rows = slice(width * n, width * (n + 1))
            grad = dot_tn(left[...], right[...])
            put_chunks(grad_own, grad_rest, rows, shares, grad)


def put_chunks(own_ref, rest_ref, rows, shares, grad):
    lanes = own_ref.shape[2]
    for j, cols in enumerate(shares):
        for c in range(own_ref.shape[0]):
            value = grad[:, cols.start + lanes * c : cols.start + lanes * (c + 1)]
            if j == 0:
                own_ref[c, rows, :] = value
            else:
                rest_ref[j - 1, c, rows, :] = value.astype(bf16)


def attn_bwd_b_kernel(
    dims, q_ref, k_ref, v_ref, probs_ref, gh_ref, first_own, first_rest, small_ref, g1_ref,
    wq, wqs, wk, wks, wv, wvs, x_hbm, gm_hbm, dv_hbm, h1_hbm, out_hbm,
    low_hbm, small_hbm, gin_ref, outs_ref, gins_ref,
    low, small_out, dq_s, dk_s, x_s, gm_s, dv_s, h1_s, rest_out, rest_s, acc, send_s, recv_s,
    small_a, small_r, small_m, small_s, small_t,
    load_sem, t_send, t_recv, x_send, x_recv, st_send, st_recv, sx_send, sx_recv, sg_send, sg_recv,
    o_send, o_recv, i_send, i_recv
):
    seq, seq_pad, key_pad, own, _ = dims
    width = q_ref.shape[2]
    step = pl.program_id(0)
    shares = shares_of(wq, wqs)
    at = pl.multiple_of(step * seq_pad, 16)
    here = pl.ds(at, seq_pad)
    experts, _ = around("expert")
    cores, core = around("tensor")
    me_e = lax.axis_index("expert")
    me_t = lax.axis_index("tensor")
    bits = experts.bit_length() - 1
    chunks, rows, _ = acc.shape[1:]
    piece_rows = small_r.shape[1]
    low_half = lane_iota((seq_pad, LANES)) < HEAD_DIM

    def my_bit(b):
        return lax.rem(me_e // (1 << b), 2)

    def partner(b):
        return {"expert": me_e + (1 << b) * (1 - 2 * my_bit(b))}

    def remote(src, dst, send, recv, there):
        return pltpu.make_async_remote_copy(
            src_ref=src, dst_ref=dst, send_sem=send, recv_sem=recv,
            device_id=there, device_id_type=MESH,
        )

    orders = []
    for c in range(chunks):
        order = list(range(bits))
        if c == 1:
            order = [1, 0] + order[2:]
        elif c == 2:
            order = order[2:] + order[:2]
        orders.append(order)

    def base_at(c, s):
        value = 0
        for n in range(s):
            value = value + my_bit(orders[c][n]) * (rows >> (n + 1))
        return value

    def inner(phase, c, k):
        source = first_rest if phase == 0 else rest_out
        return remote(
            source.at[k - 1, c], rest_s.at[phase, k - 1, c],
            t_send.at[phase, k - 1, c], t_recv.at[phase, k - 1, c], core(k),
        )

    def across(phase, c, s):
        sems = (x_send.at[phase, c, s], x_recv.at[phase, c, s])
        if s < bits:
            half = rows >> (s + 1)
            box = slice(rows - 2 * half, rows - half)
            return remote(
                send_s.at[phase, c, box, :], recv_s.at[phase, c, box, :], *sems,
                partner(orders[c][s]),
            )
        size = rows >> (2 * bits - s)
        mine = pl.ds(pl.multiple_of(base_at(c, 2 * bits - s), 16), size)
        return remote(
            low.at[phase, c, mine, :], low.at[phase, c, mine, :], *sems,
            partner(orders[c][2 * bits - 1 - s]),
        )

    def send_stage(phase, c, s):
        if s < bits:
            half = rows >> (s + 1)
            away = pl.ds(
                pl.multiple_of(base_at(c, s) + (1 - my_bit(orders[c][s])) * half, 16), half
            )
            send_s[phase, c, rows - 2 * half : rows - half, :] = acc[phase, c, away, :].astype(bf16)
        elif s == bits:
            mine = pl.ds(pl.multiple_of(base_at(c, bits), 16), rows >> bits)
            low[phase, c, mine, :] = acc[phase, c, mine, :].astype(bf16)
        across(phase, c, s).start()

    def end_stage(phase, c, s):
        across(phase, c, s).wait()
        if s < bits:
            half = rows >> (s + 1)
            keep = pl.ds(pl.multiple_of(base_at(c, s + 1), 16), half)
            acc[phase, c, keep, :] += recv_s[phase, c, rows - 2 * half : rows - half, :].astype(f32)

    def point(phase, s):
        for c in range(chunks):
            if s == 0:
                for k in range(1, cores):
                    inner(phase, c, k).wait()
                value = first_own[c] if phase == 0 else acc[phase, c]
                for k in range(cores - 1):
                    value = value + rest_s[phase, k, c].astype(f32)
                acc[phase, c] = value
            else:
                end_stage(phase, c, s - 1)
            if s < 2 * bits:
                send_stage(phase, c, s)

    def out_copy(k):
        return remote(out_hbm, outs_ref.at[k - 1], o_send.at[k - 1], o_recv.at[k - 1], core(k))

    def gin_copy(i, k):
        return remote(
            gin_ref.at[i], gins_ref.at[k - 1, i], i_send.at[i, k - 1], i_recv.at[i, k - 1], core(k)
        )

    loads = [
        pltpu.make_async_copy(src, dst, load_sem.at[n])
        for n, (src, dst) in enumerate(
            ((x_hbm, x_s), (gm_hbm, gm_s), (dv_hbm, dv_s), (h1_hbm, h1_s))
        )
    ]

    @pl.when(step == 0)
    def _():
        peers = [partner(b) for b in range(bits)] + [core(k) for k in range(1, cores)]
        greet_start(peers)
        for copy in loads:
            copy.start()
        greet_end(peers)
        for c in range(chunks):
            for k in range(1, cores):
                inner(0, c, k).start()

    pairs = width // LANES
    points = {}
    hidden_points = 4
    for n in range(hidden_points):
        turn = 4 + (n * (own * pairs - 5)) // max(hidden_points - 1, 1)
        points.setdefault((turn // pairs, turn % pairs), []).append(n)

    for p in range(pairs):
        cols = slice(LANES * p, LANES * (p + 1))
        gs = split_heads(gh_ref[0, :, cols])
        qs = split_heads(q_ref[0, :, cols])
        weights = probs_ref[0, p].astype(f32)
        mixed = weights * dot_nt(gs, v_ref[0, :, cols])
        ds = (
            (mixed - weights * jnp.sum(mixed, -1, keepdims=True)) * (HEAD_DIM**-0.5)
        ).astype(bf16)
        dq = dot(ds, k_ref[0, :, cols])
        dq_s[here, cols] = jnp.where(low_half, dq[:seq_pad], dq[seq_pad:]).astype(bf16)
        dk_s[here, cols] = dot_tn(ds, qs)[:seq_pad].astype(bf16)
        for i in range(own):
            if (i, p) in points:

                @pl.when(step == i)
                def _(i=i, p=p):
                    for n in points[i, p]:
                        point(0, n)
                        if n == 0:
                            for k in range(1, cores):
                                out_copy(k).start()

    @pl.when(step == own - 1)
    def _():
        for copy in loads:
            copy.wait()
        for n, part in enumerate((dq_s, dk_s)):
            box = slice(width * n, width * (n + 1))
            grad = dot_tn(h1_s[...].reshape(own * seq_pad, width), part[...])
            put_chunks(acc.at[1], rest_out, box, shares, grad)
        for c in range(chunks):
            for k in range(1, cores):
                inner(1, c, k).start()
        small_a[...] = small_ref[...]
        add_parts(small_a, 8, shares, dq_s[...])

        def first_norm(i):
            box = slice(seq_pad * i, seq_pad * (i + 1))
            grad_h1 = None
            for j, cols in enumerate(shares):
                for left, own_ref, rest_ref in (
                    (dq_s[box, cols], wq, wqs), (dk_s[box, cols], wk, wks), (dv_s[i, :, cols], wv, wvs)
                ):
                    term = dot_nt(left, piece(own_ref, rest_ref, j))
                    grad_h1 = term if grad_h1 is None else grad_h1 + term
            normed1, inv1 = norm_parts(x_s[i])
            for row, value in ((5, grad_h1 * normed1), (6, grad_h1)):
                small_a[row : row + 1, :] += jnp.sum(value, 0, keepdims=True)
            gin_ref[i] = gm_s[i] + norm_back(grad_h1, normed1, inv1, vec(g1_ref))
            for k in range(1, cores):
                gin_copy(i, k).start()

        def small_piece(k):
            mine = pl.ds(
                pl.multiple_of(lax.rem(me_t + k, cores) * piece_rows, 8), piece_rows
            )
            return remote(
                small_a.at[mine, :], small_r.at[k - 1], st_send.at[k - 1], st_recv.at[k - 1], core(k)
            )

        def small_across(n):
            return remote(small_s.at[n], small_t.at[n], sx_send.at[n], sx_recv.at[n], partner(n))

        mine = pl.ds(pl.multiple_of(me_t * piece_rows, 8), piece_rows)

        def small_back(k):
            return remote(
                small_m, small_out.at[mine, :], sg_send.at[k - 1], sg_recv.at[k - 1], core(k)
            )

        def small_point(n):
            if n == 0:
                for k in range(1, cores):
                    small_piece(k).wait()
                total = small_a[mine, :]
                for k in range(cores - 1):
                    total = total + small_r[k]
                small_m[...] = total
            else:
                small_across(n - 1).wait()
                small_m[...] += small_t[n - 1]
            if n < bits:
                small_s[n] = small_m[...]
                small_across(n).start()
            else:
                small_out[mine, :] = small_m[...]
                for k in range(1, cores):
                    small_back(k).start()

        older = list(range(hidden_points, 2 * bits + 1))
        newer = list(range(2 * bits + 1))
        norms = list(range(own))
        smalls = []
        while older or newer or norms or smalls:
            if norms:
                first_norm(norms.pop(0))
                if not norms:
                    for k in range(1, cores):
                        small_piece(k).start()
                    smalls = list(range(bits + 1))
            elif smalls:
                small_point(smalls.pop(0))
            if older:
                point(0, older.pop(0))
            if newer:
                point(1, newer.pop(0))
        keeps = [pltpu.make_async_copy(low, low_hbm, load_sem.at[0])]
        keeps[0].start()
        for k in range(1, cores):
            small_back(k).wait()
        keeps.append(pltpu.make_async_copy(small_out, small_hbm, load_sem.at[1]))
        keeps[1].start()
        for k in range(1, cores):
            out_copy(k).wait()
            for i in range(own):
                gin_copy(i, k).wait()
        for copy in keeps:
            copy.wait()


def small_base(cores):
    return up(8 + 2 * cores, 8)


def view(own_ref, rest_ref, j):
    return own_ref if j == 0 else rest_ref.at[j - 1]


def chunk_of(hidden):
    for size in (512, 384, 256, 128):
        if hidden % size == 0:
            return size
    return hidden


def greet_start(peers):
    barrier = pltpu.get_barrier_semaphore()
    for peer in peers:
        pl.semaphore_signal(barrier, inc=1, device_id=peer, device_id_type=MESH)


def greet_end(peers):
    pl.semaphore_wait(pltpu.get_barrier_semaphore(), len(peers))


def early_places(experts):
    return experts


def chip_at(place, experts):
    me = lax.axis_index("expert")
    flips = place // 2 + lax.rem(place, 2) * (experts // 2)
    there = me
    for b in range(experts.bit_length() - 1):
        bit = 1 << b
        there = there + lax.rem(flips // bit, 2) * bit * (1 - 2 * lax.rem(me // bit, 2))
    return there


def around(axis):
    n = lax.axis_size(axis)
    me = lax.axis_index(axis)
    return n, lambda k: {axis: lax.rem(me + n + k, n)}


def moe_kernel(
    h2x_ref, h2x_rest, post_ref, grow_hbm, sent_hbm, fidx_ref, w_in, w_ins, b_in, b_ins, w_out, w_outs,
    b_out_ref,
    back_ref, gback_ref, gin_own, gout_own, gin_rest, gout_rest,
    gbin_own, gbin_rest, gbout_ref, moe_own, moe_rest, gmoe_own, gmoe_rest,
    table, out_s, rows_s, grow_s, res_s, gate_out, gate_in, gslot_ref,
    gbin_send, gbout_send,
    m_send, m_recv, load_sem, local_sem, h_send, h_recv, c_send, c_recv, r_send, r_recv, g_send, g_recv,
    l_send, l_recv, w_send, w_recv, own_sem
):
    experts, chip = around("expert")
    cores, core = around("tensor")
    me_e = lax.axis_index("expert")
    me_t = lax.axis_index("tensor")
    cap_dev, width = rows_s.shape[1:]
    group = table.shape[1]
    share = w_in.shape[1]
    size = chunk_of(share)
    per = share // size
    peers = [chip(k) for k in range(1, experts)] + [core(k) for k in range(1, cores)]
    greet_start(peers)

    def remote(src, dst, send, recv, there):
        return pltpu.make_async_remote_copy(
            src_ref=src, dst_ref=dst, send_sem=send, recv_sem=recv,
            device_id=there, device_id_type=MESH,
        )

    early = early_places(experts)
    grow_copy = pltpu.make_async_copy(grow_hbm, grow_s.at[0:early], local_sem.at[0])
    grow_copy.start()
    fills = [
        pltpu.make_async_copy(
            h2x_ref if k == 0 else h2x_rest.at[k - 1],
            table.at[lax.rem(me_t + k, cores)], local_sem.at[1 + k],
        )
        for k in range(cores)
    ]
    for copy in fills:
        copy.start()
    for copy in fills:
        copy.wait()
    greet_end(peers)

    slots = lax.broadcasted_iota(i32, (cap_dev, group), 0).astype(f32)
    lanes = lane_iota((cap_dev, LANES))

    def select(k):
        e = chip_at(k, experts)
        total = None
        for j in range(cores):
            pick = jnp.where(post_ref[j, e] == slots, 1.0, 0.0).astype(bf16)
            term = dot(pick, table[j])
            total = term if total is None else total + term
        mine = (lanes == e) | (lanes == e + experts)
        gate = jnp.sum(jnp.where(mine, total[:, width:], 0.0), 1, keepdims=True)
        gslot_ref[pl.ds(pl.multiple_of(cap_dev * k, 8), cap_dev), :] = gate
        spread = jnp.transpose(jnp.broadcast_to(gate, (cap_dev, LANES)), (1, 0))
        return total[:, :width].astype(bf16), spread[0:8]

    def h_copy(k):
        there = {"expert": chip_at(k, experts)}
        return remote(out_s.at[k], rows_s.at[k], h_send.at[k], h_recv.at[k], there)

    def c_copy(k):
        there = {"expert": chip_at(k, experts)}
        return remote(gate_out.at[k], gate_in.at[k], c_send.at[k], c_recv.at[k], there)

    def r_copy(k):
        there = {"expert": chip_at(k, experts)}
        return remote(res_s.at[k], back_ref.at[k], r_send.at[k], r_recv.at[k], there)

    def g_copy(k):
        there = {"expert": chip_at(k, experts)}
        return remote(out_s.at[k], gback_ref.at[k], g_send.at[k], g_recv.at[k], there)

    def send_rows(j, _):
        k = lax.rem(j + 1, experts)
        rows, gate = select(k)
        out_s[k] = rows
        gate_out[k] = gate

        @pl.when(k > 0)
        def _():
            h_copy(k).start()
            c_copy(k).start()

        return 0

    def l_copy(k):
        there = {"expert": chip_at(k, experts)}
        return remote(sent_hbm.at[k], grow_s.at[k], l_send.at[k], l_recv.at[k], there)

    def send_late(k, _):
        l_copy(k).start()
        return 0

    lax.fori_loop(0, experts, send_rows, 0)
    lax.fori_loop(early, experts, send_late, 0)
    rows_s[0] = out_s[0]
    gate_in[0] = gate_out[0]
    pl.run_scoped(
        functools.partial(
            expert_phase, locals_of(
                experts=experts, cores=cores, core=core, me_t=me_t, width=width, cap_dev=cap_dev,
                share=share, size=size, per=per, w_in=w_in, w_ins=w_ins, b_in=b_in, b_ins=b_ins,
                w_out=w_out, w_outs=w_outs, b_out_ref=b_out_ref, rows_s=rows_s, res_s=res_s,
                back_ref=back_ref, own_sem=own_sem, h_copy=h_copy, r_copy=r_copy, c_copy=c_copy,
                g_copy=g_copy, grow_copy=grow_copy, grow_s=grow_s, out_s=out_s,
                gback_ref=gback_ref, gate_in=gate_in, gbout_send=gbout_send, gbout_ref=gbout_ref,
                gbin_own=gbin_own, gbin_send=gbin_send, gbin_rest=gbin_rest, gin_own=gin_own,
                gout_own=gout_own, gin_rest=gin_rest, gout_rest=gout_rest, w_send=w_send,
                w_recv=w_recv, remote=remote, l_copy=l_copy, early=early,
            ),
        ),
        pltpu.VMEM((experts * cap_dev, share * cores), bf16),
        pltpu.VMEM((experts * cap_dev, share * cores), bf16),
        pltpu.VMEM((2, width, size), bf16),
        pltpu.VMEM((2, size, width), bf16),
    )
    rows_all = experts * cap_dev
    wide = width + LANES

    def token_phase(picks, values, total):
        loads = [
            pltpu.make_async_copy(sent_hbm, grow_s, load_sem.at[0]),
            pltpu.make_async_copy(back_ref, rows_s, load_sem.at[1]),
        ]
        loads[0].start()

        def arrived(k, _):
            r_copy(k).wait()
            return 0

        lax.fori_loop(1, experts, arrived, 0)
        loads[1].start()
        step = 208 if group % 208 == 0 else group
        tiles = group // step
        slot_lanes = lane_iota((step, rows_all))

        def make_picks(i, _):
            tok = pl.ds(pl.multiple_of(i * step, 16), step)
            hit = (fidx_ref[tok, 0:1] == slot_lanes) | (fidx_ref[tok, 1:2] == slot_lanes)
            picks[tok, :] = jnp.where(hit, 1.0, 0.0).astype(bf16)
            return 0

        lax.fori_loop(0, cores * tiles, make_picks, 0)
        for copy in loads:
            copy.wait()

        def gated(k):
            return gslot_ref[pl.ds(pl.multiple_of(cap_dev * k, 8), cap_dev), :]

        def weigh(k, _):
            rows = rows_s[k].astype(f32)
            dots = jnp.sum(rows * grow_s[k].astype(f32), 1, keepdims=True)
            here = pl.ds(pl.multiple_of(cap_dev * k, 16), cap_dev)
            values[here, 0:width] = (rows * gated(k)).astype(bf16)
            mine = lanes == chip_at(k, experts)
            values[here, width:] = jnp.where(mine, dots, 0.0).astype(bf16)
            return 0

        lax.fori_loop(0, experts, weigh, 0)

        def m_copy(kind, k):
            source = table.at[k] if kind == 0 else table.at[k, :, 0:width]
            return remote(
                source, (moe_rest, gmoe_rest)[kind].at[k - 1],
                m_send.at[kind, k - 1], m_recv.at[kind, k - 1], core(k),
            )

        keep_moe = pltpu.make_async_copy(table.at[0], moe_own, load_sem.at[0])
        keep_gmoe = pltpu.make_async_copy(table.at[0, :, 0:width], gmoe_own, load_sem.at[0])

        for k in list(range(1, cores)) + [0]:

            def sums(i, _, k=k):
                tok = pl.ds(
                    pl.multiple_of(lax.rem(me_t + k, cores) * group + i * step, 16), step
                )
                to = pl.ds(pl.multiple_of(i * step, 16), step)
                table[k, to, :] = dot(picks[tok, :], values[...]).astype(bf16)
                return 0

            lax.fori_loop(0, tiles, sums, 0)
            if k > 0:
                m_copy(0, k).start()
        keep_moe.start()
        keep_moe.wait()
        for k in range(1, cores):
            m_copy(0, k).wait()

        batch = 4
        batches = experts // batch
        for b in range(batches):
            first = b * batch
            for k in range(first, first + batch):
                if k > 0:
                    g_copy(k).wait_recv()
                else:
                    own_grad.wait()
            box = pl.ds(first, batch)
            load = pltpu.make_async_copy(gback_ref.at[box], rows_s.at[box], load_sem.at[0])
            load.start()
            load.wait()
            cols = slice(cap_dev * first, cap_dev * (first + batch))
            for k in range(first, first + batch):
                rows_s[k] = (rows_s[k].astype(f32) * gated(k)).astype(bf16)
            for k in list(range(1, cores)) + [0]:

                def gsums(i, _, k=k, b=b, cols=cols, box=box):
                    tok = pl.ds(
                        pl.multiple_of(lax.rem(me_t + k, cores) * group + i * step, 16), step
                    )
                    to = pl.ds(pl.multiple_of(i * step, 16), step)
                    rows = rows_s[box].reshape(batch * cap_dev, width)
                    value = dot(picks[tok, cols], rows)
                    if b > 0:
                        value = value + total[tok, :]
                    if b < batches - 1:
                        total[tok, :] = value
                    else:
                        table[k, to, 0:width] = value.astype(bf16)
                    return 0

                lax.fori_loop(0, tiles, gsums, 0)
                if b == batches - 1 and k > 0:
                    m_copy(1, k).start()
        keep_gmoe.start()
        keep_gmoe.wait()
        for k in range(1, cores):
            m_copy(1, k).wait()

        def finish(k, _):
            g_copy(k).wait_send()
            return 0

        lax.fori_loop(1, experts, finish, 0)

    own_grad = pltpu.make_async_copy(out_s.at[0], gback_ref.at[0], own_sem.at[1])
    pl.run_scoped(
        token_phase,
        pltpu.VMEM((cores * group, rows_all), bf16),
        pltpu.VMEM((rows_all, wide), bf16),
        pltpu.VMEM((cores * group, width), f32),
    )


class Bag:
    pass


def locals_of(**names):
    bag = Bag()
    bag.__dict__.update(names)
    return bag


def expert_phase(at, hid, slope, stage_in, stage_out):
    experts, cores, core, me_t, width, cap_dev = (
        at.experts, at.cores, at.core, at.me_t, at.width, at.cap_dev
    )
    share, size, per, remote = at.share, at.size, at.per, at.remote
    w_in, w_ins, b_in, b_ins, w_out, w_outs = at.w_in, at.w_ins, at.b_in, at.b_ins, at.w_out, at.w_outs
    b_out_ref, rows_s, res_s, back_ref, own_sem = at.b_out_ref, at.rows_s, at.res_s, at.back_ref, at.own_sem
    h_copy, r_copy, c_copy, g_copy, grow_copy = at.h_copy, at.r_copy, at.c_copy, at.g_copy, at.grow_copy
    grow_s, out_s, gback_ref, gate_in = at.grow_s, at.out_s, at.gback_ref, at.gate_in
    gbout_send, gbout_ref, gbin_own, gbin_send, gbin_rest = (
        at.gbout_send, at.gbout_ref, at.gbin_own, at.gbin_send, at.gbin_rest
    )
    gin_own, gout_own, gin_rest, gout_rest = at.gin_own, at.gout_own, at.gin_rest, at.gout_rest
    w_send, w_recv = at.w_send, at.w_recv

    def forward(i):
        x = rows_s[pl.ds(2 * i, 2)].reshape(2 * cap_dev, width)
        here = pl.ds(pl.multiple_of(2 * cap_dev * i, 16), 2 * cap_dev)
        total = None
        for j in range(cores):
            for n in range(per):
                cols = slice(size * n, size * (n + 1))
                flat = slice(share * j + size * n, share * j + size * (n + 1))
                pre = dot(x, view(w_in, w_ins, j)[:, cols]) + view(b_in, b_ins, j)[:, cols]
                act, steep = gelu_parts(pre)
                act = act.astype(bf16)
                hid[here, flat] = act
                slope[here, flat] = steep.astype(bf16)
                term = dot(act, view(w_out, w_outs, j)[cols, :])
                total = term if total is None else total + term
        res = (total + b_out_ref[...]).astype(bf16)
        res_s[pl.ds(2 * i, 2)] = res.reshape(2, cap_dev, width)

    own_res = pltpu.make_async_copy(res_s.at[0], back_ref.at[0], own_sem.at[0])

    def forward_step(i, _):

        @pl.when(i > 0)
        def _():
            h_copy(2 * i).wait_recv()

        h_copy(2 * i + 1).wait_recv()
        forward(i)

        @pl.when(i > 0)
        def _():
            r_copy(2 * i).start()

        @pl.when(i == 0)
        def _():
            own_res.start()

        r_copy(2 * i + 1).start()
        return 0

    lax.fori_loop(0, experts // 2, forward_step, 0)

    def sent_rows(k, _):
        h_copy(k).wait_send()
        return 0

    lax.fori_loop(1, experts, sent_rows, 0)
    grow_copy.wait()

    def late_rows(k, _):
        at.l_copy(k).wait()
        return 0

    lax.fori_loop(at.early, experts, late_rows, 0)

    def backward(i):
        g = grow_s[pl.ds(2 * i, 2)].reshape(2 * cap_dev, width)
        here = pl.ds(pl.multiple_of(2 * cap_dev * i, 16), 2 * cap_dev)
        total = None
        for j in range(cores):
            for n in range(per):
                cols = slice(size * n, size * (n + 1))
                flat = slice(share * j + size * n, share * j + size * (n + 1))
                grad = dot_nt(g, view(w_out, w_outs, j)[cols, :])
                gpre = (grad * slope[here, flat].astype(f32)).astype(bf16)
                slope[here, flat] = gpre
                term = dot_nt(gpre, view(w_in, w_ins, j)[:, cols])
                total = term if total is None else total + term
        out_s[pl.ds(2 * i, 2)] = total.astype(bf16).reshape(2, cap_dev, width)

    own_grad = pltpu.make_async_copy(out_s.at[0], gback_ref.at[0], own_sem.at[1])

    def backward_step(i, _):
        backward(i)

        @pl.when(i > 0)
        def _():
            g_copy(2 * i).start()

        @pl.when(i == 0)
        def _():
            own_grad.start()

        g_copy(2 * i + 1).start()
        return 0

    lax.fori_loop(0, experts // 2, backward_step, 0)

    def gates_in(k, _):
        c_copy(k).wait()
        return 0

    lax.fori_loop(1, experts, gates_in, 0)

    def scale_rows(k, total):
        square = jnp.broadcast_to(gate_in[k, 0:1, :], (LANES, cap_dev))
        gate = jnp.transpose(square, (1, 0))[:, 0:1]
        rows_s[k] = (rows_s[k].astype(f32) * gate).astype(bf16)
        scaled = (grow_s[k].astype(f32) * gate).astype(bf16)
        grow_s[k] = scaled
        return total + jnp.sum(scaled.astype(f32), 0, keepdims=True)

    bias = lax.fori_loop(0, experts, scale_rows, jnp.zeros((1, width), f32))
    gbout_send[...] = jnp.broadcast_to(bias, gbout_send.shape)
    gbout_ref[me_t] = jnp.broadcast_to(bias, gbout_send.shape)
    rows_all = experts * cap_dev

    def grads(col):
        cols = pl.ds(pl.multiple_of(col, LANES), size)
        left = rows_s[...].reshape(rows_all, width)
        right = grow_s[...].reshape(rows_all, width)
        return dot_tn(left, slope[:, cols]), dot_tn(hid[:, cols], right)

    def column_sums(col):
        cols = pl.ds(pl.multiple_of(col, LANES), size)
        total = jnp.zeros((1, size), f32)
        for k in range(experts):
            square = jnp.broadcast_to(gate_in[k, 0:1, :], (LANES, cap_dev))
            gate = jnp.transpose(square, (1, 0))[:, 0:1]
            here = slice(cap_dev * k, cap_dev * (k + 1))
            total = total + jnp.sum(slope[here, cols].astype(f32) * gate, 0, keepdims=True)
        return total

    pending = []
    for j in list(range(1, cores)) + [0]:
        for n in range(per):
            cols = slice(size * n, size * (n + 1))
            slot = len(pending) % 2
            if len(pending) >= 2:
                for wait in pending[-2]:
                    wait()
            gw_in, gw_out = grads(share * j + size * n)
            stage_in[slot] = gw_in.astype(bf16)
            stage_out[slot] = gw_out.astype(bf16)
            sums = column_sums(share * j + size * n)
            if j == 0:
                gbin_own[:, cols] = sums
                a = pltpu.make_async_copy(stage_in.at[slot], gin_own.at[:, cols], own_sem.at[2 + slot])
                b = pltpu.make_async_copy(stage_out.at[slot], gout_own.at[cols, :], own_sem.at[4 + slot])
                a.start()
                b.start()
                pending.append((a.wait, b.wait))
            else:
                gbin_send[j - 1, :, cols] = sums
                at = (j - 1) * per + n
                a = remote(
                    stage_in.at[slot], gin_rest.at[j - 1, :, cols],
                    w_send.at[0, at], w_recv.at[0, at], core(j),
                )
                b = remote(
                    stage_out.at[slot], gout_rest.at[j - 1, cols, :],
                    w_send.at[1, at], w_recv.at[1, at], core(j),
                )
                a.start()
                b.start()
                pending.append((a.wait_send, b.wait_send))
        if j != 0:
            tail = [
                remote(
                    gbin_send.at[j - 1], gbin_rest.at[j - 1],
                    w_send.at[2, j - 1], w_recv.at[2, j - 1], core(j),
                ),
                remote(
                    gbout_send, gbout_ref.at[me_t],
                    w_send.at[3, j - 1], w_recv.at[3, j - 1], core(j),
                ),
            ]
            for copy in tail:
                copy.start()
    for waits in pending[-2:]:
        for wait in waits:
            wait()
    for j in range(1, cores):
        for n in range(per):
            cols = slice(size * n, size * (n + 1))
            at = (j - 1) * per + n
            remote(
                stage_in.at[0], gin_rest.at[j - 1, :, cols],
                w_send.at[0, at], w_recv.at[0, at], core(j),
            ).wait_recv()
            remote(
                stage_out.at[0], gout_rest.at[j - 1, cols, :],
                w_send.at[1, at], w_recv.at[1, at], core(j),
            ).wait_recv()
        remote(
            gbin_send.at[j - 1], gbin_rest.at[j - 1],
            w_send.at[2, j - 1], w_recv.at[2, j - 1], core(j),
        ).wait()
        remote(
            gbout_send, gbout_ref.at[me_t], w_send.at[3, j - 1], w_recv.at[3, j - 1], core(j)
        ).wait()

    own_res.wait()


def finish_kernel(
    seq, low_ref, small_ref, gbin_own, gbin_rest, gbout_ref, out_own, out_rest, gin_own, gin_rest,
    out_hbm, gin_hbm, gq_hbm, gk_hbm, gv_hbm, gwp_hbm, gl1, bl1, gbq, gbv, gbp, gl2, bl2, grout,
    gbin, gbout, rms,
    out_s, gin_s, parts_s, gq, gk, gv, gwp, in_sem, to_sem, g_sem
):
    cores, own, seq_pad, width = (out_rest.shape[0] + 1,) + out_rest.shape[1:]
    me_t = lax.axis_index("tensor")
    images = cores * own
    share = gbq.shape[0]
    experts = grout.shape[0]
    jobs = []
    for n, (mine, rest, full, hbm) in enumerate(
        ((out_own, out_rest, out_s, out_hbm), (gin_own, gin_rest, gin_s, gin_hbm))
    ):
        jobs.append((n, mine, rest, full, hbm))
    rows_all = images * seq

    def incoming(n, p, i):
        _, mine, rest, _, _ = jobs[n]
        src = mine.at[i] if p == 0 else rest.at[p - 1, i]
        return pltpu.make_async_copy(src, parts_s.at[n, p, i], in_sem.at[n, p, i])

    for n in range(2):
        for p in range(cores):
            for i in range(own):
                incoming(n, p, i).start()
    lanes = low_ref.shape[3]
    for c in range(low_ref.shape[1]):
        cols = slice(lanes * c, lanes * (c + 1))
        for grad, phase, n in ((gv, 0, 1), (gq, 1, 0), (gk, 1, 1)):
            grad[:, cols] = low_ref[phase, c, width * n : width * (n + 1), :].astype(f32)
        gwp[cols, :] = jnp.transpose(low_ref[0, c, 0:width, :].astype(f32), (1, 0))
    grads = [
        pltpu.make_async_copy(src, dst, g_sem.at[n])
        for n, (src, dst) in enumerate(((gq, gq_hbm), (gk, gk_hbm), (gv, gv_hbm), (gwp, gwp_hbm)))
    ]
    for copy in grads:
        copy.start()

    def place(c):
        for n, mine, rest, full, hbm in jobs:
            done = 0
            for im in range(images):
                p = (im // own - c) % cores
                incoming(n, p, im % own).wait()
                src = parts_s.at[n, p, im % own]
                full[seq * im : seq * (im + 1), :] = src[0:seq, :]
                upto = rows_all if im == images - 1 else seq * (im + 1) // 8 * 8
                pltpu.make_async_copy(
                    full.at[done:upto, :], hbm.at[done:upto, :], to_sem.at[n, im]
                ).start()
                done = upto

    for c in range(cores):

        @pl.when(me_t == c)
        def _(c=c):
            place(c)

    base = small_base(cores)
    for dst, row in ((gl1, 5), (bl1, 6), (gbp, 4), (gl2, 2), (bl2, 3)):
        dst[...] = small_ref[row]
    which = lax.broadcasted_iota(i32, (base, share), 0)
    for dst, row in ((gbq, 8), (gbv, 8 + cores)):
        dst[...] = jnp.sum(jnp.where(which == row + me_t, small_ref[0:base, 0:share], 0.0), 0)
    grout[...] = small_ref[base + 8 : base + 8 + experts, :]
    value = gbin_own[...]
    for k in range(cores - 1):
        value = value + gbin_rest[k]
    gbin[...] = value
    value = gbout_ref[0, 0:1, :]
    for k in range(1, cores):
        value = value + gbout_ref[k, 0:1, :]
    gbout[...] = value
    count = small_ref[7:8, 0:1] * width
    lanes = lane_iota((1, LANES))
    value = jnp.zeros((1, LANES), f32)
    for n, row in enumerate((base, base + 1, 0, base + 2, 1)):
        square = jnp.sum(small_ref[row : row + 1, :], 1, keepdims=True)
        value = jnp.where(lanes == n, jnp.sqrt(square / count), value)
    rms[...] = value[0, 0:5]
    for copy in grads:
        copy.wait()
    done = [0] * 2
    for im in range(images):
        upto = rows_all if im == images - 1 else seq * (im + 1) // 8 * 8
        for n, mine, rest, full, hbm in jobs:
            pltpu.make_async_copy(
                full.at[done[n] : upto, :], hbm.at[done[n] : upto, :], to_sem.at[n, im]
            ).wait()
            done[n] = upto


def on_device(
    tokens_in, valid, routes, ln1_gain, ln1_bias, w_query, w_key, w_value, b_query, b_value,
    w_proj, b_proj, ln2_gain, ln2_bias, w_router, w_in, b_in, w_out, b_out, cotangent,
):
    tok_rows, width = tokens_in.shape
    images, seq = valid.shape
    experts = lax.axis_size("expert")
    cores = lax.axis_size("tensor")
    core = lax.axis_index("tensor")
    capacity = (10 * tok_rows // (4 * experts) // 8 + 1) * 8
    cap_dev = up(up(capacity, cores) // cores, 16)
    rows_all = experts * cap_dev
    seq_pad = up(seq, 16)
    key_pad = up(seq_pad, LANES)
    own = images // cores
    tok_own = own * seq
    tok_pad = images * seq_pad
    pad_own = own * seq_pad
    share = w_in.shape[2]
    hidden = share * cores
    wide = width + LANES
    pairs = width // LANES
    S = jax.ShapeDtypeStruct

    dims = (seq, seq_pad, key_pad, own, experts)

    def per_image(*shape):
        return pl.BlockSpec((1,) + shape, lambda i: (i,) + (0,) * len(shape))

    anywhere = pl.BlockSpec(memory_space=pl.ANY)
    inside = pl.BlockSpec(memory_space=pltpu.VMEM)
    block = (experts, cap_dev, width)
    DMA = pltpu.SemaphoreType.DMA
    (
        h1, q, k, v, probs, heads, middle, valid_col, x_pad, h2x, acc_f, send_g, post, fidx,
        wr, wqs, wks, wvs, wps, grow, h2x_rest, w_ins, w_outs, b_ins,
    ) = pl.pallas_call(
        functools.partial(attn_fwd_kernel, (images, seq, seq_pad, key_pad, own, cap_dev)),
        grid=(own,),
        in_specs=[
            *[
                whole(a.shape)
                for a in (
                    tokens_in, cotangent, valid, routes.T, ln1_gain, ln1_bias, w_query, w_key,
                    w_value, w_proj, b_query, b_value, b_proj, ln2_gain, ln2_bias, w_router.T,
                )
            ],
            *[anywhere] * 3,
        ],
        out_specs=[
            per_image(seq_pad, width),
            per_image(seq_pad, width),
            per_image(key_pad, width),
            per_image(key_pad, width),
            per_image(pairs, 2 * seq_pad, key_pad),
            per_image(seq_pad, width),
            per_image(seq_pad, width),
            per_image(seq_pad, 1),
            per_image(seq_pad, width),
            whole((own, seq_pad, wide)),
            whole((8, width)),
            whole(block),
            whole((cores, experts, 1, pad_own)),
            whole((tok_pad, 2)),
            whole((LANES, width)),
            *[anywhere] * 9,
        ],
        out_shape=[
            S((own, seq_pad, width), bf16),
            S((own, seq_pad, width), bf16),
            S((own, key_pad, width), bf16),
            S((own, key_pad, width), bf16),
            S((own, pairs, 2 * seq_pad, key_pad), bf16),
            S((own, seq_pad, width), bf16),
            S((own, seq_pad, width), f32),
            S((own, seq_pad, 1), f32),
            S((own, seq_pad, width), f32),
            S((own, seq_pad, wide), bf16),
            S((8, width), f32),
            S(block, bf16),
            S((cores, experts, 1, pad_own), f32),
            S((tok_pad, 2), i32),
            S((LANES, width), bf16),
            *[S((cores - 1,) + w.shape, bf16) for w in (w_query, w_key, w_value, w_proj)],
            S((early_places(experts), cap_dev, width), bf16),
            S((cores - 1, own, seq_pad, wide), bf16),
            S((cores - 1, width, share), bf16),
            S((cores - 1, share, width), bf16),
            S((cores - 1, 1, share), f32),
        ],
        scratch_shapes=[
            *[
                pltpu.VMEM((cores - 1,) + w.shape, bf16)
                for w in (w_query, w_key, w_value, w_proj)
            ],
            pltpu.VMEM((tok_pad, width), bf16),
            pltpu.VMEM((8, up(tok_rows, LANES)), f32),
            pltpu.VMEM((tok_pad, 8), f32),
            pltpu.VMEM((images, key_pad), f32),
            pltpu.VMEM((8, w_query.shape[1]), f32),
            pltpu.VMEM((cores - 1, 8, w_query.shape[1]), f32),
            DMA((7, cores - 1)),
            DMA((7, cores - 1)),
            DMA((cores - 1,)),
            DMA((cores - 1,)),
            DMA((own, cores - 1)),
            DMA((own, cores - 1)),
            DMA((experts,)),
            DMA((experts,)),
            DMA,
            DMA((4,)),
        ],
        compiler_params=params(collective_id=1, has_side_effects=True),
        name="attn_fwd",
    )(
        tokens_in, cotangent, valid, routes.T, ln1_gain, ln1_bias, w_query, w_key, w_value, w_proj,
        b_query, b_value, b_proj, ln2_gain, ln2_bias, w_router.T, w_in[0], w_out[0], b_in,
    )
    attn_w = [w_query, wqs, w_key, wks, w_value, wvs, w_proj, wps]

    size = chunk_of(share)
    per = share // size
    (
        _, _, gin_w, gout_w, gin_rest, gout_rest, gbin_own, gbin_rest, gb_out,
        moe_own, moe_rest, gmoe_own, gmoe_rest,
    ) = pl.pallas_call(
        moe_kernel,
        in_specs=[anywhere, anywhere, inside, anywhere, anywhere] + [inside] * 8,
        out_specs=[anywhere] * 6 + [inside] * 3 + [anywhere] * 4,
        out_shape=[
            S(block, bf16),
            S(block, bf16),
            S((width, share), bf16),
            S((share, width), bf16),
            S((cores - 1, width, share), bf16),
            S((cores - 1, share, width), bf16),
            S((1, share), f32),
            S((cores - 1, 1, share), f32),
            S((cores, 8, width), f32),
            S((pad_own, wide), bf16),
            S((cores - 1, pad_own, wide), bf16),
            S((pad_own, width), bf16),
            S((cores - 1, pad_own, width), bf16),
        ],
        scratch_shapes=[
            pltpu.VMEM((cores, pad_own, wide), bf16),
            pltpu.VMEM(block, bf16),
            pltpu.VMEM(block, bf16),
            pltpu.VMEM(block, bf16),
            pltpu.VMEM(block, bf16),
            pltpu.VMEM((experts, 8, cap_dev), f32),
            pltpu.VMEM((experts, 8, cap_dev), f32),
            pltpu.VMEM((rows_all, 1), f32),
            pltpu.VMEM((cores - 1, 1, share), f32),
            pltpu.VMEM((8, width), f32),
            DMA((2, cores - 1)),
            DMA((2, cores - 1)),
            DMA((2,)),
            DMA((1 + cores,)),
            *[DMA((experts,))] * 10,
            DMA((4, (cores - 1) * per)),
            DMA((4, (cores - 1) * per)),
            DMA((6,)),
        ],
        compiler_params=params(collective_id=2, has_side_effects=True),
        name="moe",
    )(
        h2x.reshape(pad_own, wide), h2x_rest.reshape(cores - 1, pad_own, wide), post, grow, send_g, fidx, w_in[0], w_ins, b_in, b_ins, w_out[0], w_outs, b_out
    )
    def pieces(n):
        return pl.BlockSpec((cores - 1, 1, seq_pad, n), lambda i: (0, i, 0, 0))

    def by_image(x):
        return x.reshape(x.shape[:-2] + (own, seq_pad, x.shape[-1]))

    head_share = w_query.shape[1]
    chunks = 3 if head_share == 3 * LANES else 1
    lanes = head_share // chunks
    buffers = {"pipeline_mode": pl.Buffered(1)} if cores > 2 else {}
    small_b = small_base(cores)
    small_rows = up(small_b + 8 + experts, 8 * cores)
    (
        out_own, gm, gh, dv, first_own, first_rest, small, grad_w_in, grad_w_out,
    ) = pl.pallas_call(
        functools.partial(attn_bwd_a_kernel, dims),
        grid=(own,),
        in_specs=[
            whole(cotangent.shape),
            per_image(seq_pad, 1),
            whole((8, width)),
            per_image(seq_pad, width),
            per_image(seq_pad, wide),
            per_image(seq_pad, width),
            per_image(pairs, 2 * seq_pad, key_pad),
            per_image(seq_pad, width),
            per_image(seq_pad, wide),
            pieces(wide),
            per_image(seq_pad, width),
            pieces(width),
            pl.BlockSpec((width // own, share), lambda i: (i, 0)),
            pl.BlockSpec((cores - 1, width // own, share), lambda i: (0, i, 0), **buffers),
            pl.BlockSpec((share // own, width), lambda i: (i, 0)),
            pl.BlockSpec((cores - 1, share // own, width), lambda i: (0, i, 0), **buffers),
            whole((width,)),
            whole(w_query.shape),
            *[whole(w.shape) for w in attn_w[6:]],
            whole((LANES, width)),
        ],
        out_specs=[
            per_image(seq_pad, width),
            per_image(seq_pad, width),
            per_image(seq_pad, width),
            per_image(seq_pad, width),
            whole((chunks, 2 * width, lanes)),
            whole((cores - 1, chunks, 2 * width, lanes)),
            whole((small_rows, width)),
            pl.BlockSpec((1, width // own, share), lambda i: (0, i, 0)),
            pl.BlockSpec((1, share // own, width), lambda i: (0, i, 0)),
        ],
        out_shape=[
            S((own, seq_pad, width), f32),
            S((own, seq_pad, width), f32),
            S((own, seq_pad, width), bf16),
            S((own, seq_pad, width), bf16),
            S((chunks, 2 * width, lanes), f32),
            S((cores - 1, chunks, 2 * width, lanes), bf16),
            S((small_rows, width), f32),
            S((1, width, share), f32),
            S((1, share, width), f32),
        ],
        scratch_shapes=[pltpu.VMEM((seq_pad, width), f32)]
        + [pltpu.VMEM((pad_own, width), bf16)] * 4,
        compiler_params=params(),
        name="attn_bwd_a",
    )(
        cotangent, valid_col, acc_f, middle, h2x, h1, probs, heads,
        by_image(moe_own), by_image(moe_rest), by_image(gmoe_own), by_image(gmoe_rest),
        gin_w, gin_rest, gout_w, gout_rest, ln2_gain, w_query, *attn_w[6:], wr,
    )
    bits = experts.bit_length() - 1
    piece_rows = small_rows // cores
    low, small, gin_own, out_rest, gin_tok = pl.pallas_call(
        functools.partial(attn_bwd_b_kernel, dims),
        grid=(own,),
        in_specs=[
            per_image(seq_pad, width),
            per_image(key_pad, width),
            per_image(key_pad, width),
            per_image(pairs, 2 * seq_pad, key_pad),
            per_image(seq_pad, width),
            whole((chunks, 2 * width, lanes)),
            anywhere,
            whole((small_rows, width)),
            whole((width,)),
            *[whole(w.shape) for w in attn_w[:6]],
            *[anywhere] * 5,
        ],
        out_specs=[
            anywhere,
            anywhere,
            whole((own, seq_pad, width)),
            anywhere,
            anywhere,
        ],
        out_shape=[
            S((2, chunks, 2 * width, lanes), bf16),
            S((small_rows, width), f32),
            S((own, seq_pad, width), f32),
            S((cores - 1, own, seq_pad, width), f32),
            S((cores - 1, own, seq_pad, width), f32),
        ],
        scratch_shapes=[
            pltpu.VMEM((2, chunks, 2 * width, lanes), bf16),
            pltpu.VMEM((small_rows, width), f32),
            pltpu.VMEM((pad_own, width), bf16),
            pltpu.VMEM((pad_own, width), bf16),
            pltpu.VMEM((own, seq_pad, width), f32),
            pltpu.VMEM((own, seq_pad, width), f32),
            pltpu.VMEM((own, seq_pad, width), bf16),
            pltpu.VMEM((own, seq_pad, width), bf16),
            pltpu.VMEM((cores - 1, chunks, 2 * width, lanes), bf16),
            pltpu.VMEM((2, cores - 1, chunks, 2 * width, lanes), bf16),
            pltpu.VMEM((2, chunks, 2 * width, lanes), f32),
            pltpu.VMEM((2, chunks, 2 * width, lanes), bf16),
            pltpu.VMEM((2, chunks, 2 * width, lanes), bf16),
            pltpu.VMEM((small_rows, width), f32),
            pltpu.VMEM((cores - 1, piece_rows, width), f32),
            pltpu.VMEM((piece_rows, width), f32),
            pltpu.VMEM((bits, piece_rows, width), f32),
            pltpu.VMEM((bits, piece_rows, width), f32),
            DMA((4,)),
            DMA((2, cores - 1, chunks)),
            DMA((2, cores - 1, chunks)),
            DMA((2, chunks, 2 * bits)),
            DMA((2, chunks, 2 * bits)),
            DMA((cores - 1,)),
            DMA((cores - 1,)),
            DMA((bits,)),
            DMA((bits,)),
            DMA((cores - 1,)),
            DMA((cores - 1,)),
            DMA((cores - 1,)),
            DMA((cores - 1,)),
            DMA((own, cores - 1)),
            DMA((own, cores - 1)),
        ],
        compiler_params=params(collective_id=6, has_side_effects=True),
        name="attn_bwd_b",
    )(
        q, k, v, probs, gh, first_own, first_rest, small, ln1_gain, *attn_w[:6],
        x_pad, gm, dv, h1, out_own,
    )
    vector = S((width,), f32)
    part = S((head_share,), f32)
    square = S((width, head_share), f32)
    (
        output, grad_input, gq, gk, gv, gwp, gl1, bl1, gbq, gbv, gbp, gl2, bl2, grout,
        grad_b_in, grad_b_out, rms,
    ) = pl.pallas_call(
        functools.partial(finish_kernel, seq),
        in_specs=[inside] * 5 + [anywhere] * 4,
        out_specs=[anywhere] * 6 + [inside] * 11,
        out_shape=[
            S(tokens_in.shape, f32), S(tokens_in.shape, f32), square, square, square,
            S((head_share, width), f32), vector, vector, part, part, vector, vector, vector,
            S((experts, width), f32), S((1, share), f32), S((1, width), f32), S((5,), f32),
        ],
        scratch_shapes=[
            pltpu.VMEM(tokens_in.shape, f32),
            pltpu.VMEM(tokens_in.shape, f32),
            pltpu.VMEM((2, cores, own, seq_pad, width), f32),
            *[pltpu.VMEM((width, head_share), f32)] * 3,
            pltpu.VMEM((head_share, width), f32),
            DMA((2, cores, own)),
            DMA((2, images)),
            DMA((4,)),
        ],
        compiler_params=params(),
        name="finish",
    )(low, small, gbin_own, gbin_rest, gb_out, out_own, out_rest, gin_own, gin_tok)
    return (
        output, grad_input, gl1, bl1, gq, gk, gv, gbq, gbv, gwp, gbp, gl2, bl2, grout.T,
        grad_w_in, grad_b_in, grad_w_out, grad_b_out, rms,
    )


def solution(mesh):
    in_specs = (
        P("expert", None), P("expert", None), P("expert", None), P(), P(),
        P(None, "tensor"), P(None, "tensor"), P(None, "tensor"), P("tensor"), P("tensor"),
        P("tensor", None), P(), P(), P(), P(),
        P("expert", None, "tensor"), P("expert", "tensor"), P("expert", "tensor", None),
        P("expert", None), P("expert", None),
    )
    out_specs = (
        P("expert", None), P("expert", None), P(), P(),
        P(None, "tensor"), P(None, "tensor"), P(None, "tensor"), P("tensor"), P("tensor"),
        P("tensor", None), P(), P(), P(), P(),
        P("expert", None, "tensor"), P("expert", "tensor"), P("expert", "tensor", None),
        P("expert", None), P(),
    )
    return jax.shard_map(
        on_device, mesh=mesh, in_specs=in_specs, out_specs=out_specs, check_vma=False
    )
```

```python
import functools

import jax
import jax.numpy as jnp
from jax import lax
from jax.experimental import pallas as pl
from jax.experimental.pallas import tpu as pltpu
from jax.sharding import PartitionSpec as P

HEAD_DIM = 64
LANES = 128
LOG2E = 1.4426950408889634
MASKED = -1e30
MESH = pl.DeviceIdType.MESH
VMEM_LIMIT = 60 << 20
f32 = jnp.float32
bf16 = jnp.bfloat16
i32 = jnp.int32


def up(value, step):
    return -(-value // step) * step


def params(**more):
    return pltpu.CompilerParams(vmem_limit_bytes=VMEM_LIMIT, **more)


def whole(shape):
    return pl.BlockSpec(shape, lambda *_: (0,) * len(shape), pipeline_mode=pl.Buffered(1))


def dot(a, b):
    return lax.dot_general(a, b, (((1,), (0,)), ((), ())), preferred_element_type=f32)


def dot_nt(a, b):
    return lax.dot_general(a, b, (((1,), (1,)), ((), ())), preferred_element_type=f32)


def dot_tn(a, b):
    return lax.dot_general(a, b, (((0,), (0,)), ((), ())), preferred_element_type=f32)


def lane_iota(shape):
    return lax.broadcasted_iota(i32, shape, len(shape) - 1)


def norm_parts(values):
    center = values - jnp.mean(values, -1, keepdims=True)
    inv_std = lax.rsqrt(jnp.mean(center * center, -1, keepdims=True) + 1e-06)
    return center * inv_std, inv_std


def norm_back(grad_out, normed, inv_std, gain):
    scaled = grad_out * gain
    return inv_std * (
        scaled
        - jnp.mean(scaled, -1, keepdims=True)
        - normed * jnp.mean(scaled * normed, -1, keepdims=True)
    )


def gelu_parts(x):
    z = jnp.abs(x) * 0.7071067811865476
    t = 1.0 / (1.0 + 0.3275911 * z)
    poly = t * (
        0.254829592 * 0.5
        + t
        * (
            -0.284496736 * 0.5
            + t * (1.421413741 * 0.5 + t * (-1.453152027 * 0.5 + t * (1.061405429 * 0.5)))
        )
    )
    e = jnp.exp2(x * x * (-0.5 * LOG2E))
    half = poly * e
    cdf = jnp.where(x >= 0, 1.0 - half, half)
    return x * cdf, cdf + x * e * 0.3989422804014327


def piece(own_ref, rest_ref, j):
    return own_ref[...] if j == 0 else rest_ref[j - 1]


def read_image(dst, src, image, seq):
    for n in range(src.shape[0] // seq):

        @pl.when(image == n)
        def _(n=n):
            dst[0:seq, :] = src[seq * n : seq * (n + 1), :]


def route_rows(dims, expert, core, routes_ref, cot_ref, routes_s, post_ref, fidx_ref, g16):
    images, seq, seq_pad, experts, cap_dev = dims
    tok_pad = images * seq_pad
    wide_s, routes_s = routes_s
    routes_s[...] = jnp.full(routes_s.shape, -1.0, f32)
    wide_s[...] = jnp.zeros_like(wide_s)
    wide_s[0:2, 0 : images * seq] = routes_ref[...].astype(f32)
    turned = jnp.transpose(wide_s[...], (1, 0))
    for i in range(images):
        rows = slice(seq_pad * i, seq_pad * i + seq)
        routes_s[rows, :] = turned[seq * i : seq * (i + 1), :]
        g16[seq_pad * i : seq_pad * (i + 1), :] = jnp.zeros((seq_pad, g16.shape[1]), bf16)
        g16[rows, :] = cot_ref[seq * i : seq * (i + 1), :].astype(bf16)
    r0 = routes_s[:, 0:1].astype(i32)
    r1 = routes_s[:, 1:2].astype(i32)
    lanes = lane_iota((tok_pad, LANES))
    named0 = r0 == lanes
    named1 = r1 == lanes
    named = jnp.where(named0 | named1, 1.0, 0.0)
    named_low = named.astype(bf16)
    lower = (
        lax.broadcasted_iota(i32, (seq_pad, seq_pad), 1)
        < lax.broadcasted_iota(i32, (seq_pad, seq_pad), 0)
    ).astype(f32).astype(bf16)
    run = jnp.zeros((1, LANES), f32)
    parts = []
    for i in range(images):
        rows = slice(seq_pad * i, seq_pad * (i + 1))
        parts.append(dot(lower, named_low[rows]) + run)
        run = run + jnp.sum(named[rows], 0, keepdims=True)
    before = jnp.concatenate(parts, 0) - (core * cap_dev).astype(f32)
    pos = jnp.where(named > 0, before, -1.0)
    groups, _, _, group = post_ref.shape
    for j in range(groups):
        turned = jnp.transpose(pos[group * j : group * (j + 1)], (1, 0))
        for e in range(experts):
            post_ref[j, e] = turned[e : e + 1]
    for k, named_k, r_k in ((0, named0, r0), (1, named1, r1)):
        slot = jnp.sum(jnp.where(named_k, before, 0.0), 1, keepdims=True)
        fits = (slot >= 0) & (slot < cap_dev) & (r_k >= 0)
        turn = jnp.bitwise_xor(r_k, expert)
        half = experts // 2
        far = jnp.where(turn >= half, 1, 0)
        flat = ((turn - far * half) * 2 + far).astype(f32) * cap_dev + slot
        fidx_ref[:, k : k + 1] = jnp.where(fits, flat, -1.0).astype(i32)


def vec(ref):
    return ref[...].reshape(1, -1)


def attn_fwd_kernel(
    dims, tok_ref, cot_ref, valid_ref, routes_ref, g1_ref, b1_ref, wq, wk, wv, wp, bq, bv,
    bp_ref, g2_ref, b2_ref, wr_ref, w_in_hbm, w_out_hbm, b_in_hbm,
    h1_ref, q_ref, k_ref, v_ref, probs_ref, heads_ref, mid_ref, ok_ref, x_ref,
    h2x_ref, acc_ref, sent_ref, post_ref, fidx_ref, wr_pad,
    wqs_hbm, wks_hbm, wvs_hbm, wps_hbm, grow_ref, h2x_rest, w_ins, w_outs, b_ins,
    wqs, wks, wvs, wps, g16, wide_s, routes_s, valid_s, bias_s, bias_in,
    w_send, w_recv, b_send, b_recv, h_send, h_recv, g_send, g_recv, own_sem, keep_sem
):
    images, seq, seq_pad, key_pad, own, cap_dev = dims
    width = tok_ref.shape[1]
    step = pl.program_id(0)
    experts, chip = around("expert")
    cores, core = around("tensor")
    me_e = lax.axis_index("expert")
    me_t = lax.axis_index("tensor")
    image = me_t * own + step
    group = own * seq_pad
    shares = shares_of(wq, wqs)
    share = wq.shape[1]

    def remote(src, dst, send, recv, there):
        return pltpu.make_async_remote_copy(
            src_ref=src, dst_ref=dst, send_sem=send, recv_sem=recv,
            device_id=there, device_id_type=MESH,
        )

    def weight_copy(n, k):
        src, dst = (
            (wq, wqs), (wk, wks), (wv, wvs), (wp, wps),
            (w_in_hbm, w_ins), (w_out_hbm, w_outs), (b_in_hbm, b_ins),
        )[n]
        return remote(src, dst.at[k - 1], w_send.at[n, k - 1], w_recv.at[n, k - 1], core(-k))

    def bias_copy(k):
        return remote(
            bias_s, bias_in.at[k - 1], b_send.at[k - 1], b_recv.at[k - 1], core(-k)
        )

    def h_copy(i, k):
        return remote(
            h2x_ref.at[i], h2x_rest.at[k - 1, i], h_send.at[i, k - 1], h_recv.at[i, k - 1], core(-k)
        )

    def g_copy(k):
        there = {"expert": chip_at(k, experts)}
        return remote(sent_ref.at[k], grow_ref.at[k], g_send.at[k], g_recv.at[k], there)

    own_rows = pltpu.make_async_copy(sent_ref.at[0], grow_ref.at[0], own_sem)
    keeps = [
        pltpu.make_async_copy(src, dst, keep_sem.at[n])
        for n, (src, dst) in enumerate(
            ((wqs, wqs_hbm), (wks, wks_hbm), (wvs, wvs_hbm), (wps, wps_hbm))
        )
    ]

    @pl.when(step == 0)
    def _():
        peers = [core(k) for k in range(1, cores)] + [chip(k) for k in range(1, experts)]
        greet_start(peers)
        route_rows(
            (images, seq, seq_pad, experts, cap_dev), me_e, me_t,
            routes_ref, cot_ref, (wide_s, routes_s), post_ref, fidx_ref, g16,
        )
        greet_end(peers)
        bias_s[0:1, :] = vec(bq)
        bias_s[1:2, :] = vec(bv)
        for k in range(1, cores):
            bias_copy(k).start()
            for n in range(4):
                weight_copy(n, k).start()
        slots = lax.broadcasted_iota(i32, (cap_dev, group), 0).astype(f32)

        def send_rows(n, _):
            k = lax.rem(n + 1, experts)
            total = None
            for j in range(cores):
                named_e = post_ref[j, chip_at(k, experts)]
                pick = jnp.where(named_e == slots, 1.0, 0.0).astype(bf16)
                term = dot(pick, g16[group * j : group * (j + 1), :])
                total = term if total is None else total + term
            sent_ref[k] = total.astype(bf16)

            @pl.when((k > 0) & (k < early_places(experts)))
            def _():
                g_copy(k).start()

            return 0

        lax.fori_loop(0, experts, send_rows, 0)
        own_rows.start()
        valid_s[...] = jnp.zeros_like(valid_s)
        valid_s[:, 0:seq] = valid_ref[...].astype(f32)
        wr_pad[...] = jnp.zeros_like(wr_pad)
        wr_pad[0:experts, :] = wr_ref[...]
        acc_ref[...] = jnp.zeros_like(acc_ref)
        for k in range(1, cores):
            bias_copy(k).wait()
            for n in range(4):
                weight_copy(n, k).wait()
            for n in range(4, 7):
                weight_copy(n, k).start()
        for copy in keeps:
            copy.start()

    x_ref[...] = jnp.zeros_like(x_ref)
    read_image(x_ref.at[0], tok_ref, image, seq)
    x = x_ref[0]
    normed, _ = norm_parts(x)
    h1 = (normed * vec(g1_ref) + vec(b1_ref)).astype(bf16)
    h1_ref[0] = h1
    k_ref[0, seq_pad:, :] = jnp.zeros((key_pad - seq_pad, width), bf16)
    v_ref[0, seq_pad:, :] = jnp.zeros((key_pad - seq_pad, width), bf16)
    for j, cols in enumerate(shares):
        bias = bias_s if j == 0 else bias_in.at[j - 1]
        q_ref[0, :, cols] = (dot(h1, piece(wq, wqs, j)) + bias[0:1, :]).astype(bf16)
        k_ref[0, 0:seq_pad, cols] = dot(h1, piece(wk, wks, j)).astype(bf16)
        v_ref[0, 0:seq_pad, cols] = (dot(h1, piece(wv, wvs, j)) + bias[1:2, :]).astype(bf16)
    low_half = lane_iota((seq_pad, LANES)) < HEAD_DIM
    which = lax.broadcasted_iota(i32, valid_s.shape, 0)
    ok_row = jnp.sum(jnp.where(which == image, valid_s[...], 0.0), 0, keepdims=True)
    ok_col = jnp.transpose(jnp.broadcast_to(ok_row, (LANES, key_pad)), (1, 0))[:seq_pad, 0:1]
    ok_ref[0] = ok_col
    mask = jnp.where(ok_row > 0, 0.0, MASKED)
    for p in range(width // LANES):
        cols = slice(LANES * p, LANES * (p + 1))
        qs = split_heads(q_ref[0, :, cols])
        s = dot_nt(qs, k_ref[0, :, cols]) * (HEAD_DIM**-0.5 * LOG2E) + mask
        e = jnp.exp2(s - jnp.max(s, -1, keepdims=True))
        prob = (e * (1.0 / jnp.sum(e, -1, keepdims=True))).astype(bf16)
        probs_ref[0, p] = prob
        o = dot(prob, v_ref[0, :, cols])
        heads_ref[0, :, cols] = jnp.where(low_half, o[:seq_pad], o[seq_pad:]).astype(bf16)
    attn = vec(bp_ref)
    for j, cols in enumerate(shares):
        attn = attn + dot(heads_ref[0, :, cols], piece(wp, wps, j))
    middle = x + attn
    mid_ref[0] = middle
    for row, field in enumerate((x, middle, attn)):
        acc_ref[row : row + 1, :] += jnp.sum(ok_col * field * field, 0, keepdims=True)
    normed2, _ = norm_parts(middle)
    h2 = (normed2 * vec(g2_ref) + vec(b2_ref)).astype(bf16)
    h2x_ref[step, :, 0:width] = h2
    logits = dot_nt(h2, wr_pad[...])
    logits = jnp.where(lane_iota(logits.shape) < experts, logits, MASKED)
    e = jnp.exp(logits - jnp.max(logits, -1, keepdims=True))
    prob = e / jnp.sum(e, -1, keepdims=True)
    high = prob.astype(bf16).astype(f32)
    h2x_ref[step, :, width:] = (high + pltpu.roll(prob - high, experts, 1)).astype(bf16)
    for k in range(1, cores):
        h_copy(step, k).start()

    @pl.when(step == own - 1)
    def _():
        for k in range(1, cores):
            for n in range(4, 7):
                weight_copy(n, k).wait()
            for i in range(own):
                h_copy(i, k).wait()

        def arrived(k, _):
            g_copy(k).wait()
            return 0

        lax.fori_loop(1, early_places(experts), arrived, 0)
        own_rows.wait()
        for copy in keeps:
            copy.wait()


def split_heads(value):
    low_half = lane_iota(value.shape) < HEAD_DIM
    zero = jnp.zeros_like(value)
    return jnp.concatenate([jnp.where(low_half, value, zero), jnp.where(low_half, zero, value)], 0)


def shares_of(own_ref, rest_ref):
    share = own_ref.shape[1]
    return [slice(share * j, share * (j + 1)) for j in range(rest_ref.shape[0] + 1)]


def add_parts(acc_ref, base, shares, value):
    rows = small_base(len(shares))
    which = lax.broadcasted_iota(i32, (rows, shares[0].stop), 0)
    for j, cols in enumerate(shares):
        owner = lax.rem(lax.axis_index("tensor") + j, len(shares))
        total = jnp.sum(value[:, cols].astype(f32), 0, keepdims=True)
        acc_ref[0:rows, shares[0]] += jnp.where(which == base + owner, total, 0.0)


def attn_bwd_a_kernel(
    dims, cot_ref, valid_ref, accf_ref, mid_ref, h2x_ref, h1_ref, probs_ref, heads_ref,
    moe_own, moe_ref, gmoe_own, gmoe_ref, gin_w, gin_ws, gout_w, gout_ws, g2_ref, wq, wp, wps, wr_ref,
    out_ref, gm_ref, gh_ref, dv_ref, grad_own, grad_rest, acc_ref, gw_in_ref, gw_out_ref,
    c_s, h1_s, heads_s, ga_s, dv_s
):
    seq, seq_pad, key_pad, own, experts = dims
    width = cot_ref.shape[1]
    step = pl.program_id(0)
    shares = shares_of(wq, wps)
    small_b = small_base(len(shares))
    image = lax.axis_index("tensor") * own + step
    at = pl.multiple_of(step * seq_pad, 16)
    c_s[seq // 8 * 8 :, :] = jnp.zeros((seq_pad - seq // 8 * 8, width), f32)
    read_image(c_s, cot_ref, image, seq)
    ok = valid_ref[0]

    @pl.when(step == 0)
    def _():
        acc_ref[...] = jnp.zeros_like(acc_ref)
        acc_ref[small_b : small_b + 8, :] = accf_ref[...]

    def add(row, value):
        acc_ref[row : row + 1, :] += jnp.sum(value, 0, keepdims=True)

    def total(own_ref, rest_ref, cols):
        value = own_ref[0, :, cols].astype(f32)
        for j in range(rest_ref.shape[0]):
            value = value + rest_ref[j, 0, :, cols].astype(f32)
        return value

    for sum_ref, own_ref, rest_ref in (
        (gw_in_ref, gin_w, gin_ws), (gw_out_ref, gout_w, gout_ws)
    ):
        value = own_ref[...].astype(f32)
        for j in range(rest_ref.shape[0]):
            value = value + rest_ref[j].astype(f32)
        sum_ref[0] = value
    middle = mid_ref[0]
    moe = total(moe_own, moe_ref, slice(0, width))
    output = middle + moe
    out_ref[0] = output
    add(0, ok * output * output)
    add(1, ok * moe * moe)
    h2 = h2x_ref[0, :, 0:width]
    pair = h2x_ref[0, :, width:].astype(f32)
    prob = jnp.where(
        lane_iota(pair.shape) < experts, pair + pltpu.roll(pair, LANES - experts, 1), 0.0
    )
    grad_probs = total(moe_own, moe_ref, slice(width, width + LANES))
    grad_logits = (
        prob * (grad_probs - jnp.sum(grad_probs * prob, -1, keepdims=True))
    ).astype(bf16)
    acc_ref[small_b + 8 : small_b + 8 + experts, :] += dot_tn(grad_logits, h2)[:experts]
    grad_h2 = dot(grad_logits, wr_ref[...]) + total(gmoe_own, gmoe_ref, slice(0, width))
    normed2, inv2 = norm_parts(middle)
    add(2, grad_h2 * normed2)
    add(3, grad_h2)
    add(7, jnp.broadcast_to(ok, grad_h2.shape))
    grad_middle = c_s[...] + norm_back(grad_h2, normed2, inv2, vec(g2_ref))
    gm_ref[0] = grad_middle
    grad_attn = grad_middle.astype(bf16)
    add(4, grad_attn.astype(f32))
    here = pl.ds(at, seq_pad)
    ga_s[here, :] = grad_attn
    heads_s[here, :] = heads_ref[0]
    h1_s[here, :] = h1_ref[0]
    for j, cols in enumerate(shares):
        gh_ref[0, :, cols] = dot_nt(grad_attn, piece(wp, wps, j)).astype(bf16)
    for p in range(width // LANES):
        cols = slice(LANES * p, LANES * (p + 1))
        gs = split_heads(gh_ref[0, :, cols])
        dv_s[here, cols] = dot_tn(probs_ref[0, p], gs)[:seq_pad].astype(bf16)
    dv = dv_s[here, :]
    dv_ref[0] = dv
    add_parts(acc_ref, 8 + len(shares), shares, dv)

    @pl.when(step == own - 1)
    def _():
        for n, (left, right) in enumerate(((ga_s, heads_s), (h1_s, dv_s))):
            rows = slice(width * n, width * (n + 1))
            grad = dot_tn(left[...], right[...])
            put_chunks(grad_own, grad_rest, rows, shares, grad)


def put_chunks(own_ref, rest_ref, rows, shares, grad):
    lanes = own_ref.shape[2]
    for j, cols in enumerate(shares):
        for c in range(own_ref.shape[0]):
            value = grad[:, cols.start + lanes * c : cols.start + lanes * (c + 1)]
            if j == 0:
                own_ref[c, rows, :] = value
            else:
                rest_ref[j - 1, c, rows, :] = value.astype(bf16)


def attn_bwd_b_kernel(
    dims, q_ref, k_ref, v_ref, probs_ref, gh_ref, first_own, first_rest, small_ref, g1_ref,
    wq, wqs, wk, wks, wv, wvs, x_hbm, gm_hbm, dv_hbm, h1_hbm, out_hbm,
    low_hbm, small_hbm, gin_ref, outs_ref, gins_ref,
    low, small_out, dq_s, dk_s, x_s, gm_s, dv_s, h1_s, rest_out, rest_s, acc, send_s, recv_s,
    small_a, small_r, small_m, small_s, small_t,
    load_sem, t_send, t_recv, x_send, x_recv, st_send, st_recv, sx_send, sx_recv, sg_send, sg_recv,
    o_send, o_recv, i_send, i_recv
):
    seq, seq_pad, key_pad, own, _ = dims
    width = q_ref.shape[2]
    step = pl.program_id(0)
    shares = shares_of(wq, wqs)
    at = pl.multiple_of(step * seq_pad, 16)
    here = pl.ds(at, seq_pad)
    experts, _ = around("expert")
    cores, core = around("tensor")
    me_e = lax.axis_index("expert")
    me_t = lax.axis_index("tensor")
    bits = experts.bit_length() - 1
    chunks, rows, _ = acc.shape[1:]
    piece_rows = small_r.shape[1]
    low_half = lane_iota((seq_pad, LANES)) < HEAD_DIM

    def my_bit(b):
        return lax.rem(me_e // (1 << b), 2)

    def partner(b):
        return {"expert": me_e + (1 << b) * (1 - 2 * my_bit(b))}

    def remote(src, dst, send, recv, there):
        return pltpu.make_async_remote_copy(
            src_ref=src, dst_ref=dst, send_sem=send, recv_sem=recv,
            device_id=there, device_id_type=MESH,
        )

    orders = []
    for c in range(chunks):
        order = list(range(bits))
        if c == 1:
            order = [1, 0] + order[2:]
        elif c == 2:
            order = order[2:] + order[:2]
        orders.append(order)

    def base_at(c, s):
        value = 0
        for n in range(s):
            value = value + my_bit(orders[c][n]) * (rows >> (n + 1))
        return value

    def inner(phase, c, k):
        source = first_rest if phase == 0 else rest_out
        return remote(
            source.at[k - 1, c], rest_s.at[phase, k - 1, c],
            t_send.at[phase, k - 1, c], t_recv.at[phase, k - 1, c], core(k),
        )

    def across(phase, c, s):
        sems = (x_send.at[phase, c, s], x_recv.at[phase, c, s])
        if s < bits:
            half = rows >> (s + 1)
            box = slice(rows - 2 * half, rows - half)
            return remote(
                send_s.at[phase, c, box, :], recv_s.at[phase, c, box, :], *sems,
                partner(orders[c][s]),
            )
        size = rows >> (2 * bits - s)
        mine = pl.ds(pl.multiple_of(base_at(c, 2 * bits - s), 16), size)
        return remote(
            low.at[phase, c, mine, :], low.at[phase, c, mine, :], *sems,
            partner(orders[c][2 * bits - 1 - s]),
        )

    def send_stage(phase, c, s):
        if s < bits:
            half = rows >> (s + 1)
            away = pl.ds(
                pl.multiple_of(base_at(c, s) + (1 - my_bit(orders[c][s])) * half, 16), half
            )
            send_s[phase, c, rows - 2 * half : rows - half, :] = acc[phase, c, away, :].astype(bf16)
        elif s == bits:
            mine = pl.ds(pl.multiple_of(base_at(c, bits), 16), rows >> bits)
            low[phase, c, mine, :] = acc[phase, c, mine, :].astype(bf16)
        across(phase, c, s).start()

    def end_stage(phase, c, s):
        across(phase, c, s).wait()
        if s < bits:
            half = rows >> (s + 1)
            keep = pl.ds(pl.multiple_of(base_at(c, s + 1), 16), half)
            acc[phase, c, keep, :] += recv_s[phase, c, rows - 2 * half : rows - half, :].astype(f32)

    def point(phase, s):
        for c in range(chunks):
            if s == 0:
                for k in range(1, cores):
                    inner(phase, c, k).wait()
                value = first_own[c] if phase == 0 else acc[phase, c]
                for k in range(cores - 1):
                    value = value + rest_s[phase, k, c].astype(f32)
                acc[phase, c] = value
            else:
                end_stage(phase, c, s - 1)
            if s < 2 * bits:
                send_stage(phase, c, s)

    def out_copy(k):
        return remote(out_hbm, outs_ref.at[k - 1], o_send.at[k - 1], o_recv.at[k - 1], core(k))

    def gin_copy(i, k):
        return remote(
            gin_ref.at[i], gins_ref.at[k - 1, i], i_send.at[i, k - 1], i_recv.at[i, k - 1], core(k)
        )

    loads = [
        pltpu.make_async_copy(src, dst, load_sem.at[n])
        for n, (src, dst) in enumerate(
            ((x_hbm, x_s), (gm_hbm, gm_s), (dv_hbm, dv_s), (h1_hbm, h1_s))
        )
    ]

    @pl.when(step == 0)
    def _():
        peers = [partner(b) for b in range(bits)] + [core(k) for k in range(1, cores)]
        greet_start(peers)
        for copy in loads:
            copy.start()
        greet_end(peers)
        for c in range(chunks):
            for k in range(1, cores):
                inner(0, c, k).start()

    pairs = width // LANES
    points = {}
    hidden_points = 2
    for n in range(hidden_points):
        turn = 4 + (n * (own * pairs - 5)) // max(hidden_points - 1, 1)
        points.setdefault((turn // pairs, turn % pairs), []).append(n)

    for p in range(pairs):
        cols = slice(LANES * p, LANES * (p + 1))
        gs = split_heads(gh_ref[0, :, cols])
        qs = split_heads(q_ref[0, :, cols])
        weights = probs_ref[0, p].astype(f32)
        mixed = weights * dot_nt(gs, v_ref[0, :, cols])
        ds = (
            (mixed - weights * jnp.sum(mixed, -1, keepdims=True)) * (HEAD_DIM**-0.5)
        ).astype(bf16)
        dq = dot(ds, k_ref[0, :, cols])
        dq_s[here, cols] = jnp.where(low_half, dq[:seq_pad], dq[seq_pad:]).astype(bf16)
        dk_s[here, cols] = dot_tn(ds, qs)[:seq_pad].astype(bf16)
        for i in range(own):
            if (i, p) in points:

                @pl.when(step == i)
                def _(i=i, p=p):
                    for n in points[i, p]:
                        point(0, n)
                        if n == 0:
                            for k in range(1, cores):
                                out_copy(k).start()

    @pl.when(step == own - 1)
    def _():
        for copy in loads:
            copy.wait()
        for n, part in enumerate((dq_s, dk_s)):
            box = slice(width * n, width * (n + 1))
            grad = dot_tn(h1_s[...].reshape(own * seq_pad, width), part[...])
            put_chunks(acc.at[1], rest_out, box, shares, grad)
        for c in range(chunks):
            for k in range(1, cores):
                inner(1, c, k).start()
        small_a[...] = small_ref[...]
        add_parts(small_a, 8, shares, dq_s[...])

        def first_norm(i):
            box = slice(seq_pad * i, seq_pad * (i + 1))
            grad_h1 = None
            for j, cols in enumerate(shares):
                for left, own_ref, rest_ref in (
                    (dq_s[box, cols], wq, wqs), (dk_s[box, cols], wk, wks), (dv_s[i, :, cols], wv, wvs)
                ):
                    term = dot_nt(left, piece(own_ref, rest_ref, j))
                    grad_h1 = term if grad_h1 is None else grad_h1 + term
            normed1, inv1 = norm_parts(x_s[i])
            for row, value in ((5, grad_h1 * normed1), (6, grad_h1)):
                small_a[row : row + 1, :] += jnp.sum(value, 0, keepdims=True)
            gin_ref[i] = gm_s[i] + norm_back(grad_h1, normed1, inv1, vec(g1_ref))
            for k in range(1, cores):
                gin_copy(i, k).start()

        def small_piece(k):
            mine = pl.ds(
                pl.multiple_of(lax.rem(me_t + k, cores) * piece_rows, 8), piece_rows
            )
            return remote(
                small_a.at[mine, :], small_r.at[k - 1], st_send.at[k - 1], st_recv.at[k - 1], core(k)
            )

        def small_across(n):
            return remote(small_s.at[n], small_t.at[n], sx_send.at[n], sx_recv.at[n], partner(n))

        mine = pl.ds(pl.multiple_of(me_t * piece_rows, 8), piece_rows)

        def small_back(k):
            return remote(
                small_m, small_out.at[mine, :], sg_send.at[k - 1], sg_recv.at[k - 1], core(k)
            )

        def small_point(n):
            if n == 0:
                for k in range(1, cores):
                    small_piece(k).wait()
                total = small_a[mine, :]
                for k in range(cores - 1):
                    total = total + small_r[k]
                small_m[...] = total
            else:
                small_across(n - 1).wait()
                small_m[...] += small_t[n - 1]
            if n < bits:
                small_s[n] = small_m[...]
                small_across(n).start()
            else:
                small_out[mine, :] = small_m[...]
                for k in range(1, cores):
                    small_back(k).start()

        older = list(range(hidden_points, 2 * bits + 1))
        newer = list(range(2 * bits + 1))
        norms = list(range(own))
        smalls = []
        while older or newer or norms or smalls:
            if norms:
                first_norm(norms.pop(0))
                if not norms:
                    for k in range(1, cores):
                        small_piece(k).start()
                    smalls = list(range(bits + 1))
            elif smalls:
                small_point(smalls.pop(0))
            if older:
                point(0, older.pop(0))
            if newer:
                point(1, newer.pop(0))
        keeps = [pltpu.make_async_copy(low, low_hbm, load_sem.at[0])]
        keeps[0].start()
        for k in range(1, cores):
            small_back(k).wait()
        keeps.append(pltpu.make_async_copy(small_out, small_hbm, load_sem.at[1]))
        keeps[1].start()
        for k in range(1, cores):
            out_copy(k).wait()
            for i in range(own):
                gin_copy(i, k).wait()
        for copy in keeps:
            copy.wait()


def small_base(cores):
    return up(8 + 2 * cores, 8)


def view(own_ref, rest_ref, j):
    return own_ref if j == 0 else rest_ref.at[j - 1]


def chunk_of(hidden):
    for size in (512, 384, 256, 128):
        if hidden % size == 0:
            return size
    return hidden


def greet_start(peers):
    barrier = pltpu.get_barrier_semaphore()
    for peer in peers:
        pl.semaphore_signal(barrier, inc=1, device_id=peer, device_id_type=MESH)


def greet_end(peers):
    pl.semaphore_wait(pltpu.get_barrier_semaphore(), len(peers))


def early_places(experts):
    return experts


def chip_at(place, experts):
    me = lax.axis_index("expert")
    flips = place // 2 + lax.rem(place, 2) * (experts // 2)
    there = me
    for b in range(experts.bit_length() - 1):
        bit = 1 << b
        there = there + lax.rem(flips // bit, 2) * bit * (1 - 2 * lax.rem(me // bit, 2))
    return there


def around(axis):
    n = lax.axis_size(axis)
    me = lax.axis_index(axis)
    return n, lambda k: {axis: lax.rem(me + n + k, n)}


def moe_kernel(
    h2x_ref, h2x_rest, post_ref, grow_hbm, sent_hbm, fidx_ref, w_in, w_ins, b_in, b_ins, w_out, w_outs,
    b_out_ref,
    back_ref, gback_ref, gin_own, gout_own, gin_rest, gout_rest,
    gbin_own, gbin_rest, gbout_ref, moe_own, moe_rest, gmoe_own, gmoe_rest,
    table, out_s, rows_s, grow_s, res_s, gate_out, gate_in, gslot_ref,
    gbin_send, gbout_send,
    m_send, m_recv, load_sem, local_sem, h_send, h_recv, c_send, c_recv, r_send, r_recv, g_send, g_recv,
    l_send, l_recv, w_send, w_recv, own_sem
):
    experts, chip = around("expert")
    cores, core = around("tensor")
    me_e = lax.axis_index("expert")
    me_t = lax.axis_index("tensor")
    cap_dev, width = rows_s.shape[1:]
    group = table.shape[1]
    share = w_in.shape[1]
    size = chunk_of(share)
    per = share // size
    peers = [chip(k) for k in range(1, experts)] + [core(k) for k in range(1, cores)]
    greet_start(peers)

    def remote(src, dst, send, recv, there):
        return pltpu.make_async_remote_copy(
            src_ref=src, dst_ref=dst, send_sem=send, recv_sem=recv,
            device_id=there, device_id_type=MESH,
        )

    early = early_places(experts)
    grow_copy = pltpu.make_async_copy(grow_hbm, grow_s.at[0:early], local_sem.at[0])
    grow_copy.start()
    fills = [
        pltpu.make_async_copy(
            h2x_ref if k == 0 else h2x_rest.at[k - 1],
            table.at[lax.rem(me_t + k, cores)], local_sem.at[1 + k],
        )
        for k in range(cores)
    ]
    for copy in fills:
        copy.start()
    for copy in fills:
        copy.wait()
    greet_end(peers)

    slots = lax.broadcasted_iota(i32, (cap_dev, group), 0).astype(f32)
    lanes = lane_iota((cap_dev, LANES))

    def select(k):
        e = chip_at(k, experts)
        total = None
        for j in range(cores):
            pick = jnp.where(post_ref[j, e] == slots, 1.0, 0.0).astype(bf16)
            term = dot(pick, table[j])
            total = term if total is None else total + term
        mine = (lanes == e) | (lanes == e + experts)
        gate = jnp.sum(jnp.where(mine, total[:, width:], 0.0), 1, keepdims=True)
        gslot_ref[pl.ds(pl.multiple_of(cap_dev * k, 8), cap_dev), :] = gate
        spread = jnp.transpose(jnp.broadcast_to(gate, (cap_dev, LANES)), (1, 0))
        return total[:, :width].astype(bf16), spread[0:8]

    def h_copy(k):
        there = {"expert": chip_at(k, experts)}
        return remote(out_s.at[k], rows_s.at[k], h_send.at[k], h_recv.at[k], there)

    def c_copy(k):
        there = {"expert": chip_at(k, experts)}
        return remote(gate_out.at[k], gate_in.at[k], c_send.at[k], c_recv.at[k], there)

    def r_copy(k):
        there = {"expert": chip_at(k, experts)}
        return remote(res_s.at[k], back_ref.at[k], r_send.at[k], r_recv.at[k], there)

    def g_copy(k):
        there = {"expert": chip_at(k, experts)}
        return remote(out_s.at[k], gback_ref.at[k], g_send.at[k], g_recv.at[k], there)

    def send_rows(j, _):
        k = lax.rem(j + 1, experts)
        rows, gate = select(k)
        out_s[k] = rows
        gate_out[k] = gate

        @pl.when(k > 0)
        def _():
            h_copy(k).start()
            c_copy(k).start()

        return 0

    def l_copy(k):
        there = {"expert": chip_at(k, experts)}
        return remote(sent_hbm.at[k], grow_s.at[k], l_send.at[k], l_recv.at[k], there)

    def send_late(k, _):
        l_copy(k).start()
        return 0

    lax.fori_loop(0, experts, send_rows, 0)
    lax.fori_loop(early, experts, send_late, 0)
    rows_s[0] = out_s[0]
    gate_in[0] = gate_out[0]
    pl.run_scoped(
        functools.partial(
            expert_phase, locals_of(
                experts=experts, cores=cores, core=core, me_t=me_t, width=width, cap_dev=cap_dev,
                share=share, size=size, per=per, w_in=w_in, w_ins=w_ins, b_in=b_in, b_ins=b_ins,
                w_out=w_out, w_outs=w_outs, b_out_ref=b_out_ref, rows_s=rows_s, res_s=res_s,
                back_ref=back_ref, own_sem=own_sem, h_copy=h_copy, r_copy=r_copy, c_copy=c_copy,
                g_copy=g_copy, grow_copy=grow_copy, grow_s=grow_s, out_s=out_s,
                gback_ref=gback_ref, gate_in=gate_in, gbout_send=gbout_send, gbout_ref=gbout_ref,
                gbin_own=gbin_own, gbin_send=gbin_send, gbin_rest=gbin_rest, gin_own=gin_own,
                gout_own=gout_own, gin_rest=gin_rest, gout_rest=gout_rest, w_send=w_send,
                w_recv=w_recv, remote=remote, l_copy=l_copy, early=early,
            ),
        ),
        pltpu.VMEM((experts * cap_dev, share * cores), bf16),
        pltpu.VMEM((experts * cap_dev, share * cores), bf16),
        pltpu.VMEM((2, width, size), bf16),
        pltpu.VMEM((2, size, width), bf16),
    )
    rows_all = experts * cap_dev
    wide = width + LANES

    def token_phase(picks, values, total):
        loads = [
            pltpu.make_async_copy(sent_hbm, grow_s, load_sem.at[0]),
            pltpu.make_async_copy(back_ref, rows_s, load_sem.at[1]),
        ]
        loads[0].start()

        def arrived(k, _):
            r_copy(k).wait()
            return 0

        lax.fori_loop(1, experts, arrived, 0)
        loads[1].start()
        step = 208 if group % 208 == 0 else group
        tiles = group // step
        slot_lanes = lane_iota((step, rows_all))

        def make_picks(i, _):
            tok = pl.ds(pl.multiple_of(i * step, 16), step)
            hit = (fidx_ref[tok, 0:1] == slot_lanes) | (fidx_ref[tok, 1:2] == slot_lanes)
            picks[tok, :] = jnp.where(hit, 1.0, 0.0).astype(bf16)
            return 0

        lax.fori_loop(0, cores * tiles, make_picks, 0)
        for copy in loads:
            copy.wait()

        def gated(k):
            return gslot_ref[pl.ds(pl.multiple_of(cap_dev * k, 8), cap_dev), :]

        def weigh(k, _):
            rows = rows_s[k].astype(f32)
            dots = jnp.sum(rows * grow_s[k].astype(f32), 1, keepdims=True)
            here = pl.ds(pl.multiple_of(cap_dev * k, 16), cap_dev)
            values[here, 0:width] = (rows * gated(k)).astype(bf16)
            mine = lanes == chip_at(k, experts)
            values[here, width:] = jnp.where(mine, dots, 0.0).astype(bf16)
            return 0

        lax.fori_loop(0, experts, weigh, 0)

        def m_copy(kind, k):
            source = table.at[k] if kind == 0 else table.at[k, :, 0:width]
            return remote(
                source, (moe_rest, gmoe_rest)[kind].at[k - 1],
                m_send.at[kind, k - 1], m_recv.at[kind, k - 1], core(k),
            )

        keep_moe = pltpu.make_async_copy(table.at[0], moe_own, load_sem.at[0])
        keep_gmoe = pltpu.make_async_copy(table.at[0, :, 0:width], gmoe_own, load_sem.at[0])

        for k in list(range(1, cores)) + [0]:

            def sums(i, _, k=k):
                tok = pl.ds(
                    pl.multiple_of(lax.rem(me_t + k, cores) * group + i * step, 16), step
                )
                to = pl.ds(pl.multiple_of(i * step, 16), step)
                table[k, to, :] = dot(picks[tok, :], values[...]).astype(bf16)
                return 0

            lax.fori_loop(0, tiles, sums, 0)
            if k > 0:
                m_copy(0, k).start()
        keep_moe.start()
        keep_moe.wait()
        for k in range(1, cores):
            m_copy(0, k).wait()

        batch = 4
        batches = experts // batch
        for b in range(batches):
            first = b * batch
            for k in range(first, first + batch):
                if k > 0:
                    g_copy(k).wait_recv()
                else:
                    own_grad.wait()
            box = pl.ds(first, batch)
            load = pltpu.make_async_copy(gback_ref.at[box], rows_s.at[box], load_sem.at[0])
            load.start()
            load.wait()
            cols = slice(cap_dev * first, cap_dev * (first + batch))
            for k in range(first, first + batch):
                rows_s[k] = (rows_s[k].astype(f32) * gated(k)).astype(bf16)
            for k in list(range(1, cores)) + [0]:

                def gsums(i, _, k=k, b=b, cols=cols, box=box):
                    tok = pl.ds(
                        pl.multiple_of(lax.rem(me_t + k, cores) * group + i * step, 16), step
                    )
                    to = pl.ds(pl.multiple_of(i * step, 16), step)
                    rows = rows_s[box].reshape(batch * cap_dev, width)
                    value = dot(picks[tok, cols], rows)
                    if b > 0:
                        value = value + total[tok, :]
                    if b < batches - 1:
                        total[tok, :] = value
                    else:
                        table[k, to, 0:width] = value.astype(bf16)
                    return 0

                lax.fori_loop(0, tiles, gsums, 0)
                if b == batches - 1 and k > 0:
                    m_copy(1, k).start()
        keep_gmoe.start()
        keep_gmoe.wait()
        for k in range(1, cores):
            m_copy(1, k).wait()

        def finish(k, _):
            g_copy(k).wait_send()
            return 0

        lax.fori_loop(1, experts, finish, 0)

    own_grad = pltpu.make_async_copy(out_s.at[0], gback_ref.at[0], own_sem.at[1])
    pl.run_scoped(
        token_phase,
        pltpu.VMEM((cores * group, rows_all), bf16),
        pltpu.VMEM((rows_all, wide), bf16),
        pltpu.VMEM((cores * group, width), f32),
    )


class Bag:
    pass


def locals_of(**names):
    bag = Bag()
    bag.__dict__.update(names)
    return bag


def expert_phase(at, hid, slope, stage_in, stage_out):
    experts, cores, core, me_t, width, cap_dev = (
        at.experts, at.cores, at.core, at.me_t, at.width, at.cap_dev
    )
    share, size, per, remote = at.share, at.size, at.per, at.remote
    w_in, w_ins, b_in, b_ins, w_out, w_outs = at.w_in, at.w_ins, at.b_in, at.b_ins, at.w_out, at.w_outs
    b_out_ref, rows_s, res_s, back_ref, own_sem = at.b_out_ref, at.rows_s, at.res_s, at.back_ref, at.own_sem
    h_copy, r_copy, c_copy, g_copy, grow_copy = at.h_copy, at.r_copy, at.c_copy, at.g_copy, at.grow_copy
    grow_s, out_s, gback_ref, gate_in = at.grow_s, at.out_s, at.gback_ref, at.gate_in
    gbout_send, gbout_ref, gbin_own, gbin_send, gbin_rest = (
        at.gbout_send, at.gbout_ref, at.gbin_own, at.gbin_send, at.gbin_rest
    )
    gin_own, gout_own, gin_rest, gout_rest = at.gin_own, at.gout_own, at.gin_rest, at.gout_rest
    w_send, w_recv = at.w_send, at.w_recv

    def forward(i):
        x = rows_s[pl.ds(2 * i, 2)].reshape(2 * cap_dev, width)
        here = pl.ds(pl.multiple_of(2 * cap_dev * i, 16), 2 * cap_dev)
        total = None
        for j in range(cores):
            for n in range(per):
                cols = slice(size * n, size * (n + 1))
                flat = slice(share * j + size * n, share * j + size * (n + 1))
                pre = dot(x, view(w_in, w_ins, j)[:, cols]) + view(b_in, b_ins, j)[:, cols]
                act, steep = gelu_parts(pre)
                act = act.astype(bf16)
                hid[here, flat] = act
                slope[here, flat] = steep.astype(bf16)
                term = dot(act, view(w_out, w_outs, j)[cols, :])
                total = term if total is None else total + term
        res = (total + b_out_ref[...]).astype(bf16)
        res_s[pl.ds(2 * i, 2)] = res.reshape(2, cap_dev, width)

    own_res = pltpu.make_async_copy(res_s.at[0], back_ref.at[0], own_sem.at[0])

    def forward_step(i, _):

        @pl.when(i > 0)
        def _():
            h_copy(2 * i).wait_recv()

        h_copy(2 * i + 1).wait_recv()
        forward(i)

        @pl.when(i > 0)
        def _():
            r_copy(2 * i).start()

        @pl.when(i == 0)
        def _():
            own_res.start()

        r_copy(2 * i + 1).start()
        return 0

    lax.fori_loop(0, experts // 2, forward_step, 0)

    def sent_rows(k, _):
        h_copy(k).wait_send()
        return 0

    lax.fori_loop(1, experts, sent_rows, 0)
    grow_copy.wait()

    def late_rows(k, _):
        at.l_copy(k).wait()
        return 0

    lax.fori_loop(at.early, experts, late_rows, 0)

    def backward(i):
        g = grow_s[pl.ds(2 * i, 2)].reshape(2 * cap_dev, width)
        here = pl.ds(pl.multiple_of(2 * cap_dev * i, 16), 2 * cap_dev)
        total = None
        for j in range(cores):
            for n in range(per):
                cols = slice(size * n, size * (n + 1))
                flat = slice(share * j + size * n, share * j + size * (n + 1))
                grad = dot_nt(g, view(w_out, w_outs, j)[cols, :])
                gpre = (grad * slope[here, flat].astype(f32)).astype(bf16)
                slope[here, flat] = gpre
                term = dot_nt(gpre, view(w_in, w_ins, j)[:, cols])
                total = term if total is None else total + term
        out_s[pl.ds(2 * i, 2)] = total.astype(bf16).reshape(2, cap_dev, width)

    own_grad = pltpu.make_async_copy(out_s.at[0], gback_ref.at[0], own_sem.at[1])

    def backward_step(i, _):
        backward(i)

        @pl.when(i > 0)
        def _():
            g_copy(2 * i).start()

        @pl.when(i == 0)
        def _():
            own_grad.start()

        g_copy(2 * i + 1).start()
        return 0

    lax.fori_loop(0, experts // 2, backward_step, 0)

    def gates_in(k, _):
        c_copy(k).wait()
        return 0

    lax.fori_loop(1, experts, gates_in, 0)

    def scale_rows(k, total):
        square = jnp.broadcast_to(gate_in[k, 0:1, :], (LANES, cap_dev))
        gate = jnp.transpose(square, (1, 0))[:, 0:1]
        rows_s[k] = (rows_s[k].astype(f32) * gate).astype(bf16)
        scaled = (grow_s[k].astype(f32) * gate).astype(bf16)
        grow_s[k] = scaled
        return total + jnp.sum(scaled.astype(f32), 0, keepdims=True)

    bias = lax.fori_loop(0, experts, scale_rows, jnp.zeros((1, width), f32))
    gbout_send[...] = jnp.broadcast_to(bias, gbout_send.shape)
    gbout_ref[me_t] = jnp.broadcast_to(bias, gbout_send.shape)
    rows_all = experts * cap_dev

    def grads(col):
        cols = pl.ds(pl.multiple_of(col, LANES), size)
        left = rows_s[...].reshape(rows_all, width)
        right = grow_s[...].reshape(rows_all, width)
        return dot_tn(left, slope[:, cols]), dot_tn(hid[:, cols], right)

    def column_sums(col):
        cols = pl.ds(pl.multiple_of(col, LANES), size)
        total = jnp.zeros((1, size), f32)
        for k in range(experts):
            square = jnp.broadcast_to(gate_in[k, 0:1, :], (LANES, cap_dev))
            gate = jnp.transpose(square, (1, 0))[:, 0:1]
            here = slice(cap_dev * k, cap_dev * (k + 1))
            total = total + jnp.sum(slope[here, cols].astype(f32) * gate, 0, keepdims=True)
        return total

    pending = []
    for j in list(range(1, cores)) + [0]:
        for n in range(per):
            cols = slice(size * n, size * (n + 1))
            slot = len(pending) % 2
            if len(pending) >= 2:
                for wait in pending[-2]:
                    wait()
            gw_in, gw_out = grads(share * j + size * n)
            stage_in[slot] = gw_in.astype(bf16)
            stage_out[slot] = gw_out.astype(bf16)
            sums = column_sums(share * j + size * n)
            if j == 0:
                gbin_own[:, cols] = sums
                a = pltpu.make_async_copy(stage_in.at[slot], gin_own.at[:, cols], own_sem.at[2 + slot])
                b = pltpu.make_async_copy(stage_out.at[slot], gout_own.at[cols, :], own_sem.at[4 + slot])
                a.start()
                b.start()
                pending.append((a.wait, b.wait))
            else:
                gbin_send[j - 1, :, cols] = sums
                at = (j - 1) * per + n
                a = remote(
                    stage_in.at[slot], gin_rest.at[j - 1, :, cols],
                    w_send.at[0, at], w_recv.at[0, at], core(j),
                )
                b = remote(
                    stage_out.at[slot], gout_rest.at[j - 1, cols, :],
                    w_send.at[1, at], w_recv.at[1, at], core(j),
                )
                a.start()
                b.start()
                pending.append((a.wait_send, b.wait_send))
        if j != 0:
            tail = [
                remote(
                    gbin_send.at[j - 1], gbin_rest.at[j - 1],
                    w_send.at[2, j - 1], w_recv.at[2, j - 1], core(j),
                ),
                remote(
                    gbout_send, gbout_ref.at[me_t],
                    w_send.at[3, j - 1], w_recv.at[3, j - 1], core(j),
                ),
            ]
            for copy in tail:
                copy.start()
    for waits in pending[-2:]:
        for wait in waits:
            wait()
    for j in range(1, cores):
        for n in range(per):
            cols = slice(size * n, size * (n + 1))
            at = (j - 1) * per + n
            remote(
                stage_in.at[0], gin_rest.at[j - 1, :, cols],
                w_send.at[0, at], w_recv.at[0, at], core(j),
            ).wait_recv()
            remote(
                stage_out.at[0], gout_rest.at[j - 1, cols, :],
                w_send.at[1, at], w_recv.at[1, at], core(j),
            ).wait_recv()
        remote(
            gbin_send.at[j - 1], gbin_rest.at[j - 1],
            w_send.at[2, j - 1], w_recv.at[2, j - 1], core(j),
        ).wait()
        remote(
            gbout_send, gbout_ref.at[me_t], w_send.at[3, j - 1], w_recv.at[3, j - 1], core(j)
        ).wait()

    own_res.wait()


def finish_kernel(
    seq, low_ref, small_ref, gbin_own, gbin_rest, gbout_ref, out_own, out_rest, gin_own, gin_rest,
    out_hbm, gin_hbm, gq_hbm, gk_hbm, gv_hbm, gwp_hbm, gl1, bl1, gbq, gbv, gbp, gl2, bl2, grout,
    gbin, gbout, rms,
    out_s, gin_s, parts_s, gq, gk, gv, gwp, in_sem, to_sem, g_sem
):
    cores, own, seq_pad, width = (out_rest.shape[0] + 1,) + out_rest.shape[1:]
    me_t = lax.axis_index("tensor")
    images = cores * own
    share = gbq.shape[0]
    experts = grout.shape[0]
    jobs = []
    for n, (mine, rest, full, hbm) in enumerate(
        ((out_own, out_rest, out_s, out_hbm), (gin_own, gin_rest, gin_s, gin_hbm))
    ):
        jobs.append((n, mine, rest, full, hbm))
    rows_all = images * seq

    def incoming(n, p, i):
        _, mine, rest, _, _ = jobs[n]
        src = mine.at[i] if p == 0 else rest.at[p - 1, i]
        return pltpu.make_async_copy(src, parts_s.at[n, p, i], in_sem.at[n, p, i])

    for n in range(2):
        for p in range(cores):
            for i in range(own):
                incoming(n, p, i).start()
    lanes = low_ref.shape[3]
    for c in range(low_ref.shape[1]):
        cols = slice(lanes * c, lanes * (c + 1))
        for grad, phase, n in ((gv, 0, 1), (gq, 1, 0), (gk, 1, 1)):
            grad[:, cols] = low_ref[phase, c, width * n : width * (n + 1), :].astype(f32)
        gwp[cols, :] = jnp.transpose(low_ref[0, c, 0:width, :].astype(f32), (1, 0))
    grads = [
        pltpu.make_async_copy(src, dst, g_sem.at[n])
        for n, (src, dst) in enumerate(((gq, gq_hbm), (gk, gk_hbm), (gv, gv_hbm), (gwp, gwp_hbm)))
    ]
    for copy in grads:
        copy.start()

    def place(c):
        for n, mine, rest, full, hbm in jobs:
            done = 0
            for im in range(images):
                p = (im // own - c) % cores
                incoming(n, p, im % own).wait()
                src = parts_s.at[n, p, im % own]
                full[seq * im : seq * (im + 1), :] = src[0:seq, :]
                upto = rows_all if im == images - 1 else seq * (im + 1) // 8 * 8
                pltpu.make_async_copy(
                    full.at[done:upto, :], hbm.at[done:upto, :], to_sem.at[n, im]
                ).start()
                done = upto

    for c in range(cores):

        @pl.when(me_t == c)
        def _(c=c):
            place(c)

    base = small_base(cores)
    for dst, row in ((gl1, 5), (bl1, 6), (gbp, 4), (gl2, 2), (bl2, 3)):
        dst[...] = small_ref[row]
    which = lax.broadcasted_iota(i32, (base, share), 0)
    for dst, row in ((gbq, 8), (gbv, 8 + cores)):
        dst[...] = jnp.sum(jnp.where(which == row + me_t, small_ref[0:base, 0:share], 0.0), 0)
    grout[...] = small_ref[base + 8 : base + 8 + experts, :]
    value = gbin_own[...]
    for k in range(cores - 1):
        value = value + gbin_rest[k]
    gbin[...] = value
    value = gbout_ref[0, 0:1, :]
    for k in range(1, cores):
        value = value + gbout_ref[k, 0:1, :]
    gbout[...] = value
    count = small_ref[7:8, 0:1] * width
    lanes = lane_iota((1, LANES))
    value = jnp.zeros((1, LANES), f32)
    for n, row in enumerate((base, base + 1, 0, base + 2, 1)):
        square = jnp.sum(small_ref[row : row + 1, :], 1, keepdims=True)
        value = jnp.where(lanes == n, jnp.sqrt(square / count), value)
    rms[...] = value[0, 0:5]
    for copy in grads:
        copy.wait()
    done = [0] * 2
    for im in range(images):
        upto = rows_all if im == images - 1 else seq * (im + 1) // 8 * 8
        for n, mine, rest, full, hbm in jobs:
            pltpu.make_async_copy(
                full.at[done[n] : upto, :], hbm.at[done[n] : upto, :], to_sem.at[n, im]
            ).wait()
            done[n] = upto


def on_device(
    tokens_in, valid, routes, ln1_gain, ln1_bias, w_query, w_key, w_value, b_query, b_value,
    w_proj, b_proj, ln2_gain, ln2_bias, w_router, w_in, b_in, w_out, b_out, cotangent,
):
    tok_rows, width = tokens_in.shape
    images, seq = valid.shape
    experts = lax.axis_size("expert")
    cores = lax.axis_size("tensor")
    core = lax.axis_index("tensor")
    capacity = (10 * tok_rows // (4 * experts) // 8 + 1) * 8
    cap_dev = up(up(capacity, cores) // cores, 16)
    rows_all = experts * cap_dev
    seq_pad = up(seq, 16)
    key_pad = up(seq_pad, LANES)
    own = images // cores
    tok_own = own * seq
    tok_pad = images * seq_pad
    pad_own = own * seq_pad
    share = w_in.shape[2]
    hidden = share * cores
    wide = width + LANES
    pairs = width // LANES
    S = jax.ShapeDtypeStruct

    dims = (seq, seq_pad, key_pad, own, experts)

    def per_image(*shape):
        return pl.BlockSpec((1,) + shape, lambda i: (i,) + (0,) * len(shape))

    anywhere = pl.BlockSpec(memory_space=pl.ANY)
    inside = pl.BlockSpec(memory_space=pltpu.VMEM)
    block = (experts, cap_dev, width)
    DMA = pltpu.SemaphoreType.DMA
    (
        h1, q, k, v, probs, heads, middle, valid_col, x_pad, h2x, acc_f, send_g, post, fidx,
        wr, wqs, wks, wvs, wps, grow, h2x_rest, w_ins, w_outs, b_ins,
    ) = pl.pallas_call(
        functools.partial(attn_fwd_kernel, (images, seq, seq_pad, key_pad, own, cap_dev)),
        grid=(own,),
        in_specs=[
            *[
                whole(a.shape)
                for a in (
                    tokens_in, cotangent, valid, routes.T, ln1_gain, ln1_bias, w_query, w_key,
                    w_value, w_proj, b_query, b_value, b_proj, ln2_gain, ln2_bias, w_router.T,
                )
            ],
            *[anywhere] * 3,
        ],
        out_specs=[
            per_image(seq_pad, width),
            per_image(seq_pad, width),
            per_image(key_pad, width),
            per_image(key_pad, width),
            per_image(pairs, 2 * seq_pad, key_pad),
            per_image(seq_pad, width),
            per_image(seq_pad, width),
            per_image(seq_pad, 1),
            per_image(seq_pad, width),
            whole((own, seq_pad, wide)),
            whole((8, width)),
            whole(block),
            whole((cores, experts, 1, pad_own)),
            whole((tok_pad, 2)),
            whole((LANES, width)),
            *[anywhere] * 9,
        ],
        out_shape=[
            S((own, seq_pad, width), bf16),
            S((own, seq_pad, width), bf16),
            S((own, key_pad, width), bf16),
            S((own, key_pad, width), bf16),
            S((own, pairs, 2 * seq_pad, key_pad), bf16),
            S((own, seq_pad, width), bf16),
            S((own, seq_pad, width), f32),
            S((own, seq_pad, 1), f32),
            S((own, seq_pad, width), f32),
            S((own, seq_pad, wide), bf16),
            S((8, width), f32),
            S(block, bf16),
            S((cores, experts, 1, pad_own), f32),
            S((tok_pad, 2), i32),
            S((LANES, width), bf16),
            *[S((cores - 1,) + w.shape, bf16) for w in (w_query, w_key, w_value, w_proj)],
            S((early_places(experts), cap_dev, width), bf16),
            S((cores - 1, own, seq_pad, wide), bf16),
            S((cores - 1, width, share), bf16),
            S((cores - 1, share, width), bf16),
            S((cores - 1, 1, share), f32),
        ],
        scratch_shapes=[
            *[
                pltpu.VMEM((cores - 1,) + w.shape, bf16)
                for w in (w_query, w_key, w_value, w_proj)
            ],
            pltpu.VMEM((tok_pad, width), bf16),
            pltpu.VMEM((8, up(tok_rows, LANES)), f32),
            pltpu.VMEM((tok_pad, 8), f32),
            pltpu.VMEM((images, key_pad), f32),
            pltpu.VMEM((8, w_query.shape[1]), f32),
            pltpu.VMEM((cores - 1, 8, w_query.shape[1]), f32),
            DMA((7, cores - 1)),
            DMA((7, cores - 1)),
            DMA((cores - 1,)),
            DMA((cores - 1,)),
            DMA((own, cores - 1)),
            DMA((own, cores - 1)),
            DMA((experts,)),
            DMA((experts,)),
            DMA,
            DMA((4,)),
        ],
        compiler_params=params(collective_id=1, has_side_effects=True),
        name="attn_fwd",
    )(
        tokens_in, cotangent, valid, routes.T, ln1_gain, ln1_bias, w_query, w_key, w_value, w_proj,
        b_query, b_value, b_proj, ln2_gain, ln2_bias, w_router.T, w_in[0], w_out[0], b_in,
    )
    attn_w = [w_query, wqs, w_key, wks, w_value, wvs, w_proj, wps]

    size = chunk_of(share)
    per = share // size
    (
        _, _, gin_w, gout_w, gin_rest, gout_rest, gbin_own, gbin_rest, gb_out,
        moe_own, moe_rest, gmoe_own, gmoe_rest,
    ) = pl.pallas_call(
        moe_kernel,
        in_specs=[anywhere, anywhere, inside, anywhere, anywhere] + [inside] * 8,
        out_specs=[anywhere] * 6 + [inside] * 3 + [anywhere] * 4,
        out_shape=[
            S(block, bf16),
            S(block, bf16),
            S((width, share), bf16),
            S((share, width), bf16),
            S((cores - 1, width, share), bf16),
            S((cores - 1, share, width), bf16),
            S((1, share), f32),
            S((cores - 1, 1, share), f32),
            S((cores, 8, width), f32),
            S((pad_own, wide), bf16),
            S((cores - 1, pad_own, wide), bf16),
            S((pad_own, width), bf16),
            S((cores - 1, pad_own, width), bf16),
        ],
        scratch_shapes=[
            pltpu.VMEM((cores, pad_own, wide), bf16),
            pltpu.VMEM(block, bf16),
            pltpu.VMEM(block, bf16),
            pltpu.VMEM(block, bf16),
            pltpu.VMEM(block, bf16),
            pltpu.VMEM((experts, 8, cap_dev), f32),
            pltpu.VMEM((experts, 8, cap_dev), f32),
            pltpu.VMEM((rows_all, 1), f32),
            pltpu.VMEM((cores - 1, 1, share), f32),
            pltpu.VMEM((8, width), f32),
            DMA((2, cores - 1)),
            DMA((2, cores - 1)),
            DMA((2,)),
            DMA((1 + cores,)),
            *[DMA((experts,))] * 10,
            DMA((4, (cores - 1) * per)),
            DMA((4, (cores - 1) * per)),
            DMA((6,)),
        ],
        compiler_params=params(collective_id=2, has_side_effects=True),
        name="moe",
    )(
        h2x.reshape(pad_own, wide), h2x_rest.reshape(cores - 1, pad_own, wide), post, grow, send_g, fidx, w_in[0], w_ins, b_in, b_ins, w_out[0], w_outs, b_out
    )
    def pieces(n):
        return pl.BlockSpec((cores - 1, 1, seq_pad, n), lambda i: (0, i, 0, 0))

    def by_image(x):
        return x.reshape(x.shape[:-2] + (own, seq_pad, x.shape[-1]))

    head_share = w_query.shape[1]
    chunks = 3 if head_share == 3 * LANES else 1
    lanes = head_share // chunks
    buffers = {"pipeline_mode": pl.Buffered(1)} if cores > 2 else {}
    small_b = small_base(cores)
    small_rows = up(small_b + 8 + experts, 8 * cores)
    (
        out_own, gm, gh, dv, first_own, first_rest, small, grad_w_in, grad_w_out,
    ) = pl.pallas_call(
        functools.partial(attn_bwd_a_kernel, dims),
        grid=(own,),
        in_specs=[
            whole(cotangent.shape),
            per_image(seq_pad, 1),
            whole((8, width)),
            per_image(seq_pad, width),
            per_image(seq_pad, wide),
            per_image(seq_pad, width),
            per_image(pairs, 2 * seq_pad, key_pad),
            per_image(seq_pad, width),
            per_image(seq_pad, wide),
            pieces(wide),
            per_image(seq_pad, width),
            pieces(width),
            pl.BlockSpec((width // own, share), lambda i: (i, 0)),
            pl.BlockSpec((cores - 1, width // own, share), lambda i: (0, i, 0), **buffers),
            pl.BlockSpec((share // own, width), lambda i: (i, 0)),
            pl.BlockSpec((cores - 1, share // own, width), lambda i: (0, i, 0), **buffers),
            whole((width,)),
            whole(w_query.shape),
            *[whole(w.shape) for w in attn_w[6:]],
            whole((LANES, width)),
        ],
        out_specs=[
            per_image(seq_pad, width),
            per_image(seq_pad, width),
            per_image(seq_pad, width),
            per_image(seq_pad, width),
            whole((chunks, 2 * width, lanes)),
            whole((cores - 1, chunks, 2 * width, lanes)),
            whole((small_rows, width)),
            pl.BlockSpec((1, width // own, share), lambda i: (0, i, 0)),
            pl.BlockSpec((1, share // own, width), lambda i: (0, i, 0)),
        ],
        out_shape=[
            S((own, seq_pad, width), f32),
            S((own, seq_pad, width), f32),
            S((own, seq_pad, width), bf16),
            S((own, seq_pad, width), bf16),
            S((chunks, 2 * width, lanes), f32),
            S((cores - 1, chunks, 2 * width, lanes), bf16),
            S((small_rows, width), f32),
            S((1, width, share), f32),
            S((1, share, width), f32),
        ],
        scratch_shapes=[pltpu.VMEM((seq_pad, width), f32)]
        + [pltpu.VMEM((pad_own, width), bf16)] * 4,
        compiler_params=params(),
        name="attn_bwd_a",
    )(
        cotangent, valid_col, acc_f, middle, h2x, h1, probs, heads,
        by_image(moe_own), by_image(moe_rest), by_image(gmoe_own), by_image(gmoe_rest),
        gin_w, gin_rest, gout_w, gout_rest, ln2_gain, w_query, *attn_w[6:], wr,
    )
    bits = experts.bit_length() - 1
    piece_rows = small_rows // cores
    low, small, gin_own, out_rest, gin_tok = pl.pallas_call(
        functools.partial(attn_bwd_b_kernel, dims),
        grid=(own,),
        in_specs=[
            per_image(seq_pad, width),
            per_image(key_pad, width),
            per_image(key_pad, width),
            per_image(pairs, 2 * seq_pad, key_pad),
            per_image(seq_pad, width),
            whole((chunks, 2 * width, lanes)),
            anywhere,
            whole((small_rows, width)),
            whole((width,)),
            *[whole(w.shape) for w in attn_w[:6]],
            *[anywhere] * 5,
        ],
        out_specs=[
            anywhere,
            anywhere,
            whole((own, seq_pad, width)),
            anywhere,
            anywhere,
        ],
        out_shape=[
            S((2, chunks, 2 * width, lanes), bf16),
            S((small_rows, width), f32),
            S((own, seq_pad, width), f32),
            S((cores - 1, own, seq_pad, width), f32),
            S((cores - 1, own, seq_pad, width), f32),
        ],
        scratch_shapes=[
            pltpu.VMEM((2, chunks, 2 * width, lanes), bf16),
            pltpu.VMEM((small_rows, width), f32),
            pltpu.VMEM((pad_own, width), bf16),
            pltpu.VMEM((pad_own, width), bf16),
            pltpu.VMEM((own, seq_pad, width), f32),
            pltpu.VMEM((own, seq_pad, width), f32),
            pltpu.VMEM((own, seq_pad, width), bf16),
            pltpu.VMEM((own, seq_pad, width), bf16),
            pltpu.VMEM((cores - 1, chunks, 2 * width, lanes), bf16),
            pltpu.VMEM((2, cores - 1, chunks, 2 * width, lanes), bf16),
            pltpu.VMEM((2, chunks, 2 * width, lanes), f32),
            pltpu.VMEM((2, chunks, 2 * width, lanes), bf16),
            pltpu.VMEM((2, chunks, 2 * width, lanes), bf16),
            pltpu.VMEM((small_rows, width), f32),
            pltpu.VMEM((cores - 1, piece_rows, width), f32),
            pltpu.VMEM((piece_rows, width), f32),
            pltpu.VMEM((bits, piece_rows, width), f32),
            pltpu.VMEM((bits, piece_rows, width), f32),
            DMA((4,)),
            DMA((2, cores - 1, chunks)),
            DMA((2, cores - 1, chunks)),
            DMA((2, chunks, 2 * bits)),
            DMA((2, chunks, 2 * bits)),
            DMA((cores - 1,)),
            DMA((cores - 1,)),
            DMA((bits,)),
            DMA((bits,)),
            DMA((cores - 1,)),
            DMA((cores - 1,)),
            DMA((cores - 1,)),
            DMA((cores - 1,)),
            DMA((own, cores - 1)),
            DMA((own, cores - 1)),
        ],
        compiler_params=params(collective_id=6, has_side_effects=True),
        name="attn_bwd_b",
    )(
        q, k, v, probs, gh, first_own, first_rest, small, ln1_gain, *attn_w[:6],
        x_pad, gm, dv, h1, out_own,
    )
    vector = S((width,), f32)
    part = S((head_share,), f32)
    square = S((width, head_share), f32)
    (
        output, grad_input, gq, gk, gv, gwp, gl1, bl1, gbq, gbv, gbp, gl2, bl2, grout,
        grad_b_in, grad_b_out, rms,
    ) = pl.pallas_call(
        functools.partial(finish_kernel, seq),
        in_specs=[inside] * 5 + [anywhere] * 4,
        out_specs=[anywhere] * 6 + [inside] * 11,
        out_shape=[
            S(tokens_in.shape, f32), S(tokens_in.shape, f32), square, square, square,
            S((head_share, width), f32), vector, vector, part, part, vector, vector, vector,
            S((experts, width), f32), S((1, share), f32), S((1, width), f32), S((5,), f32),
        ],
        scratch_shapes=[
            pltpu.VMEM(tokens_in.shape, f32),
            pltpu.VMEM(tokens_in.shape, f32),
            pltpu.VMEM((2, cores, own, seq_pad, width), f32),
            *[pltpu.VMEM((width, head_share), f32)] * 3,
            pltpu.VMEM((head_share, width), f32),
            DMA((2, cores, own)),
            DMA((2, images)),
            DMA((4,)),
        ],
        compiler_params=params(),
        name="finish",
    )(low, small, gbin_own, gbin_rest, gb_out, out_own, out_rest, gin_own, gin_tok)
    return (
        output, grad_input, gl1, bl1, gq, gk, gv, gbq, gbv, gwp, gbp, gl2, bl2, grout.T,
        grad_w_in, grad_b_in, grad_w_out, grad_b_out, rms,
    )


def solution(mesh):
    in_specs = (
        P("expert", None), P("expert", None), P("expert", None), P(), P(),
        P(None, "tensor"), P(None, "tensor"), P(None, "tensor"), P("tensor"), P("tensor"),
        P("tensor", None), P(), P(), P(), P(),
        P("expert", None, "tensor"), P("expert", "tensor"), P("expert", "tensor", None),
        P("expert", None), P("expert", None),
    )
    out_specs = (
        P("expert", None), P("expert", None), P(), P(),
        P(None, "tensor"), P(None, "tensor"), P(None, "tensor"), P("tensor"), P("tensor"),
        P("tensor", None), P(), P(), P(), P(),
        P("expert", None, "tensor"), P("expert", "tensor"), P("expert", "tensor", None),
        P("expert", None), P(),
    )
    return jax.shard_map(
        on_device, mesh=mesh, in_specs=in_specs, out_specs=out_specs, check_vma=False
    )
```
